256 devices in a mesh: dp: 32 (over x, y, core), seq: 8 (over z).
Axes of the slice: x: 4, y: 4, z: 8, core: 2. Of those that a mesh axis runs over, the one named last changes fastest.
Arguments:
- features: bfloat16 [65536, 1024], P(('dp', 'seq')), may hold values from -16 to 16
- out_grad: bfloat16 [65536, 1024], P(('dp', 'seq')), may hold values from -6 to 6
- norm_gain: float32 [1024], replicated, may hold values from 0.25 to 1.75
- w_qkv: bfloat16 [1024, 1536], replicated, may hold values from -0.1875 to 0.1875
- w_out: bfloat16 [512, 1024], replicated, may hold values from -0.25 to 0.25
- w_msg: bfloat16 [1024, 1024], replicated, may hold values from -0.1875 to 0.1875
- block_ids: int32 [512, 4], P(('dp', 'seq')), may hold values from 0 to 15, as said below
- block_counts: int32 [512], P(('dp', 'seq')), may hold values from 1 to 4, as said below
- edge_tiles: bfloat16 [512, 4, 128, 128], P(('dp', 'seq')), may hold values from -0.375 to 0.375
Outputs:
- block_result_array: bfloat16 [65536, 1024], P(('dp', 'seq'))
- grad_input: bfloat16 [65536, 1024], P(('dp', 'seq'))
- grad_gain: float32 [1024], P('dp')
- grad_qkv: float32 [1024, 1536], P('dp')
- grad_w_out: float32 [512, 1024], P('dp')
- grad_msg: float32 [1024, 1024], P('dp')
The draws below stay inside these ranges and needn't reach their ends.
Inputs may be any that keep to these rules, and one draw needn't show every extreme that they name: `block_ids`: slot 0 of a block's list is the block itself; every entry names a block of the same cluster at most 2 blocks away, and that distance is reached in every cluster. `block_counts`: every cluster has a block with all 4 slots live.
All inputs are finite; a program needn't handle non-finite values.
Results may differ from the reference program's by a relative error of at most 0.035.
Values may be sent and summed in bfloat16 or wider, within the bound.
No kernel may reach another device: no remote copies, remote signals or barrier semaphores. Data moves between devices by JAX's collectives and lax.ppermute only.
A program may use at most 128 MiB of HBM per device.

```python
import math
import jax
import jax.numpy as jnp
from jax import lax

D = 1024
HEADS = 8
HEAD_DIM = 64
BLOCK = 128
NBLK = 4
NODE_DEV = 256
HD = 512
NODES = 2048
ROWS = 65536
BLOCKS = 512
N_DP = 32
N_SEQ = 8


def draw_features(key, part):
    key = jax.random.fold_in(key, 11)
    key_a, key_b = jax.random.split(key, 2)
    row_total = N_DP * NODES
    values = jax.random.truncated_normal(key_a, -6.0, 6.0, (row_total, D), jnp.float32)
    row_scale = jnp.exp(jax.random.uniform(key_b, (row_total, 1), jnp.float32, math.log(0.5), math.log(2.0)))
    values = values * row_scale
    return values.astype(jnp.bfloat16)


def draw_block_ids(key, part):
    key = jax.random.fold_in(key, 12)
    block_total = N_DP * NODES // BLOCK
    block_reach = NODE_DEV // BLOCK
    cluster_blocks = NODES // BLOCK
    own_block = jnp.arange(block_total, dtype=jnp.int32) % cluster_blocks
    offsets = jax.random.randint(key, (block_total, NBLK), -block_reach, block_reach + 1, dtype=jnp.int32)
    listed = jnp.clip(own_block[:, None] + offsets, 0, cluster_blocks - 1)
    listed = listed.at[:, 0].set(own_block)
    first_block = own_block == 0
    last_block = own_block == cluster_blocks - 1
    tail_slot = jnp.where(first_block, block_reach, jnp.where(last_block, cluster_blocks - 1 - block_reach, listed[:, NBLK - 1]))
    listed = listed.at[:, NBLK - 1].set(tail_slot.astype(jnp.int32))
    return listed.astype(jnp.int32)


def draw_block_counts(key, part):
    key = jax.random.fold_in(key, 13)
    key_a, key_b, key_c, key_d = jax.random.split(key, 4)
    block_total = N_DP * NODES // BLOCK
    cluster_blocks = NODES // BLOCK
    counts = jax.random.randint(key_a, (block_total,), 1, NBLK + 1, dtype=jnp.int32)
    counts = jnp.minimum(counts, jax.random.randint(key_b, (block_total,), 1, NBLK + 1, dtype=jnp.int32))
    counts = jnp.minimum(counts, jax.random.randint(key_c, (block_total,), 1, NBLK + 1, dtype=jnp.int32))
    full_pick = jax.random.randint(key_d, (N_DP,), 0, cluster_blocks, dtype=jnp.int32)
    position = jnp.arange(block_total, dtype=jnp.int32) % cluster_blocks
    cluster = jnp.arange(block_total, dtype=jnp.int32) // cluster_blocks
    counts = jnp.where(position == full_pick[cluster], NBLK, counts)
    return counts.astype(jnp.int32)


def shard_levels(stream_key, dims, cuts, least, largest):
    loudness = 1.0
    for dim, blocks in cuts:
        draws = jax.random.uniform(jax.random.fold_in(jax.random.fold_in(stream_key, 6), dim), (blocks,), jnp.float32, least / len(cuts), largest / len(cuts))
        loudness = loudness * jnp.repeat(jnp.exp(draws), dims[dim] // blocks).reshape((-1,) + (1,) * (len(dims) - 1 - dim))
    return loudness


def noise(stream_key, dims, spread, limit, cuts=(), kind=jnp.bfloat16):
    level = shard_levels(stream_key, dims, cuts, -0.22, 0.18) if cuts else 1.0
    result = jax.random.normal(stream_key, dims, jnp.float32) * spread * level
    return jnp.minimum(jnp.maximum(result, -limit), limit).astype(kind)


def setup_inputs(seed: int = 0) -> dict:
    splits = jax.random.split(jax.random.key(seed), 10)
    features = draw_features(jax.random.fold_in(splits[9], 71), 0)
    out_grad = noise(splits[1], (ROWS, D), 1.0, 6.0, ((0, 256),))
    norm_gain = jnp.clip(1.0 + 0.15 * jax.random.normal(splits[2], (D,), jnp.float32), 0.25, 1.75)
    w_qkv = noise(splits[3], (D, 3 * HD), D ** -0.5, 0.1875)
    w_out = noise(splits[4], (HD, D), HD ** -0.5, 0.25)
    w_msg = noise(splits[5], (D, D), D ** -0.5, 0.1875)
    block_ids = draw_block_ids(jax.random.fold_in(splits[9], 71), 0)
    block_counts = draw_block_counts(jax.random.fold_in(splits[9], 71), 0)
    edge_tiles = noise(splits[8], (BLOCKS, NBLK, BLOCK, BLOCK), (2 * BLOCK) ** -0.5, 0.375, ((0, 256),))
    return {"features": features, "out_grad": out_grad, "norm_gain": norm_gain, "w_qkv": w_qkv, "w_out": w_out, "w_msg": w_msg, "block_ids": block_ids, "block_counts": block_counts, "edge_tiles": edge_tiles}


exponent_divisor = 32.0
epsilon = 1e-06

def unit_rows(block):
    wide = block.astype(jnp.float32)
    factor = lax.rsqrt(lax.optimization_barrier(jnp.mean(wide * wide, axis=-1, keepdims=True)) + epsilon)
    return (wide, factor)

def attend_head(asker_vector_split, k_head, payload_subspace):
    q_wide, q_factor = unit_rows(asker_vector_split)
    k_wide, k_factor = unit_rows(k_head)
    q_unit = (q_wide * q_factor).astype(jnp.bfloat16)
    k_unit = (k_wide * k_factor).astype(jnp.bfloat16)
    similarity_multiplier = exponent_divisor / asker_vector_split.shape[-1]
    scores = lax.dot_general(q_unit, k_unit, (((1,), (1,)), ((), ())), preferred_element_type=jnp.float32) * similarity_multiplier
    exp_scores = jnp.exp(scores)
    attention_weights_matrix = exp_scores / lax.optimization_barrier(jnp.sum(exp_scores, axis=-1, keepdims=True))
    prob_low = attention_weights_matrix.astype(jnp.bfloat16)
    head_out = jnp.dot(prob_low, payload_subspace, preferred_element_type=jnp.float32).astype(jnp.bfloat16)
    return (head_out, attention_weights_matrix, q_unit, k_unit)

def attend_back(asker_vector_split, k_head, payload_subspace, q_unit, k_unit, attention_weights_matrix, head_out, d_head):
    prob_low = attention_weights_matrix.astype(jnp.bfloat16)
    d_value = lax.dot_general(prob_low, d_head, (((0,), (0,)), ((), ())), preferred_element_type=jnp.float32).astype(jnp.bfloat16)
    d_prob = lax.dot_general(d_head, payload_subspace, (((1,), (1,)), ((), ())), preferred_element_type=jnp.float32)
    row_dot = lax.optimization_barrier(jnp.sum(d_head.astype(jnp.float32) * head_out.astype(jnp.float32), axis=-1, keepdims=True))
    d_scores = (attention_weights_matrix * (d_prob - row_dot)).astype(jnp.bfloat16)
    similarity_multiplier = exponent_divisor / asker_vector_split.shape[-1]
    grad_query_normalized = jnp.dot(d_scores, k_unit, preferred_element_type=jnp.float32) * similarity_multiplier
    d_kunit = lax.dot_general(d_scores, q_unit, (((0,), (0,)), ((), ())), preferred_element_type=jnp.float32) * similarity_multiplier
    q_wide, q_factor = unit_rows(asker_vector_split)
    k_wide, k_factor = unit_rows(k_head)
    d_query = q_factor * grad_query_normalized - q_factor ** 3 * q_wide * lax.optimization_barrier(jnp.mean(grad_query_normalized * q_wide, axis=-1, keepdims=True))
    d_key = k_factor * d_kunit - k_factor ** 3 * k_wide * lax.optimization_barrier(jnp.mean(d_kunit * k_wide, axis=-1, keepdims=True))
    return (d_query.astype(jnp.bfloat16), d_key.astype(jnp.bfloat16), d_value)

def rounded(value):
    return lax.optimization_barrier(value.astype(jnp.bfloat16)).astype(jnp.float32)

def reference(features, out_grad, norm_gain, w_qkv, w_out, w_msg, block_ids, block_counts, edge_tiles):
    cluster_blocks = NODES // BLOCK
    feat_c = features.reshape(N_DP, NODES, D)
    grad_c = out_grad.reshape(N_DP, NODES, D)
    ids_c = block_ids.reshape(N_DP, cluster_blocks, NBLK)
    count_c = block_counts.reshape(N_DP, cluster_blocks)
    tile_c = edge_tiles.reshape(N_DP, cluster_blocks, NBLK, BLOCK, BLOCK)
    zero_acc = (jnp.zeros((N_SEQ, D, 3 * HD), jnp.float32), jnp.zeros((N_SEQ, HD, D), jnp.float32), jnp.zeros((N_SEQ, D, D), jnp.float32), jnp.zeros((N_SEQ, D), jnp.float32))

    def split_heads(arr):
        return arr.reshape(NODES, HEADS, HEAD_DIM).transpose(1, 0, 2)

    def merge_heads(arr):
        return arr.transpose(1, 0, 2).reshape(NODES, HD)

    def head_pass(operands):
        asker_vector_split, k_head, payload_subspace, d_head = operands
        head_out, attention_weights_matrix, q_unit, k_unit = attend_head(asker_vector_split, k_head, payload_subspace)
        d_query, d_key, d_value = attend_back(asker_vector_split, k_head, payload_subspace, q_unit, k_unit, attention_weights_matrix, head_out, d_head)
        return (head_out, d_query, d_key, d_value)

    def one_cluster(totals, inputs):
        feat, grad, listed, counts, tiles = inputs
        feat_wide = feat.astype(jnp.float32)
        inv_rms = lax.rsqrt(lax.optimization_barrier(jnp.mean(feat_wide * feat_wide, axis=-1, keepdims=True)) + epsilon)
        x_hat = feat_wide * inv_rms
        normed = (x_hat * norm_gain).astype(jnp.bfloat16)
        proj = jnp.dot(normed, w_qkv, preferred_element_type=jnp.float32).astype(jnp.bfloat16)
        d_out = lax.dot_general(grad, w_out, (((1,), (1,)), ((), ())), preferred_element_type=jnp.float32).astype(jnp.bfloat16)
        head_out, d_query, d_key, d_value = lax.map(head_pass, (split_heads(proj[:, :HD]), split_heads(proj[:, HD:2 * HD]), split_heads(proj[:, 2 * HD:]), split_heads(d_out)))
        out_rows = merge_heads(head_out)
        d_proj = jnp.concatenate([merge_heads(d_query), merge_heads(d_key), merge_heads(d_value)], axis=1)
        msg_rows = jnp.dot(normed, w_msg, preferred_element_type=jnp.float32).astype(jnp.bfloat16)
        live_mask = (jnp.arange(NBLK, dtype=jnp.int32)[None, :] < counts[:, None]).astype(jnp.bfloat16)
        live = tiles * live_mask[:, :, None, None]
        source = msg_rows.reshape(cluster_blocks, BLOCK, D)[listed]
        agg = jnp.einsum('bsij,bsjd->bid', live.astype(jnp.float32), source.astype(jnp.float32), precision=lax.Precision.HIGHEST).reshape(NODES, D)
        attn_part = jnp.dot(out_rows, w_out, preferred_element_type=jnp.float32)
        block_result_array = (feat_wide + attn_part + jax.nn.silu(agg)).astype(jnp.bfloat16)
        grad_wide = grad.astype(jnp.float32)
        sigma = jax.nn.sigmoid(agg)
        d_agg = (grad_wide * sigma * (1.0 + agg * (1.0 - sigma))).astype(jnp.bfloat16)
        contrib = jnp.einsum('bsij,bid->bsjd', live.astype(jnp.float32), d_agg.reshape(cluster_blocks, BLOCK, D).astype(jnp.float32), precision=lax.Precision.HIGHEST)
        landed = jnp.zeros((cluster_blocks, BLOCK, D), jnp.float32).at[listed.reshape(-1)].add(contrib.reshape(-1, BLOCK, D))
        d_msg = landed.reshape(NODES, D).astype(jnp.bfloat16)
        d_norm = jnp.dot(d_proj, w_qkv.T, preferred_element_type=jnp.float32) + jnp.dot(d_msg, w_msg.T, preferred_element_type=jnp.float32)
        scaled_logits = d_norm * norm_gain
        d_feat = inv_rms * (scaled_logits - x_hat * lax.optimization_barrier(jnp.mean(scaled_logits * x_hat, axis=-1, keepdims=True)))
        grad_input = (grad_wide + d_feat).astype(jnp.bfloat16)

        def slices(arr):
            return arr.astype(jnp.float32).reshape(N_SEQ, NODE_DEV, arr.shape[1])
        high = lax.Precision.HIGHEST
        part_qkv = jnp.einsum('snd,snf->sdf', slices(normed), slices(d_proj), precision=high)
        part_out = jnp.einsum('snd,snf->sdf', slices(out_rows), slices(grad), precision=high)
        part_msg = jnp.einsum('snd,snf->sdf', slices(normed), slices(d_msg), precision=high)
        part_gain = lax.optimization_barrier(jnp.sum(slices(d_norm * x_hat), axis=1))
        new_totals = (totals[0] + rounded(part_qkv), totals[1] + rounded(part_out), totals[2] + rounded(part_msg), totals[3] + rounded(part_gain))
        return (new_totals, (block_result_array, grad_input))
    totals, (outs, grads) = lax.scan(one_cluster, zero_acc, (feat_c, grad_c, ids_c, count_c, tile_c))
    block_result_array = outs.reshape(ROWS, D)
    grad_input = grads.reshape(ROWS, D)
    grad_qkv = lax.optimization_barrier(jnp.sum(totals[0], axis=0)) / NODES
    grad_w_out = lax.optimization_barrier(jnp.sum(totals[1], axis=0)) / NODES
    grad_msg = lax.optimization_barrier(jnp.sum(totals[2], axis=0)) / NODES
    grad_gain = lax.optimization_barrier(jnp.sum(totals[3], axis=0)) / NODES
    return (block_result_array, grad_input, grad_gain, grad_qkv, grad_w_out, grad_msg)
```

```python
import jax
import jax.numpy as jnp
from jax import lax
from jax.sharding import Mesh
from jax.sharding import PartitionSpec as P

HEAD_DIM = 64
BLOCK = 128
N_SEQ = 8
N_XY = 16

exponent_divisor = 32.0
epsilon = 1e-06


def unit_rows(block):
    wide = block.astype(jnp.float32)
    factor = lax.rsqrt(jnp.mean(wide * wide, axis=-1, keepdims=True) + epsilon)
    return (wide, factor)


def attend(query, keyrow, valrow, d_head):
    scale = exponent_divisor / HEAD_DIM
    q_wide, q_factor = unit_rows(query)
    k_wide, k_factor = unit_rows(keyrow)
    q_unit = (q_wide * q_factor).astype(jnp.bfloat16)
    k_unit = (k_wide * k_factor).astype(jnp.bfloat16)
    exp_scores = jnp.exp(contract_cols(q_unit, k_unit) * scale)
    prob = exp_scores / jnp.sum(exp_scores, axis=-1, keepdims=True)
    prob_low = prob.astype(jnp.bfloat16)
    head_out = jnp.dot(prob_low, valrow, preferred_element_type=jnp.float32).astype(jnp.bfloat16)
    d_value = contract_rows(prob_low, d_head).astype(jnp.bfloat16)
    d_prob = contract_cols(d_head, valrow)
    row_dot = jnp.sum(
        d_head.astype(jnp.float32) * head_out.astype(jnp.float32), axis=-1, keepdims=True
    )
    d_scores = (prob * (d_prob - row_dot)).astype(jnp.bfloat16)
    d_qunit = jnp.dot(d_scores, k_unit, preferred_element_type=jnp.float32) * scale
    d_kunit = contract_rows(d_scores, q_unit) * scale
    d_query = q_factor * d_qunit - q_factor**3 * q_wide * jnp.mean(
        d_qunit * q_wide, axis=-1, keepdims=True
    )
    d_key = k_factor * d_kunit - k_factor**3 * k_wide * jnp.mean(
        d_kunit * k_wide, axis=-1, keepdims=True
    )
    return head_out, d_query.astype(jnp.bfloat16), d_key.astype(jnp.bfloat16), d_value


def contract_rows(left, right):
    return lax.dot_general(
        left, right, (((0,), (0,)), ((), ())), preferred_element_type=jnp.float32
    )


def contract_cols(left, right):
    return lax.dot_general(
        left, right, (((1,), (1,)), ((), ())), preferred_element_type=jnp.float32
    )


def exchange(array, axis):
    return lax.all_to_all(array, axis, split_axis=0, concat_axis=0, tiled=True)


def up(array):
    return lax.ppermute(array, "z", [(i, (i + 1) % N_SEQ) for i in range(N_SEQ)])


def down(array):
    return lax.ppermute(array, "z", [((i + 1) % N_SEQ, i) for i in range(N_SEQ)])


def sum_over_dp(partial):
    rows, width = partial.shape
    core = lax.axis_index("c")
    parts = partial.astype(jnp.bfloat16).reshape(N_XY, 2, rows // (2 * N_XY), width)
    keep = lax.dynamic_index_in_dim(parts, core, 1, keepdims=False)
    give = lax.dynamic_index_in_dim(parts, 1 - core, 1, keepdims=False)
    got = lax.ppermute(give, "c", [(0, 1), (1, 0)])
    pair = (keep.astype(jnp.float32) + got.astype(jnp.float32)).astype(jnp.bfloat16)
    shares = exchange(pair, ("x", "y"))
    return jnp.sum(shares.astype(jnp.float32), axis=0)


def on_device(
    features, out_grad, norm_gain, w_qkv, w_out, w_msg, block_ids, block_counts, edge_tiles
):
    node_rows, width = features.shape
    hd = w_out.shape[0]
    z = lax.axis_index("z")
    feat_wide = features.astype(jnp.float32)
    inv_rms = lax.rsqrt(jnp.mean(feat_wide * feat_wide, axis=-1, keepdims=True) + epsilon)
    x_hat = feat_wide * inv_rms
    normed = (x_hat * norm_gain).astype(jnp.bfloat16)

    a1, b1 = up(normed), down(normed)
    a2, b2 = up(a1), down(b1)
    a3, b3 = up(a2), down(b2)
    half = node_rows // 2
    c4 = jnp.concatenate([up(a3[:half]), down(b3[half:])], axis=0)
    chunks = [normed, a1, a2, a3, c4, b3, b2, b1]

    d_out = contract_cols(out_grad, w_out).astype(jnp.bfloat16)
    d_out = d_out.reshape(2, half, N_SEQ, HEAD_DIM).transpose(2, 1, 0, 3).reshape(N_SEQ, half, 2 * HEAD_DIM)
    d_heads = exchange(d_out, "z")
    relative = (z - jnp.arange(N_SEQ)) % N_SEQ
    d_heads = d_heads[relative].reshape(N_SEQ, half, 2, HEAD_DIM).transpose(0, 2, 1, 3)
    d_heads = d_heads.reshape(N_SEQ * node_rows, HEAD_DIM)

    w_head = lax.dynamic_index_in_dim(w_qkv.reshape(width, 3, N_SEQ, HEAD_DIM), z, 2, keepdims=False)
    w_head = w_head.reshape(width, 3 * HEAD_DIM)
    proj = jnp.concatenate(
        [jnp.dot(c, w_head, preferred_element_type=jnp.float32).astype(jnp.bfloat16) for c in chunks], axis=0
    )
    head_out, d_query, d_key, d_value = attend(
        proj[:, :HEAD_DIM], proj[:, HEAD_DIM : 2 * HEAD_DIM], proj[:, 2 * HEAD_DIM :], d_heads
    )
    back = (z - jnp.arange(N_SEQ)) % N_SEQ

    def home(left, right):
        both = jnp.concatenate([left, right], axis=1).reshape(N_SEQ, node_rows, 2 * HEAD_DIM)
        both = exchange(both[back], "z")
        flat = both.reshape(N_SEQ, node_rows, 2, HEAD_DIM).transpose(2, 1, 0, 3)
        flat = flat.reshape(2, node_rows, hd)
        return flat[0], flat[1]

    out_rows, dv_rows = home(head_out, d_value)
    dq_rows, dk_rows = home(d_query, d_key)

    wide = jnp.concatenate([a1, normed, b1], axis=0)
    blocks_here = node_rows // BLOCK
    wide_msg = jnp.dot(wide, w_msg, preferred_element_type=jnp.float32).astype(jnp.bfloat16)
    local_ids = block_ids - (z - 1) * blocks_here
    source = wide_msg.reshape(3 * blocks_here, BLOCK, width)[local_ids]
    slots = block_ids.shape[1]
    live_mask = (jnp.arange(slots, dtype=jnp.int32)[None, :] < block_counts[:, None]).astype(jnp.bfloat16)
    live = edge_tiles * live_mask[:, :, None, None]
    agg = jnp.einsum("bsij,bsjd->bid", live, source, preferred_element_type=jnp.float32).reshape(
        node_rows, width
    )
    grad_wide = out_grad.astype(jnp.float32)
    sigma = jax.nn.sigmoid(agg)
    d_agg = (grad_wide * sigma * (1.0 + agg * (1.0 - sigma))).astype(jnp.bfloat16)
    contrib = jnp.einsum(
        "bsij,bid->bsjd",
        live,
        d_agg.reshape(blocks_here, BLOCK, width),
        preferred_element_type=jnp.float32,
    )
    tally = (
        local_ids[:, :, None] == jnp.arange(3 * blocks_here, dtype=jnp.int32)[None, None, :]
    ).astype(jnp.float32)
    landed = jnp.einsum("bsk,bsjd->kjd", tally, contrib, precision=lax.Precision.HIGHEST)
    from_above = down(landed[:blocks_here].astype(jnp.bfloat16)).astype(jnp.float32)
    from_below = up(landed[2 * blocks_here :].astype(jnp.bfloat16)).astype(jnp.float32)
    d_msg = (
        (landed[blocks_here : 2 * blocks_here] + from_above + from_below)
        .reshape(node_rows, width)
        .astype(jnp.bfloat16)
    )
    sum_msg = sum_over_dp(contract_rows(normed, d_msg))

    attn_part = jnp.dot(out_rows, w_out, preferred_element_type=jnp.float32)
    block_result_array = (feat_wide + attn_part + agg * sigma).astype(jnp.bfloat16)
    sum_out = sum_over_dp(contract_rows(out_rows, out_grad))

    d_proj = jnp.concatenate([dq_rows, dk_rows, dv_rows], axis=1)
    d_norm = contract_cols(d_proj, w_qkv) + contract_cols(d_msg, w_msg)
    scaled = d_norm * norm_gain
    d_feat = inv_rms * (scaled - x_hat * jnp.mean(scaled * x_hat, axis=-1, keepdims=True))
    grad_input = (grad_wide + d_feat).astype(jnp.bfloat16)

    d_head_proj = jnp.concatenate([d_query, d_key, d_value], axis=1)
    normed_all = jnp.concatenate(chunks, axis=0)
    sum_head = sum_over_dp(contract_rows(normed_all, d_head_proj))

    tall = jnp.concatenate([sum_msg, sum_out], axis=0).astype(jnp.bfloat16)
    tall = tall.reshape(N_SEQ, tall.shape[0] // N_SEQ, width)
    share = jnp.sum(exchange(tall, "z").astype(jnp.float32), axis=0)
    mine = jnp.concatenate([share.astype(jnp.bfloat16).reshape(-1, 2 * BLOCK), sum_head.astype(jnp.bfloat16).reshape(-1, 2 * BLOCK)], axis=0)
    every = exchange(jnp.broadcast_to(mine[None], (N_SEQ,) + mine.shape), "z")
    cut = share.size // (2 * BLOCK)
    nodes = N_SEQ * node_rows
    flat = every[:, :cut].reshape(-1, width).astype(jnp.float32) / nodes
    grad_msg = flat[: sum_msg.shape[0]]
    grad_out = flat[sum_msg.shape[0] :]
    heads = every[:, cut:].reshape(N_SEQ, -1, 3, HEAD_DIM).transpose(1, 2, 0, 3)
    grad_qkv = heads.reshape(-1, 3 * hd).astype(jnp.float32) / nodes

    rows_here = grad_qkv.shape[0]
    first = ((lax.axis_index("x") * 4 + lax.axis_index("y")) * 2 + lax.axis_index("c")) * rows_here
    w_rows = lax.dynamic_slice_in_dim(w_qkv, first, rows_here, 0).astype(jnp.float32)
    m_rows = lax.dynamic_slice_in_dim(w_msg, first, rows_here, 0).astype(jnp.float32)
    gain_rows = lax.dynamic_slice_in_dim(norm_gain, first, rows_here, 0)
    grad_gain = (
        jnp.sum(w_rows * grad_qkv, axis=1) + jnp.sum(m_rows * grad_msg, axis=1)
    ) / gain_rows
    return block_result_array, grad_input, grad_gain, grad_qkv, grad_out, grad_msg


def solution(mesh):
    fine = Mesh(mesh.devices.reshape(4, 4, 2, N_SEQ), ("x", "y", "c", "z"))
    dp = ("x", "y", "c")
    rows = ("x", "y", "c", "z")
    return jax.shard_map(
        on_device,
        mesh=fine,
        in_specs=(
            P(rows, None),
            P(rows, None),
            P(),
            P(),
            P(),
            P(),
            P(rows, None),
            P(rows),
            P(rows, None, None, None),
        ),
        out_specs=(
            P(rows, None),
            P(rows, None),
            P(dp),
            P(dp, None),
            P(dp, None),
            P(dp, None),
        ),
        check_vma=False,
    )
```

```python
import jax
import jax.numpy as jnp
from jax import lax
from jax.experimental import pallas as pl
from jax.experimental.pallas import tpu as pltpu
from jax.sharding import Mesh
from jax.sharding import PartitionSpec as P

HEAD_DIM = 64
BLOCK = 128
N_SEQ = 8
N_XY = 16
CHUNK = 256

exponent_divisor = 32.0
epsilon = 1e-06


def unit_rows(block):
    wide = block.astype(jnp.float32)
    factor = lax.rsqrt(jnp.mean(wide * wide, axis=-1, keepdims=True) + epsilon)
    return (wide, factor)


def matmul(left, right):
    return jnp.dot(left, right, preferred_element_type=jnp.float32)


def forward_kernel(*refs):
    z_ref = refs[0]
    chunks = refs[1:9]
    w_ref, dh_ref = refs[9:11]
    att_ref, rows_ref, turned_ref, raw_ref, stats_ref = refs[11:16]
    dv_sum = refs[16]
    z = z_ref[0]
    scale = exponent_divisor / HEAD_DIM
    half = CHUNK // 2
    for j in range(N_SEQ):
        proj = matmul(chunks[j][...], w_ref[...]).astype(jnp.bfloat16)
        wide = proj.astype(jnp.float32)
        query, keyrow, valrow = (wide[:, i * HEAD_DIM : (i + 1) * HEAD_DIM] for i in range(3))
        _, q_factor = unit_rows(query)
        _, k_factor = unit_rows(keyrow)
        q_unit = query * q_factor
        k_unit = keyrow * k_factor
        folded = dh_ref[lax.rem(z - j + N_SEQ, N_SEQ)]
        d_head = jnp.concatenate([folded[:, :HEAD_DIM], folded[:, HEAD_DIM:]], axis=0)
        rows_ref[0, j] = q_unit.astype(jnp.bfloat16)
        rows_ref[1, j] = k_unit.astype(jnp.bfloat16)
        rows_ref[2, j] = valrow.astype(jnp.bfloat16)
        rows_ref[3, j] = d_head
        raw_ref[0, j] = jnp.concatenate([keyrow, jnp.broadcast_to(k_factor, keyrow.shape)], axis=1)
        first = jnp.concatenate([q_unit, d_head.astype(jnp.float32)], axis=1).T
        second = jnp.concatenate([k_unit, valrow], axis=1).T
        turned_ref[0, j] = first[:HEAD_DIM].astype(jnp.bfloat16)
        turned_ref[1, j] = first[HEAD_DIM:].astype(jnp.bfloat16)
        turned_ref[2, j] = second[:HEAD_DIM].astype(jnp.bfloat16)
        turned_ref[3, j] = second[HEAD_DIM:].astype(jnp.bfloat16)
        raw_ref[1, j] = jnp.concatenate([query, jnp.broadcast_to(q_factor, query.shape)], axis=1)
    dv_sum[...] = jnp.zeros_like(dv_sum)

    def step(i, carry):
        keys = rows_ref[1].reshape(N_SEQ * CHUNK, HEAD_DIM)
        scores = matmul(keys, turned_ref[0, i]) * scale
        exps = jnp.exp(scores)
        inverse = 1.0 / jnp.sum(exps, axis=0, keepdims=True)
        prob_low = (exps * inverse).astype(jnp.bfloat16)
        out = jnp.zeros((HEAD_DIM, CHUNK), jnp.float32)
        for j in range(N_SEQ):
            out += matmul(turned_ref[3, j], prob_low[j * CHUNK : (j + 1) * CHUNK])
        dv_sum[...] += matmul(prob_low, rows_ref[3, i])
        out = out.astype(jnp.bfloat16).astype(jnp.float32)
        d_head = turned_ref[1, i].astype(jnp.float32)
        stats_ref[i, 0:1] = inverse
        stats_ref[i, 1:2] = jnp.sum(out * d_head, axis=0, keepdims=True)
        both = jnp.concatenate([out, out], axis=0).T
        att_ref[lax.rem(z - i + N_SEQ, N_SEQ)] = both.astype(jnp.bfloat16)
        return carry

    lax.fori_loop(0, N_SEQ, step, 0)
    for j in range(N_SEQ):
        place = lax.rem(z - j + N_SEQ, N_SEQ)
        att_ref[place, :, HEAD_DIM:] = dv_sum[j * CHUNK : (j + 1) * CHUNK].astype(jnp.bfloat16)


def backward_kernel(*refs):
    place_ref = refs[0]
    chunks = refs[1:9]
    att_ref, rows_ref, turned_ref, raw_ref, stats_ref = refs[9:14]
    dqk_ref, keep_ref, give_ref = refs[14:17]
    dk_sum, dqt, grad_t, grad = refs[17:21]
    z = place_ref[0]
    core = place_ref[1]
    scale = exponent_divisor / HEAD_DIM
    dk_sum[...] = jnp.zeros_like(dk_sum)

    def step(i, carry):
        keys = rows_ref[1].reshape(N_SEQ * CHUNK, HEAD_DIM)
        vals = rows_ref[2].reshape(N_SEQ * CHUNK, HEAD_DIM)
        scores = matmul(keys, turned_ref[0, i]) * scale
        prob = jnp.exp(scores) * stats_ref[i, 0:1]
        d_prob = matmul(vals, turned_ref[1, i])
        d_scores = (prob * (d_prob - stats_ref[i, 1:2])).astype(jnp.bfloat16)
        d_qunit = jnp.zeros((HEAD_DIM, CHUNK), jnp.float32)
        for j in range(N_SEQ):
            d_qunit += matmul(turned_ref[2, j], d_scores[j * CHUNK : (j + 1) * CHUNK])
        dk_sum[...] += matmul(d_scores, rows_ref[0, i])
        dqt[i] = d_qunit * scale
        return carry

    lax.fori_loop(0, N_SEQ, step, 0)
    for j in range(N_SEQ):
        place = lax.rem(z - j + N_SEQ, N_SEQ)
        d_qunit = jnp.concatenate([dqt[j], dqt[j]], axis=0).T[:, :HEAD_DIM]
        d_kunit = dk_sum[j * CHUNK : (j + 1) * CHUNK] * scale
        parts = []
        for raw, d_unit in ((raw_ref[1, j], d_qunit), (raw_ref[0, j], d_kunit)):
            wide = raw[:, :HEAD_DIM]
            factor = raw[:, HEAD_DIM:]
            mean = jnp.mean(d_unit * wide, axis=-1, keepdims=True)
            parts.append(factor * d_unit - factor * factor * factor * wide * mean)
        both = jnp.concatenate(parts, axis=1)
        dqk_ref[place] = both.astype(jnp.bfloat16)
        d_val = att_ref[place].astype(jnp.float32)
        d_val = jnp.concatenate([d_val[:, HEAD_DIM:], jnp.zeros_like(d_val[:, HEAD_DIM:])], axis=1)
        stacked = jnp.concatenate([both.T, d_val.T], axis=0).astype(jnp.bfloat16)
        term = matmul(stacked, chunks[j][...])
        if j == 0:
            grad_t[...] = term
        else:
            grad_t[...] += term
    grad[...] = grad_t[...].T
    rows = grad.shape[0] // (2 * N_XY)
    for i in range(N_XY):
        keep_ref[i] = grad[pl.ds((2 * i + core) * rows, rows), :].astype(jnp.bfloat16)
        give_ref[i] = grad[pl.ds((2 * i + 1 - core) * rows, rows), :].astype(jnp.bfloat16)


def in_vmem(count):
    return [pl.BlockSpec(memory_space=pltpu.VMEM)] * count


def attend_forward(z, chunks, w_head, d_heads):
    nodes = N_SEQ * CHUNK
    flops = 2 * nodes * (chunks[0].shape[1] * 3 * HEAD_DIM + 3 * nodes * HEAD_DIM)
    return pl.pallas_call(
        forward_kernel,
        out_shape=(
            jax.ShapeDtypeStruct((N_SEQ, CHUNK, 2 * HEAD_DIM), jnp.bfloat16),
            jax.ShapeDtypeStruct((4, N_SEQ, CHUNK, HEAD_DIM), jnp.bfloat16),
            jax.ShapeDtypeStruct((4, N_SEQ, HEAD_DIM, CHUNK), jnp.bfloat16),
            jax.ShapeDtypeStruct((2, N_SEQ, CHUNK, 2 * HEAD_DIM), jnp.float32),
            jax.ShapeDtypeStruct((N_SEQ, 8, CHUNK), jnp.float32),
        ),
        in_specs=[pl.BlockSpec(memory_space=pltpu.SMEM)] + in_vmem(10),
        out_specs=tuple(in_vmem(5)),
        scratch_shapes=[pltpu.VMEM((nodes, HEAD_DIM), jnp.float32)],
        compiler_params=pltpu.CompilerParams(vmem_limit_bytes=48 * 1024 * 1024),
        cost_estimate=pl.CostEstimate(
            flops=4 * flops, bytes_accessed=12 * 1024 * 1024, transcendentals=nodes * nodes
        ),
        name="attend_forward",
    )(z, *chunks, w_head, d_heads)


def attend_backward(place, chunks, att, saved):
    nodes = N_SEQ * CHUNK
    width = chunks[0].shape[1]
    flops = 2 * nodes * (width * 3 * HEAD_DIM + 4 * nodes * HEAD_DIM)
    part = jax.ShapeDtypeStruct((N_XY, width // (2 * N_XY), 4 * HEAD_DIM), jnp.bfloat16)
    return pl.pallas_call(
        backward_kernel,
        out_shape=(jax.ShapeDtypeStruct((N_SEQ, CHUNK, 2 * HEAD_DIM), jnp.bfloat16), part, part),
        in_specs=[pl.BlockSpec(memory_space=pltpu.SMEM)] + in_vmem(13),
        out_specs=tuple(in_vmem(3)),
        scratch_shapes=[
            pltpu.VMEM((nodes, HEAD_DIM), jnp.float32),
            pltpu.VMEM((N_SEQ, HEAD_DIM, CHUNK), jnp.float32),
            pltpu.VMEM((4 * HEAD_DIM, width), jnp.float32),
            pltpu.VMEM((width, 4 * HEAD_DIM), jnp.float32),
        ],
        compiler_params=pltpu.CompilerParams(vmem_limit_bytes=48 * 1024 * 1024),
        cost_estimate=pl.CostEstimate(
            flops=4 * flops, bytes_accessed=12 * 1024 * 1024, transcendentals=nodes * nodes
        ),
        name="attend_backward",
    )(place, *chunks, att, *saved)


def after(value, *others):
    return lax.optimization_barrier((value,) + others)[0]


def contract_rows(left, right):
    return lax.dot_general(
        left, right, (((0,), (0,)), ((), ())), preferred_element_type=jnp.float32
    )


def contract_cols(left, right):
    return lax.dot_general(
        left, right, (((1,), (1,)), ((), ())), preferred_element_type=jnp.float32
    )


def exchange(array, axis):
    return lax.all_to_all(array, axis, split_axis=0, concat_axis=0, tiled=True)


def up(array):
    return lax.ppermute(array, "z", [(i, (i + 1) % N_SEQ) for i in range(N_SEQ)])


def down(array):
    return lax.ppermute(array, "z", [((i + 1) % N_SEQ, i) for i in range(N_SEQ)])


def halves(partial):
    rows, width = partial.shape
    core = lax.axis_index("c")
    parts = partial.astype(jnp.bfloat16).reshape(N_XY, 2, rows // (2 * N_XY), width)
    keep = lax.dynamic_index_in_dim(parts, core, 1, keepdims=False)
    give = lax.dynamic_index_in_dim(parts, 1 - core, 1, keepdims=False)
    return keep, give


def sum_over_cores(keep, give):
    got = lax.ppermute(give, "c", [(0, 1), (1, 0)])
    return (keep.astype(jnp.float32) + got.astype(jnp.float32)).astype(jnp.bfloat16)


def sum_over_chips(pair):
    return jnp.sum(exchange(pair, ("x", "y")).astype(jnp.float32), axis=0)


def on_device(
    features, out_grad, norm_gain, w_qkv, w_out, w_msg, block_ids, block_counts, edge_tiles
):
    node_rows, width = features.shape
    hd = w_out.shape[0]
    z = lax.axis_index("z")
    core = lax.axis_index("c")
    place = jnp.stack([z, core]).astype(jnp.int32)
    feat_wide = features.astype(jnp.float32)
    inv_rms = lax.rsqrt(jnp.mean(feat_wide * feat_wide, axis=-1, keepdims=True) + epsilon)
    x_hat = feat_wide * inv_rms
    normed = (x_hat * norm_gain).astype(jnp.bfloat16)

    a1, b1 = up(normed), down(normed)
    a2, b2 = up(a1), down(b1)
    a3, b3 = up(a2), down(b2)
    half = node_rows // 2
    c4 = jnp.concatenate([up(a3[:half]), down(b3[half:])], axis=0)
    chunks = [normed, a1, a2, a3, c4, b3, b2, b1]

    d_out = contract_cols(out_grad, w_out).astype(jnp.bfloat16)
    d_out = d_out.reshape(2, half, N_SEQ, HEAD_DIM).transpose(2, 1, 0, 3).reshape(N_SEQ, half, 2 * HEAD_DIM)
    d_heads = exchange(d_out, "z")
    w_head = lax.dynamic_index_in_dim(w_qkv.reshape(width, 3, N_SEQ, HEAD_DIM), z, 2, keepdims=False)
    w_head = w_head.reshape(width, 3 * HEAD_DIM)

    wide = jnp.concatenate([after(a1, a2, b2), normed, b1], axis=0)
    blocks_here = node_rows // BLOCK
    wide_msg = jnp.dot(wide, w_msg, preferred_element_type=jnp.float32).astype(jnp.bfloat16)
    local_ids = block_ids - (z - 1) * blocks_here
    source = wide_msg.reshape(3 * blocks_here, BLOCK, width)[local_ids]
    slots = block_ids.shape[1]
    live_mask = (jnp.arange(slots, dtype=jnp.int32)[None, :] < block_counts[:, None]).astype(jnp.bfloat16)
    live = edge_tiles * live_mask[:, :, None, None]
    agg = jnp.einsum("bsij,bsjd->bid", live, source, preferred_element_type=jnp.float32).reshape(
        node_rows, width
    )
    grad_wide = out_grad.astype(jnp.float32)
    sigma = jax.nn.sigmoid(agg)
    d_agg = (grad_wide * sigma * (1.0 + agg * (1.0 - sigma))).astype(jnp.bfloat16)
    contrib = jnp.einsum(
        "bsij,bid->bsjd",
        live,
        d_agg.reshape(blocks_here, BLOCK, width),
        preferred_element_type=jnp.float32,
    )
    tally = (
        local_ids[:, :, None] == jnp.arange(3 * blocks_here, dtype=jnp.int32)[None, None, :]
    ).astype(jnp.float32)
    landed = jnp.einsum("bsk,bsjd->kjd", tally, contrib, precision=lax.Precision.HIGHEST)
    from_above = down(landed[:blocks_here].astype(jnp.bfloat16)).astype(jnp.float32)
    from_below = up(landed[2 * blocks_here :].astype(jnp.bfloat16)).astype(jnp.float32)
    d_msg = (
        (landed[blocks_here : 2 * blocks_here] + from_above + from_below)
        .reshape(node_rows, width)
        .astype(jnp.bfloat16)
    )
    sum_msg = sum_over_chips(sum_over_cores(*halves(contract_rows(normed, d_msg))))
    rows_msg = sum_msg.shape[0]
    cut_msg = sum_msg.astype(jnp.bfloat16).reshape(rows_msg, N_SEQ, width // N_SEQ).transpose(1, 0, 2)
    share_msg = jnp.sum(exchange(cut_msg, "z").astype(jnp.float32), axis=0).astype(jnp.bfloat16)

    att, *saved = attend_forward(place, chunks, w_head, d_heads)
    att_home = exchange(att, "z")
    d_heads_qk, keep, give = attend_backward(place, chunks, att, saved)

    out_rows = att_home[:, :, :HEAD_DIM].transpose(1, 0, 2).reshape(node_rows, hd)
    dv_rows = att_home[:, :, HEAD_DIM:].transpose(1, 0, 2).reshape(node_rows, hd)
    attn_part = jnp.dot(out_rows, w_out, preferred_element_type=jnp.float32)
    block_result_array = (feat_wide + attn_part + agg * sigma).astype(jnp.bfloat16)
    pair_out = sum_over_cores(*halves(contract_rows(out_rows, out_grad)))
    rows_out = pair_out.shape[1]

    pair_head = sum_over_cores(keep, give)
    lanes = pair_head.shape[2]
    pair_out = pair_out.reshape(N_XY, rows_out, width // lanes, lanes).transpose(0, 2, 1, 3)
    pair = jnp.concatenate([pair_head, pair_out.reshape(N_XY, -1, lanes)], axis=1)
    both = sum_over_chips(pair)
    sum_head = both[:rows_msg]
    sum_out = both[rows_msg:]

    dqk_home = exchange(d_heads_qk, "z")
    dq_rows = dqk_home[:, :, :HEAD_DIM].transpose(1, 0, 2).reshape(node_rows, hd)
    dk_rows = dqk_home[:, :, HEAD_DIM:].transpose(1, 0, 2).reshape(node_rows, hd)
    d_proj = jnp.concatenate([dq_rows, dk_rows, dv_rows], axis=1)
    d_norm = contract_cols(d_proj, w_qkv) + contract_cols(d_msg, w_msg)
    scaled = d_norm * norm_gain
    d_feat = inv_rms * (scaled - x_hat * jnp.mean(scaled * x_hat, axis=-1, keepdims=True))
    grad_input = (grad_wide + d_feat).astype(jnp.bfloat16)

    mine = jnp.concatenate(
        [sum_head[:, :BLOCK], sum_head[:, BLOCK:], sum_out[:, :BLOCK], sum_out[:, BLOCK:]], axis=0
    ).astype(jnp.bfloat16)
    mine = jnp.concatenate([mine, share_msg], axis=0)
    every = exchange(jnp.broadcast_to(mine[None], (N_SEQ,) + mine.shape), "z")
    nodes = N_SEQ * node_rows
    first_block = every[:, :rows_msg]
    heads = jnp.stack(
        [first_block[:, :, :HEAD_DIM], first_block[:, :, HEAD_DIM:], every[:, rows_msg : 2 * rows_msg, :HEAD_DIM]]
    )
    grad_qkv = heads.transpose(2, 0, 1, 3).reshape(rows_msg, 3 * hd).astype(jnp.float32) / nodes
    count = sum_out.shape[0]
    tall = jnp.sum(every[:, 2 * rows_msg : 2 * rows_msg + 2 * count].astype(jnp.float32), axis=0) / nodes
    tall = tall.reshape(2, width // lanes, rows_out, BLOCK).transpose(2, 1, 0, 3)
    grad_out = tall.reshape(rows_out, width)
    grad_msg = every[:, 2 * rows_msg + 2 * count :].transpose(1, 0, 2).reshape(rows_msg, width).astype(jnp.float32)
    grad_msg = grad_msg / nodes

    first = ((lax.axis_index("x") * 4 + lax.axis_index("y")) * 2 + core) * rows_msg
    w_rows = lax.dynamic_slice_in_dim(w_qkv, first, rows_msg, 0).astype(jnp.float32)
    m_rows = lax.dynamic_slice_in_dim(w_msg, first, rows_msg, 0).astype(jnp.float32)
    gain_rows = lax.dynamic_slice_in_dim(norm_gain, first, rows_msg, 0)
    grad_gain = (
        jnp.sum(w_rows * grad_qkv, axis=1) + jnp.sum(m_rows * grad_msg, axis=1)
    ) / gain_rows
    return block_result_array, grad_input, grad_gain, grad_qkv, grad_out, grad_msg


def solution(mesh):
    fine = Mesh(mesh.devices.reshape(4, 4, 2, N_SEQ), ("x", "y", "c", "z"))
    dp = ("x", "y", "c")
    rows = ("x", "y", "c", "z")
    return jax.shard_map(
        on_device,
        mesh=fine,
        in_specs=(
            P(rows, None),
            P(rows, None),
            P(),
            P(),
            P(),
            P(),
            P(rows, None),
            P(rows),
            P(rows, None, None, None),
        ),
        out_specs=(
            P(rows, None),
            P(rows, None),
            P(dp),
            P(dp, None),
            P(dp, None),
            P(dp, None),
        ),
        check_vma=False,
    )
```

```python
import jax
import jax.numpy as jnp
from jax import lax
from jax.experimental import pallas as pl
from jax.experimental.pallas import tpu as pltpu
from jax.sharding import Mesh
from jax.sharding import PartitionSpec as P

HEAD_DIM = 64
BLOCK = 128
SLOTS = 4
N_SEQ = 8
N_XY = 16
CHUNK = 256
ONES = 16

exponent_divisor = 32.0
epsilon = 1e-06
SCALE = exponent_divisor / HEAD_DIM


def matmul(left, right):
    return jnp.dot(left, right, preferred_element_type=jnp.float32)


def contract_rows(left, right):
    return lax.dot_general(
        left, right, (((0,), (0,)), ((), ())), preferred_element_type=jnp.float32
    )


def contract_cols(left, right):
    return lax.dot_general(
        left, right, (((1,), (1,)), ((), ())), preferred_element_type=jnp.float32
    )


def unit_factor(wide, axis):
    return lax.rsqrt(jnp.mean(wide * wide, axis=axis, keepdims=True) + epsilon)


def call(kernel, name, out_shape, scalars, arrays, scratch=(), flops=0, exps=0, moved=0):
    specs = [pl.BlockSpec(memory_space=pltpu.SMEM)] * len(scalars)
    specs += [pl.BlockSpec(memory_space=pltpu.VMEM)] * len(arrays)
    return pl.pallas_call(
        kernel,
        out_shape=tuple(jax.ShapeDtypeStruct(s, t) for s, t in out_shape),
        in_specs=specs,
        out_specs=tuple(pl.BlockSpec(memory_space=pltpu.VMEM) for _ in out_shape),
        scratch_shapes=list(scratch),
        compiler_params=pltpu.CompilerParams(vmem_limit_bytes=50 * 1024 * 1024),
        cost_estimate=pl.CostEstimate(flops=flops, bytes_accessed=moved, transcendentals=exps),
        name=name,
    )(*scalars, *arrays)


def normalize_kernel(x_ref, gain_ref, out_ref):
    wide = x_ref[...].astype(jnp.float32)
    out_ref[...] = (wide * unit_factor(wide, -1) * gain_ref[...]).astype(jnp.bfloat16)


def d_out_kernel(place_ref, grad_ref, w_ref, out_ref, turned):
    z = place_ref[0]
    turned[...] = contract_cols(w_ref[...], grad_ref[...])
    for s in range(N_SEQ):
        head = lax.rem(z + s, N_SEQ)
        out_ref[s] = turned[pl.ds(head * HEAD_DIM, HEAD_DIM), :].astype(jnp.bfloat16)


def pick_kernel(place_ref, q_ref, k_ref, v_ref, out_ref, turned):
    odd = lax.rem(place_ref[0], 2)
    for t, ref in enumerate((q_ref, k_ref, v_ref)):
        turned[...] = ref[...].astype(jnp.float32).T
        out_ref[t * HEAD_DIM : (t + 1) * HEAD_DIM] = turned[
            pl.ds(odd * HEAD_DIM, HEAD_DIM), :
        ].astype(jnp.bfloat16)


def pick_head(place, w_qkv):
    width, columns = w_qkv.shape
    step = columns // 3 // (2 * HEAD_DIM)

    def block(t):
        return pl.BlockSpec((width, 2 * HEAD_DIM), lambda i, place: (0, t * step + place[0] // 2))

    return pl.pallas_call(
        pick_kernel,
        grid_spec=pltpu.PrefetchScalarGridSpec(
            num_scalar_prefetch=1,
            grid=(1,),
            in_specs=[block(0), block(1), block(2)],
            out_specs=pl.BlockSpec((3 * HEAD_DIM, width), lambda i, place: (0, 0)),
            scratch_shapes=[pltpu.VMEM((2 * HEAD_DIM, width), jnp.float32)],
        ),
        out_shape=jax.ShapeDtypeStruct((3 * HEAD_DIM, width), jnp.bfloat16),
        cost_estimate=pl.CostEstimate(flops=0, bytes_accessed=4 << 20, transcendentals=0),
        name="pick_head",
    )(place, w_qkv, w_qkv, w_qkv)


def message_kernel(*refs):
    place_ref, ids_ref, counts_ref, low_ref, own_ref, high_ref, w_ref, tiles_ref, grad_ref = refs[:9]
    act_ref, to_low_ref, mid_ref, to_high_ref, msg, landed = refs[9:]
    z = place_ref[0]
    for t, ref in enumerate((low_ref, own_ref, high_ref)):
        rows = matmul(ref[...], w_ref[...]).astype(jnp.bfloat16)
        msg[2 * t] = rows[:BLOCK]
        msg[2 * t + 1] = rows[BLOCK:]
    landed[...] = jnp.zeros_like(landed)
    for b in range(2):
        spots = []
        live = []
        for s in range(SLOTS):
            spots.append(jnp.clip(ids_ref[b, s] - 2 * (z - 1), 0, 5))
            mask = jnp.where(s < counts_ref[b], 1.0, 0.0)
            live.append(tiles_ref[b, s].astype(jnp.float32) * mask)
        source = jnp.concatenate([msg[spot] for spot in spots], axis=0)
        agg = matmul(jnp.concatenate(live, axis=1).astype(jnp.bfloat16), source)
        sigma = 1.0 / (1.0 + jnp.exp(-agg))
        rows = slice(b * BLOCK, (b + 1) * BLOCK)
        act_ref[rows] = agg * sigma
        d_agg = grad_ref[rows].astype(jnp.float32) * sigma * (1.0 + agg * (1.0 - sigma))
        d_agg = d_agg.astype(jnp.bfloat16)
        for s in range(SLOTS):
            landed[spots[s]] += matmul(live[s].T.astype(jnp.bfloat16), d_agg)
    for b in range(2):
        rows = slice(b * BLOCK, (b + 1) * BLOCK)
        to_low_ref[rows] = landed[b].astype(jnp.bfloat16)
        mid_ref[rows] = landed[2 + b]
        to_high_ref[rows] = landed[4 + b].astype(jnp.bfloat16)


def split_rows(core, source, keep_ref, give_ref):
    rows = source.shape[0] // (2 * N_XY)
    for i in range(N_XY):
        keep_ref[i] = source[pl.ds((2 * i + core) * rows, rows), :].astype(jnp.bfloat16)
        give_ref[i] = source[pl.ds((2 * i + 1 - core) * rows, rows), :].astype(jnp.bfloat16)


def message_grad_kernel(*refs):
    place_ref, mid_ref, above_ref, below_ref, normed_ref, w_ref = refs[:6]
    keep_ref, give_ref, d_norm_ref, grad = refs[6:]
    total = mid_ref[...] + above_ref[...].astype(jnp.float32) + below_ref[...].astype(jnp.float32)
    d_msg = total.astype(jnp.bfloat16)
    d_norm_ref[...] = contract_cols(d_msg, w_ref[...])
    grad[...] = contract_rows(normed_ref[...], d_msg)
    split_rows(place_ref[1], grad, keep_ref, give_ref)


def forward_kernel(*refs):
    chunks = refs[:8]
    w_ref = refs[8]
    d_refs = refs[9:17]
    out_ref, kv_ref, qd_ref, hq_ref, ku_ref, raw_ref, stats_ref = refs[17:24]
    v_ext = refs[24]
    for j in range(N_SEQ):
        proj = contract_cols(w_ref[...], chunks[j][...]).astype(jnp.bfloat16)
        raw_ref[j] = proj[: 2 * HEAD_DIM]
        query = proj[:HEAD_DIM].astype(jnp.float32)
        keyrow = proj[HEAD_DIM : 2 * HEAD_DIM].astype(jnp.float32)
        val = proj[2 * HEAD_DIM :]
        q_unit = (query * unit_factor(query, 0)).astype(jnp.bfloat16).astype(jnp.float32) * SCALE
        k_unit = keyrow * unit_factor(keyrow, 0)
        hq_ref[j] = q_unit.astype(jnp.bfloat16)
        ku_ref[j] = k_unit.astype(jnp.bfloat16)
        v_ext[j, :HEAD_DIM] = val
        v_ext[j, HEAD_DIM:] = jnp.ones((ONES, CHUNK), jnp.bfloat16)
        kv_ref[j] = jnp.concatenate([k_unit, val.astype(jnp.float32)], axis=0).T.astype(jnp.bfloat16)
        d_head = d_refs[j][...].astype(jnp.float32)
        qd_ref[j] = jnp.concatenate([q_unit, d_head], axis=0).T.astype(jnp.bfloat16)

    def step(i, carry):
        query = jnp.concatenate([hq_ref[i], jnp.zeros_like(hq_ref[i])], axis=0)
        out = jnp.zeros((HEAD_DIM + ONES, CHUNK), jnp.float32)
        for j in range(N_SEQ):
            exps = jnp.exp(matmul(kv_ref[j], query)).astype(jnp.bfloat16)
            out += matmul(v_ext[j], exps)
        inverse = 1.0 / out[HEAD_DIM : HEAD_DIM + 1]
        stats_ref[i, 0:1] = inverse
        out_ref[i] = (out[:HEAD_DIM] * inverse).astype(jnp.bfloat16)
        return carry

    lax.fori_loop(0, N_SEQ, step, 0)
    for j in range(N_SEQ):
        out = out_ref[j].astype(jnp.float32)
        stats_ref[j, 1:2] = jnp.sum(out * d_refs[j][...].astype(jnp.float32), axis=0, keepdims=True)


def backward_kernel(*refs):
    place_ref = refs[0]
    chunks = refs[1:9]
    kv_ref, qd_ref, hq_ref, ku_ref, raw_ref, stats_ref = refs[9:15]
    d_refs = refs[15:23]
    stack_ref, keep_ref, give_ref = refs[23:26]
    sums, dqt, d_all, grad_t, grad = refs[26:31]
    sums[...] = jnp.zeros_like(sums)
    for j in range(N_SEQ):
        d_all[j] = d_refs[j][...]

    def step(i, carry):
        zero = jnp.zeros_like(hq_ref[i])
        query = jnp.concatenate([hq_ref[i], zero], axis=0)
        d_head = jnp.concatenate([zero, d_all[i]], axis=0)
        rows = qd_ref[i].astype(jnp.float32)
        left = lax.broadcasted_iota(jnp.int32, rows.shape, 1) < HEAD_DIM
        rhs = jnp.concatenate([jnp.where(left, 0.0, rows), jnp.where(left, rows, 0.0)], axis=0)
        rhs = rhs.astype(jnp.bfloat16)
        inverse = stats_ref[i, 0:1]
        row_dot = stats_ref[i, 1:2]
        d_qunit = jnp.zeros((HEAD_DIM, CHUNK), jnp.float32)
        for j in range(N_SEQ):
            prob = jnp.exp(matmul(kv_ref[j], query)) * inverse
            d_scores = (prob * (matmul(kv_ref[j], d_head) - row_dot)).astype(jnp.bfloat16)
            d_qunit += matmul(ku_ref[j], d_scores)
            both = jnp.concatenate([prob.astype(jnp.bfloat16), d_scores], axis=1)
            sums[j] += matmul(both, rhs)
        dqt[i] = d_qunit * SCALE
        return carry

    lax.fori_loop(0, N_SEQ, step, 0)
    for j in range(N_SEQ):
        turned = sums[j].T
        pieces = []
        for t, d_unit in enumerate((dqt[j], turned[:HEAD_DIM])):
            wide = raw_ref[j, t * HEAD_DIM : (t + 1) * HEAD_DIM].astype(jnp.float32)
            factor = unit_factor(wide, 0)
            mean = jnp.mean(d_unit * wide, axis=0, keepdims=True)
            pieces.append(factor * d_unit - factor * factor * factor * wide * mean)
        stacked = jnp.concatenate(pieces + [turned[HEAD_DIM:]], axis=0).astype(jnp.bfloat16)
        stack_ref[j] = stacked
        term = matmul(stacked, chunks[j][...])
        if j == 0:
            grad_t[: 3 * HEAD_DIM] = term
        else:
            grad_t[: 3 * HEAD_DIM] += term
    grad_t[3 * HEAD_DIM :] = jnp.zeros((HEAD_DIM, grad_t.shape[1]), jnp.float32)
    grad[...] = grad_t[...].T
    split_rows(place_ref[1], grad, keep_ref, give_ref)


def result_kernel(*refs):
    place_ref = refs[0]
    heads = refs[1:9]
    w_ref, grad_ref, x_ref, act_ref = refs[9:13]
    out_ref, keep_ref, give_ref, gathered, grad = refs[13:]
    z = place_ref[0]
    for j in range(N_SEQ):
        head = lax.rem(z + j, N_SEQ)
        gathered[pl.ds(head * HEAD_DIM, HEAD_DIM), :] = heads[j][...]
    every = gathered[...]
    grad[...] = matmul(every, grad_ref[...])
    split_rows(place_ref[1], grad, keep_ref, give_ref)
    attn = contract_rows(every, w_ref[...])
    out_ref[...] = (x_ref[...].astype(jnp.float32) + attn + act_ref[...]).astype(jnp.bfloat16)


def input_grad_kernel(*refs):
    place_ref = refs[0]
    stacks = refs[1:9]
    w_ref, d_norm_ref, x_ref, grad_ref, gain_ref = refs[9:14]
    out_ref, gathered = refs[14:]
    z = place_ref[0]
    hd = N_SEQ * HEAD_DIM
    for j in range(N_SEQ):
        head = lax.rem(z + j, N_SEQ)
        for t in range(3):
            gathered[pl.ds(t * hd + head * HEAD_DIM, HEAD_DIM), :] = stacks[j][
                t * HEAD_DIM : (t + 1) * HEAD_DIM
            ]
    d_norm = matmul(w_ref[...], gathered[...]).T + d_norm_ref[...]
    wide = x_ref[...].astype(jnp.float32)
    inv_rms = unit_factor(wide, -1)
    x_hat = wide * inv_rms
    scaled = d_norm * gain_ref[...]
    d_feat = inv_rms * (scaled - x_hat * jnp.mean(scaled * x_hat, axis=-1, keepdims=True))
    out_ref[...] = (grad_ref[...].astype(jnp.float32) + d_feat).astype(jnp.bfloat16)


def after(value, *others):
    return lax.optimization_barrier((value,) + others)[0]


def exchange(array, axis):
    return lax.all_to_all(array, axis, split_axis=0, concat_axis=0, tiled=True)


def shift(array, distance):
    return lax.ppermute(array, "z", [(i, (i + distance) % N_SEQ) for i in range(N_SEQ)])


def up(array):
    return shift(array, 1)


def down(array):
    return shift(array, -1)


def sum_over_cores(keep, give):
    got = lax.ppermute(give, "c", [(0, 1), (1, 0)])
    return (keep.astype(jnp.float32) + got.astype(jnp.float32)).astype(jnp.bfloat16)


def sum_over_chips(pair):
    return jnp.sum(exchange(pair, ("x", "y")).astype(jnp.float32), axis=0)


def on_device(
    features, out_grad, norm_gain, w_qkv, w_out, w_msg, block_ids, block_counts, edge_tiles
):
    node_rows, width = features.shape
    hd = w_out.shape[0]
    nodes = N_SEQ * node_rows
    bf16, f32 = jnp.bfloat16, jnp.float32
    z = lax.axis_index("z")
    core = lax.axis_index("c")
    place = jnp.stack([z, core]).astype(jnp.int32)
    gain = norm_gain.reshape(1, width)
    wide_shape = ((node_rows, width), f32)
    low_shape = ((node_rows, width), bf16)

    (normed,) = call(normalize_kernel, "normalize", (low_shape,), (), (features, gain), moved=1 << 20)

    a1, b1 = up(normed), down(normed)
    (d_out,) = call(
        d_out_kernel, "d_out", (((N_SEQ, HEAD_DIM, node_rows), bf16),), (place,), (out_grad, w_out),
        [pltpu.VMEM((hd, node_rows), f32)], flops=2 * node_rows * width * hd, moved=2 << 20,
    )
    d_heads = [d_out[0]] + [shift(d_out[s], s) for s in range(1, N_SEQ)]
    w_head = pick_head(place, w_qkv)
    a1, b1, *d_heads = lax.optimization_barrier((a1, b1, *d_heads))
    a2, b2 = up(a1), down(b1)

    act, to_low, mid, to_high = call(
        message_kernel, "messages", (wide_shape, low_shape, wide_shape, low_shape),
        (place, block_ids, block_counts), (a1, normed, b1, w_msg, edge_tiles, out_grad),
        [pltpu.VMEM((6, BLOCK, width), bf16), pltpu.VMEM((6, BLOCK, width), f32)],
        flops=8 * node_rows * width * width, exps=node_rows * width, moved=8 << 20,
    )
    a2, b2, w_head, to_low, to_high = lax.optimization_barrier((a2, b2, w_head, to_low, to_high))
    a3, b3 = up(a2), down(b2)
    above, below = down(to_low), up(to_high)
    half = node_rows // 2
    a3, b3 = lax.optimization_barrier((a3, b3))
    c4 = jnp.concatenate([up(a3[:half]), down(b3[half:])], axis=0)
    chunks = (normed, a1, a2, a3, c4, b3, b2, b1)

    rows_here = width // (2 * N_XY)
    part_msg = ((N_XY, rows_here, width), bf16)
    keep, give, d_norm = call(
        message_grad_kernel, "message_grad", (part_msg, part_msg, wide_shape), (place,),
        (mid, above, below, normed, w_msg), [pltpu.VMEM((width, width), f32)],
        flops=4 * node_rows * width * width, moved=8 << 20,
    )
    sum_msg = sum_over_chips(sum_over_cores(keep, give))

    lanes_in = ((N_SEQ, CHUNK, 2 * HEAD_DIM), bf16)
    turned = ((N_SEQ, HEAD_DIM, CHUNK), bf16)
    out_t, *saved = call(
        forward_kernel, "attend_forward",
        (turned, lanes_in, lanes_in, turned, turned,
         ((N_SEQ, 2 * HEAD_DIM, CHUNK), bf16), ((N_SEQ, 8, CHUNK), f32)),
        (), chunks + (w_head, *d_heads),
        [pltpu.VMEM((N_SEQ, HEAD_DIM + ONES, CHUNK), bf16)],
        flops=12 * nodes * nodes * HEAD_DIM, exps=nodes * nodes, moved=8 << 20,
    )
    heads = [out_t[0]] + [shift(out_t[j], -j) for j in range(1, N_SEQ)]

    cut_msg = sum_msg.astype(bf16).reshape(rows_here, N_SEQ, width // N_SEQ).transpose(1, 0, 2)
    share_msg = jnp.sum(exchange(cut_msg, "z").astype(f32), axis=0).astype(bf16)

    part_head = ((N_XY, rows_here, 4 * HEAD_DIM), bf16)
    stack, keep, give = call(
        backward_kernel, "attend_backward",
        (((N_SEQ, 3 * HEAD_DIM, CHUNK), bf16), part_head, part_head),
        (place,), chunks + (*saved, *d_heads),
        [
            pltpu.VMEM((N_SEQ, CHUNK, 2 * HEAD_DIM), f32),
            pltpu.VMEM((N_SEQ, HEAD_DIM, CHUNK), f32),
            pltpu.VMEM((N_SEQ, HEAD_DIM, CHUNK), bf16),
            pltpu.VMEM((4 * HEAD_DIM, width), f32),
            pltpu.VMEM((width, 4 * HEAD_DIM), f32),
        ],
        flops=24 * nodes * nodes * HEAD_DIM, exps=nodes * nodes, moved=8 << 20,
    )
    stacks = [stack[0]] + [shift(stack[j], -j) for j in range(1, N_SEQ)]

    rows_out = hd // (2 * N_XY)
    part_out = ((N_XY, rows_out, width), bf16)
    block_result_array, keep_out, give_out = call(
        result_kernel, "result", (low_shape, part_out, part_out), (place,),
        (*heads, w_out, out_grad, features, act),
        [pltpu.VMEM((hd, node_rows), bf16), pltpu.VMEM((hd, width), f32)],
        flops=4 * node_rows * width * hd, moved=6 << 20,
    )
    pair_out = sum_over_cores(keep_out, give_out)
    pair_head = sum_over_cores(keep, give)
    lanes = pair_head.shape[2]
    pair_out = pair_out.reshape(N_XY, rows_out, width // lanes, lanes).transpose(0, 2, 1, 3)
    pair = jnp.concatenate([pair_head, pair_out.reshape(N_XY, -1, lanes)], axis=1)
    both = sum_over_chips(pair)
    sum_head = both[:rows_here]
    sum_out = both[rows_here:]

    (grad_input,) = call(
        input_grad_kernel, "input_grad", (low_shape,), (place,),
        (*stacks, w_qkv, d_norm, features, out_grad, gain),
        [pltpu.VMEM((3 * hd, node_rows), bf16)],
        flops=6 * node_rows * width * hd, moved=8 << 20,
    )

    mine = jnp.concatenate(
        [sum_head[:, :BLOCK], sum_head[:, BLOCK:], sum_out[:, :BLOCK], sum_out[:, BLOCK:]], axis=0
    ).astype(bf16)
    mine = jnp.concatenate([mine, share_msg], axis=0)
    every = exchange(jnp.broadcast_to(mine[None], (N_SEQ,) + mine.shape), "z")
    first_block = every[:, :rows_here]
    cut = jnp.stack(
        [first_block[:, :, :HEAD_DIM], first_block[:, :, HEAD_DIM:], every[:, rows_here : 2 * rows_here, :HEAD_DIM]]
    )
    grad_qkv = cut.transpose(2, 0, 1, 3).reshape(rows_here, 3 * hd).astype(f32) / nodes
    count = sum_out.shape[0]
    tall = jnp.sum(every[:, 2 * rows_here : 2 * rows_here + 2 * count].astype(f32), axis=0) / nodes
    grad_out = tall.reshape(2, width // lanes, rows_out, BLOCK).transpose(2, 1, 0, 3).reshape(rows_out, width)
    grad_msg = every[:, 2 * rows_here + 2 * count :].transpose(1, 0, 2).reshape(rows_here, width)
    grad_msg = grad_msg.astype(f32) / nodes

    first = ((lax.axis_index("x") * 4 + lax.axis_index("y")) * 2 + core) * rows_here
    w_rows = lax.dynamic_slice_in_dim(w_qkv, first, rows_here, 0).astype(f32)
    m_rows = lax.dynamic_slice_in_dim(w_msg, first, rows_here, 0).astype(f32)
    gain_rows = lax.dynamic_slice_in_dim(norm_gain, first, rows_here, 0)
    grad_gain = (
        jnp.sum(w_rows * grad_qkv, axis=1) + jnp.sum(m_rows * grad_msg, axis=1)
    ) / gain_rows
    return block_result_array, grad_input, grad_gain, grad_qkv, grad_out, grad_msg


def solution(mesh):
    fine = Mesh(mesh.devices.reshape(4, 4, 2, N_SEQ), ("x", "y", "c", "z"))
    dp = ("x", "y", "c")
    rows = ("x", "y", "c", "z")
    return jax.shard_map(
        on_device,
        mesh=fine,
        in_specs=(
            P(rows, None),
            P(rows, None),
            P(),
            P(),
            P(),
            P(),
            P(rows, None),
            P(rows),
            P(rows, None, None, None),
        ),
        out_specs=(
            P(rows, None),
            P(rows, None),
            P(dp),
            P(dp, None),
            P(dp, None),
            P(dp, None),
        ),
        check_vma=False,
    )
```

```python
import jax
import jax.numpy as jnp
from jax import lax
from jax.experimental import pallas as pl
from jax.experimental.pallas import tpu as pltpu
from jax.sharding import Mesh
from jax.sharding import PartitionSpec as P

HEAD_DIM = 64
BLOCK = 128
SLOTS = 4
N_SEQ = 8
N_XY = 16
CHUNK = 256
ONES = 16

exponent_divisor = 32.0
epsilon = 1e-06
SCALE = exponent_divisor / HEAD_DIM


def matmul(left, right):
    return jnp.dot(left, right, preferred_element_type=jnp.float32)


def contract_rows(left, right):
    return lax.dot_general(
        left, right, (((0,), (0,)), ((), ())), preferred_element_type=jnp.float32
    )


def contract_cols(left, right):
    return lax.dot_general(
        left, right, (((1,), (1,)), ((), ())), preferred_element_type=jnp.float32
    )


def unit_factor(wide, axis):
    return lax.rsqrt(jnp.mean(wide * wide, axis=axis, keepdims=True) + epsilon)


def call(kernel, name, out_shape, scalars, arrays, scratch=(), flops=0, exps=0, moved=0):
    specs = [pl.BlockSpec(memory_space=pltpu.SMEM)] * len(scalars)
    specs += [pl.BlockSpec(memory_space=pltpu.VMEM)] * len(arrays)
    return pl.pallas_call(
        kernel,
        out_shape=tuple(jax.ShapeDtypeStruct(s, t) for s, t in out_shape),
        in_specs=specs,
        out_specs=tuple(pl.BlockSpec(memory_space=pltpu.VMEM) for _ in out_shape),
        scratch_shapes=list(scratch),
        compiler_params=pltpu.CompilerParams(vmem_limit_bytes=50 * 1024 * 1024),
        cost_estimate=pl.CostEstimate(flops=flops, bytes_accessed=moved, transcendentals=exps),
        name=name,
    )(*scalars, *arrays)


def normalize_kernel(x_ref, gain_ref, out_ref):
    wide = x_ref[...].astype(jnp.float32)
    out_ref[...] = (wide * unit_factor(wide, -1) * gain_ref[...]).astype(jnp.bfloat16)


def d_out_kernel(grad_ref, w_ref, out_ref):
    turned = contract_cols(w_ref[...], grad_ref[...]).astype(jnp.bfloat16)
    for h in range(N_SEQ):
        out_ref[h] = turned[h * HEAD_DIM : (h + 1) * HEAD_DIM]


def pick_kernel(place_ref, q_ref, k_ref, v_ref, out_ref, turned):
    odd = lax.rem(place_ref[0], 2)
    for t, ref in enumerate((q_ref, k_ref, v_ref)):
        turned[...] = ref[...].astype(jnp.float32).T
        out_ref[t * HEAD_DIM : (t + 1) * HEAD_DIM] = turned[
            pl.ds(odd * HEAD_DIM, HEAD_DIM), :
        ].astype(jnp.bfloat16)


def pick_head(place, w_qkv):
    width, columns = w_qkv.shape
    step = columns // 3 // (2 * HEAD_DIM)

    def block(t):
        return pl.BlockSpec((width, 2 * HEAD_DIM), lambda i, place: (0, t * step + place[0] // 2))

    return pl.pallas_call(
        pick_kernel,
        grid_spec=pltpu.PrefetchScalarGridSpec(
            num_scalar_prefetch=1,
            grid=(1,),
            in_specs=[block(0), block(1), block(2)],
            out_specs=pl.BlockSpec((3 * HEAD_DIM, width), lambda i, place: (0, 0)),
            scratch_shapes=[pltpu.VMEM((2 * HEAD_DIM, width), jnp.float32)],
        ),
        out_shape=jax.ShapeDtypeStruct((3 * HEAD_DIM, width), jnp.bfloat16),
        cost_estimate=pl.CostEstimate(flops=0, bytes_accessed=4 << 20, transcendentals=0),
        name="pick_head",
    )(place, w_qkv, w_qkv, w_qkv)


def message_kernel(*refs):
    place_ref, ids_ref, counts_ref, low_ref, own_ref, high_ref, w_ref, tiles_ref, grad_ref = refs[:9]
    act_ref, to_low_ref, mid_ref, to_high_ref, msg, landed = refs[9:]
    z = place_ref[0]
    for t, ref in enumerate((low_ref, own_ref, high_ref)):
        rows = matmul(ref[...], w_ref[...]).astype(jnp.bfloat16)
        msg[2 * t] = rows[:BLOCK]
        msg[2 * t + 1] = rows[BLOCK:]
    landed[...] = jnp.zeros_like(landed)
    for b in range(2):
        spots = []
        live = []
        for s in range(SLOTS):
            spots.append(jnp.clip(ids_ref[b, s] - 2 * (z - 1), 0, 5))
            mask = jnp.where(s < counts_ref[b], 1.0, 0.0)
            live.append(tiles_ref[b, s].astype(jnp.float32) * mask)
        source = jnp.concatenate([msg[spot] for spot in spots], axis=0)
        agg = matmul(jnp.concatenate(live, axis=1).astype(jnp.bfloat16), source)
        sigma = 1.0 / (1.0 + jnp.exp(-agg))
        rows = slice(b * BLOCK, (b + 1) * BLOCK)
        act_ref[rows] = agg * sigma
        d_agg = grad_ref[rows].astype(jnp.float32) * sigma * (1.0 + agg * (1.0 - sigma))
        d_agg = d_agg.astype(jnp.bfloat16)
        for s in range(SLOTS):
            landed[spots[s]] += matmul(live[s].T.astype(jnp.bfloat16), d_agg)
    for b in range(2):
        rows = slice(b * BLOCK, (b + 1) * BLOCK)
        to_low_ref[rows] = landed[b].astype(jnp.bfloat16)
        mid_ref[rows] = landed[2 + b]
        to_high_ref[rows] = landed[4 + b].astype(jnp.bfloat16)


def split_rows(core, source, keep_ref, give_ref, offset=0):
    rows = source.shape[0] // (2 * N_XY)
    for i in range(N_XY):
        for t in range(source.shape[1] // BLOCK):
            spot = slice(offset + t * rows, offset + (t + 1) * rows)
            columns = slice(t * BLOCK, (t + 1) * BLOCK)
            keep_ref[i, spot] = source[pl.ds((2 * i + core) * rows, rows), columns].astype(jnp.bfloat16)
            give_ref[i, spot] = source[pl.ds((2 * i + 1 - core) * rows, rows), columns].astype(
                jnp.bfloat16
            )


def message_grad_kernel(*refs):
    mid_ref, above_ref, below_ref, w_ref = refs[:4]
    cut_ref, d_norm_ref = refs[4:]
    total = mid_ref[...] + above_ref[...].astype(jnp.float32) + below_ref[...].astype(jnp.float32)
    d_msg = total.astype(jnp.bfloat16)
    for t in range(N_SEQ):
        cut_ref[t] = d_msg[:, t * BLOCK : (t + 1) * BLOCK]
    d_norm_ref[...] = contract_cols(d_msg, w_ref[...])


def place_of(z, j):
    return lax.rem(z - j + N_SEQ, N_SEQ)


def forward_kernel(*refs):
    z = refs[0][0]
    chunks = refs[1:9]
    w_ref, d_ref = refs[9:11]
    out_ref, kv_ref, qd_ref, hq_ref, ku_ref, raw_ref, stats_ref = refs[11:18]
    v_ext = refs[18]
    for j in range(N_SEQ):
        proj = contract_cols(w_ref[...], chunks[j][...]).astype(jnp.bfloat16)
        raw_ref[j] = proj[: 2 * HEAD_DIM]
        query = proj[:HEAD_DIM].astype(jnp.float32)
        keyrow = proj[HEAD_DIM : 2 * HEAD_DIM].astype(jnp.float32)
        val = proj[2 * HEAD_DIM :]
        q_unit = (query * unit_factor(query, 0)).astype(jnp.bfloat16).astype(jnp.float32) * SCALE
        k_unit = keyrow * unit_factor(keyrow, 0)
        hq_ref[j] = q_unit.astype(jnp.bfloat16)
        ku_ref[j] = k_unit.astype(jnp.bfloat16)
        v_ext[j, :HEAD_DIM] = val
        v_ext[j, HEAD_DIM:] = jnp.ones((ONES, CHUNK), jnp.bfloat16)
        kv_ref[j] = jnp.concatenate([k_unit, val.astype(jnp.float32)], axis=0).T.astype(jnp.bfloat16)
        d_head = d_ref[place_of(z, j)].astype(jnp.float32)
        qd_ref[j] = jnp.concatenate([q_unit, d_head], axis=0).T.astype(jnp.bfloat16)

    def step(i, carry):
        query = jnp.concatenate([hq_ref[i], jnp.zeros_like(hq_ref[i])], axis=0)
        out = jnp.zeros((HEAD_DIM + ONES, CHUNK), jnp.float32)
        for j in range(N_SEQ):
            exps = jnp.exp(matmul(kv_ref[j], query)).astype(jnp.bfloat16)
            out += matmul(v_ext[j], exps)
        inverse = 1.0 / out[HEAD_DIM : HEAD_DIM + 1]
        stats_ref[i, 0:1] = inverse
        out_ref[place_of(z, i)] = (out[:HEAD_DIM] * inverse).astype(jnp.bfloat16)
        return carry

    lax.fori_loop(0, N_SEQ, step, 0)
    for j in range(N_SEQ):
        out = out_ref[place_of(z, j)].astype(jnp.float32)
        d_head = d_ref[place_of(z, j)].astype(jnp.float32)
        stats_ref[j, 1:2] = jnp.sum(out * d_head, axis=0, keepdims=True)


def backward_kernel(*refs):
    place_ref = refs[0]
    chunks = refs[1:9]
    kv_ref, qd_ref, hq_ref, ku_ref, raw_ref, stats_ref = refs[9:15]
    d_ref = refs[15]
    stacks = refs[16:24]
    keep_ref, give_ref = refs[24:26]
    sums, dqt, grad_t, grad = refs[26:30]
    z = place_ref[0]
    sums[...] = jnp.zeros_like(sums)

    def step(i, carry):
        zero = jnp.zeros_like(hq_ref[i])
        query = jnp.concatenate([hq_ref[i], zero], axis=0)
        d_head = jnp.concatenate([zero, d_ref[place_of(z, i)]], axis=0)
        rows = qd_ref[i].astype(jnp.float32)
        left = lax.broadcasted_iota(jnp.int32, rows.shape, 1) < HEAD_DIM
        rhs = jnp.concatenate([jnp.where(left, 0.0, rows), jnp.where(left, rows, 0.0)], axis=0)
        rhs = rhs.astype(jnp.bfloat16)
        inverse = stats_ref[i, 0:1]
        row_dot = stats_ref[i, 1:2]
        d_qunit = jnp.zeros((HEAD_DIM, CHUNK), jnp.float32)
        for j in range(N_SEQ):
            prob = jnp.exp(matmul(kv_ref[j], query)) * inverse
            d_scores = (prob * (matmul(kv_ref[j], d_head) - row_dot)).astype(jnp.bfloat16)
            d_qunit += matmul(ku_ref[j], d_scores)
            both = jnp.concatenate([prob.astype(jnp.bfloat16), d_scores], axis=1)
            sums[j] += matmul(both, rhs)
        dqt[i] = d_qunit * SCALE
        return carry

    lax.fori_loop(0, N_SEQ, step, 0)
    for j in range(N_SEQ):
        turned = sums[j].T
        pieces = []
        for t, d_unit in enumerate((dqt[j], turned[:HEAD_DIM])):
            wide = raw_ref[j, t * HEAD_DIM : (t + 1) * HEAD_DIM].astype(jnp.float32)
            factor = unit_factor(wide, 0)
            mean = jnp.mean(d_unit * wide, axis=0, keepdims=True)
            pieces.append(factor * d_unit - factor * factor * factor * wide * mean)
        stacked = jnp.concatenate(pieces + [turned[HEAD_DIM:]], axis=0).astype(jnp.bfloat16)
        stacks[j][...] = stacked
        term = matmul(stacked, chunks[j][...])
        if j == 0:
            grad_t[: 3 * HEAD_DIM] = term
        else:
            grad_t[: 3 * HEAD_DIM] += term
    grad_t[3 * HEAD_DIM :] = jnp.zeros((HEAD_DIM, grad_t.shape[1]), jnp.float32)
    grad[...] = grad_t[...].T
    split_rows(place_ref[1], grad, keep_ref, give_ref)


def result_kernel(*refs):
    place_ref = refs[0]
    chunks = refs[1:9]
    heads_ref, w_ref, grad_ref, x_ref, act_ref, cut_ref = refs[9:15]
    out_ref, keep_ref, give_ref, grad_t, grad_msg, grad_out = refs[15:]
    z = place_ref[0]
    every = jnp.concatenate([heads_ref[h] for h in range(N_SEQ)], axis=0)
    grad_out[...] = matmul(every, grad_ref[...])
    for j in range(N_SEQ):
        columns = cut_ref[place_of(z, j)].astype(jnp.float32).T.astype(jnp.bfloat16)
        term = matmul(columns, chunks[j][...])
        if j == 0:
            grad_t[...] = term
        else:
            grad_t[...] += term
    grad_msg[...] = grad_t[...].T
    split_rows(place_ref[1], grad_msg, keep_ref, give_ref)
    split_rows(place_ref[1], grad_out, keep_ref, give_ref, grad_msg.shape[0] // (2 * N_XY))
    attn = contract_rows(every, w_ref[...])
    out_ref[...] = (x_ref[...].astype(jnp.float32) + attn + act_ref[...]).astype(jnp.bfloat16)


def pair_kernel(keep_a, got_a, keep_b, got_b, out_ref):
    cut = keep_a.shape[1]
    for i in range(N_XY):
        out_ref[i, :cut] = (keep_a[i].astype(jnp.float32) + got_a[i].astype(jnp.float32)).astype(jnp.bfloat16)
        out_ref[i, cut:] = (keep_b[i].astype(jnp.float32) + got_b[i].astype(jnp.float32)).astype(jnp.bfloat16)


def share_kernel(shares_ref, out_ref):
    total = jnp.zeros(shares_ref.shape[1:], jnp.float32)
    for i in range(N_XY):
        total += shares_ref[i].astype(jnp.float32)
    for h in range(N_SEQ):
        out_ref[h] = total.astype(jnp.bfloat16)


def finish_kernel(every_ref, w_ref, m_ref, gain_ref, qkv_ref, out_ref, msg_ref, gain_out_ref):
    rows = msg_ref.shape[0]
    hd = N_SEQ * HEAD_DIM
    nodes = N_SEQ * CHUNK
    gain_sum = jnp.zeros((rows, BLOCK), jnp.float32)
    low = slice(0, HEAD_DIM)
    high = slice(HEAD_DIM, 2 * HEAD_DIM)
    for t, (band, half) in enumerate(((0, low), (0, high), (1, low))):
        for p in range(N_SEQ // 2):
            pieces = [every_ref[h, band * rows : (band + 1) * rows, half] for h in (2 * p, 2 * p + 1)]
            block = jnp.concatenate(pieces, axis=1).astype(jnp.float32) * (1.0 / nodes)
            columns = slice(t * hd + p * BLOCK, t * hd + (p + 1) * BLOCK)
            qkv_ref[:, columns] = block
            gain_sum += block * w_ref[:, columns].astype(jnp.float32)
    total = jnp.zeros((every_ref.shape[1] - 3 * rows, BLOCK), jnp.float32)
    for h in range(N_SEQ):
        columns = slice(h * BLOCK, (h + 1) * BLOCK)
        block = every_ref[h, 2 * rows : 3 * rows].astype(jnp.float32) * (1.0 / nodes)
        msg_ref[:, columns] = block
        gain_sum += block * m_ref[:, columns].astype(jnp.float32)
        total += every_ref[h, 3 * rows :].astype(jnp.float32)
    half_rows = out_ref.shape[0]
    for t in range(N_SEQ):
        out_ref[:, t * BLOCK : (t + 1) * BLOCK] = total[t * half_rows : (t + 1) * half_rows] * (1.0 / nodes)
    gain_out_ref[...] = jnp.sum(gain_sum, axis=1, keepdims=True) / gain_ref[...]


def input_grad_kernel(*refs):
    place_ref = refs[0]
    stacks = refs[1:9]
    w_ref, d_norm_ref, x_ref, grad_ref, gain_ref = refs[9:14]
    out_ref, gathered = refs[14:]
    z = place_ref[0]
    hd = N_SEQ * HEAD_DIM
    for j in range(N_SEQ):
        head = lax.rem(z + j, N_SEQ)
        for t in range(3):
            gathered[pl.ds(t * hd + head * HEAD_DIM, HEAD_DIM), :] = stacks[j][
                t * HEAD_DIM : (t + 1) * HEAD_DIM
            ]
    d_norm = matmul(w_ref[...], gathered[...]).T + d_norm_ref[...]
    wide = x_ref[...].astype(jnp.float32)
    inv_rms = unit_factor(wide, -1)
    x_hat = wide * inv_rms
    scaled = d_norm * gain_ref[...]
    d_feat = inv_rms * (scaled - x_hat * jnp.mean(scaled * x_hat, axis=-1, keepdims=True))
    out_ref[...] = (grad_ref[...].astype(jnp.float32) + d_feat).astype(jnp.bfloat16)


def after(value, *others):
    return lax.optimization_barrier((value,) + others)[0]


def exchange(array, axis):
    return lax.all_to_all(array, axis, split_axis=0, concat_axis=0, tiled=True)


def shift(array, distance):
    return lax.ppermute(array, "z", [(i, (i + distance) % N_SEQ) for i in range(N_SEQ)])


def up(array):
    return shift(array, 1)


def down(array):
    return shift(array, -1)


def sum_over_cores(keep, give):
    got = lax.ppermute(give, "c", [(0, 1), (1, 0)])
    return (keep.astype(jnp.float32) + got.astype(jnp.float32)).astype(jnp.bfloat16)


def sum_over_chips(pair):
    return jnp.sum(exchange(pair, ("x", "y")).astype(jnp.float32), axis=0)


def on_device(
    features, out_grad, norm_gain, w_qkv, w_out, w_msg, block_ids, block_counts, edge_tiles
):
    node_rows, width = features.shape
    hd = w_out.shape[0]
    nodes = N_SEQ * node_rows
    bf16, f32 = jnp.bfloat16, jnp.float32
    z = lax.axis_index("z")
    core = lax.axis_index("c")
    place = jnp.stack([z, core]).astype(jnp.int32)
    gain = norm_gain.reshape(1, width)
    wide_shape = ((node_rows, width), f32)
    low_shape = ((node_rows, width), bf16)

    (normed,) = call(normalize_kernel, "normalize", (low_shape,), (), (features, gain), moved=1 << 20)

    a1, b1 = up(normed), down(normed)
    (d_out,) = call(
        d_out_kernel, "d_out", (((N_SEQ, HEAD_DIM, node_rows), bf16),), (), (out_grad, w_out),
        flops=2 * node_rows * width * hd, moved=2 << 20,
    )
    d_heads = exchange(d_out, "z")
    w_head = pick_head(place, w_qkv)
    a1, b1, d_heads = lax.optimization_barrier((a1, b1, d_heads))
    a2, b2 = up(a1), down(b1)

    act, to_low, mid, to_high = call(
        message_kernel, "messages", (wide_shape, low_shape, wide_shape, low_shape),
        (place, block_ids, block_counts), (a1, normed, b1, w_msg, edge_tiles, out_grad),
        [pltpu.VMEM((6, BLOCK, width), bf16), pltpu.VMEM((6, BLOCK, width), f32)],
        flops=8 * node_rows * width * width, exps=node_rows * width, moved=8 << 20,
    )
    a2, b2, w_head, to_low, to_high = lax.optimization_barrier((a2, b2, w_head, to_low, to_high))
    a3, b3 = up(a2), down(b2)
    above, below = down(to_low), up(to_high)
    a3, b3, above, below = lax.optimization_barrier((a3, b3, above, below))
    half = node_rows // 2
    c4 = (up(a3[:half]), down(b3[half:]))
    d_msg_cut, d_norm = call(
        message_grad_kernel, "message_grad", (((N_SEQ, node_rows, width // N_SEQ), bf16), wide_shape),
        (), (mid, above, below, w_msg), flops=2 * node_rows * width * width, moved=8 << 20,
    )
    *c4, d_msg_cut, d_norm = lax.optimization_barrier((*c4, d_msg_cut, d_norm))
    c4 = jnp.concatenate(c4, axis=0)
    chunks = (normed, a1, a2, a3, c4, b3, b2, b1)
    d_msg_cut = exchange(d_msg_cut, "z")

    lanes_in = ((N_SEQ, CHUNK, 2 * HEAD_DIM), bf16)
    turned = ((N_SEQ, HEAD_DIM, CHUNK), bf16)
    out_t, *saved = call(
        forward_kernel, "attend_forward",
        (turned, lanes_in, lanes_in, turned, turned,
         ((N_SEQ, 2 * HEAD_DIM, CHUNK), bf16), ((N_SEQ, 8, CHUNK), f32)),
        (place,), chunks + (w_head, d_heads),
        [pltpu.VMEM((N_SEQ, HEAD_DIM + ONES, CHUNK), bf16)],
        flops=12 * nodes * nodes * HEAD_DIM, exps=nodes * nodes, moved=8 << 20,
    )
    out_t, d_msg_cut = lax.optimization_barrier((out_t, d_msg_cut))
    heads = exchange(out_t, "z")

    rows_here = width // (2 * N_XY)
    rows_out = hd // (2 * N_XY)
    part_head = ((N_XY, 2 * rows_here, BLOCK), bf16)
    *stacks, keep, give = call(
        backward_kernel, "attend_backward",
        (((3 * HEAD_DIM, CHUNK), bf16),) * N_SEQ + (part_head, part_head),
        (place,), chunks + (*saved, d_heads),
        [
            pltpu.VMEM((N_SEQ, CHUNK, 2 * HEAD_DIM), f32),
            pltpu.VMEM((N_SEQ, HEAD_DIM, CHUNK), f32),
            pltpu.VMEM((4 * HEAD_DIM, width), f32),
            pltpu.VMEM((width, 4 * HEAD_DIM), f32),
        ],
        flops=24 * nodes * nodes * HEAD_DIM, exps=nodes * nodes, moved=8 << 20,
    )
    got = lax.ppermute(give, "c", [(0, 1), (1, 0)])

    part_out = ((N_XY, rows_here + rows_out * width // BLOCK, BLOCK), bf16)
    block_result_array, keep_out, give_out = call(
        result_kernel, "result", (low_shape, part_out, part_out), (place,),
        chunks + (after(heads, keep), w_out, out_grad, features, act, d_msg_cut),
        [pltpu.VMEM((BLOCK, width), f32), pltpu.VMEM((width, BLOCK), f32), pltpu.VMEM((hd, width), f32)],
        flops=6 * node_rows * width * width, moved=10 << 20,
    )
    got_out = lax.ppermute(give_out, "c", [(0, 1), (1, 0)])
    all_rows = part_head[0][1] + part_out[0][1]
    (pair,) = call(
        pair_kernel, "pair_sum", (((N_XY, all_rows, BLOCK), bf16),), (), (keep, got, keep_out, got_out),
        moved=3 << 20,
    )
    pair, *stacks = lax.optimization_barrier((pair, *stacks))
    shares = exchange(pair, ("x", "y"))
    stacks = [stacks[0]] + [shift(stacks[j], -j) for j in range(1, N_SEQ)]
    (mine,) = call(
        share_kernel, "share_sum", (((N_SEQ, all_rows, BLOCK), bf16),), (), (shares,), moved=2 << 20,
    )
    every = exchange(mine, "z")

    (grad_input,) = call(
        input_grad_kernel, "input_grad", (low_shape,), (place,),
        (*stacks, w_qkv, d_norm, features, out_grad, gain),
        [pltpu.VMEM((3 * hd, node_rows), bf16)],
        flops=6 * node_rows * width * hd, moved=8 << 20,
    )

    first = ((lax.axis_index("x") * 4 + lax.axis_index("y")) * 2 + core) * rows_here
    w_rows = lax.dynamic_slice_in_dim(w_qkv, first, rows_here, 0)
    m_rows = lax.dynamic_slice_in_dim(w_msg, first, rows_here, 0)
    gain_rows = lax.dynamic_slice_in_dim(norm_gain, first, rows_here, 0).reshape(rows_here, 1)
    grad_qkv, grad_out, grad_msg, grad_gain = call(
        finish_kernel, "finish",
        (((rows_here, 3 * hd), f32), ((rows_out, width), f32), ((rows_here, width), f32), ((rows_here, 1), f32)),
        (), (every, w_rows, m_rows, gain_rows), moved=2 << 20,
    )
    return block_result_array, grad_input, grad_gain.reshape(rows_here), grad_qkv, grad_out, grad_msg


def solution(mesh):
    fine = Mesh(mesh.devices.reshape(4, 4, 2, N_SEQ), ("x", "y", "c", "z"))
    dp = ("x", "y", "c")
    rows = ("x", "y", "c", "z")
    return jax.shard_map(
        on_device,
        mesh=fine,
        in_specs=(
            P(rows, None),
            P(rows, None),
            P(),
            P(),
            P(),
            P(),
            P(rows, None),
            P(rows),
            P(rows, None, None, None),
        ),
        out_specs=(
            P(rows, None),
            P(rows, None),
            P(dp),
            P(dp, None),
            P(dp, None),
            P(dp, None),
        ),
        check_vma=False,
    )
```

```python
import jax
import jax.numpy as jnp
from jax import lax
from jax.experimental import pallas as pl
from jax.experimental.pallas import tpu as pltpu
from jax.sharding import Mesh
from jax.sharding import PartitionSpec as P

HEAD_DIM = 64
BLOCK = 128
SLOTS = 4
N_SEQ = 8
N_XY = 16
CHUNK = 256
ONES = 16

exponent_divisor = 32.0
epsilon = 1e-06
SCALE = exponent_divisor / HEAD_DIM


def matmul(left, right):
    return jnp.dot(left, right, preferred_element_type=jnp.float32)


def contract_rows(left, right):
    return lax.dot_general(
        left, right, (((0,), (0,)), ((), ())), preferred_element_type=jnp.float32
    )


def contract_cols(left, right):
    return lax.dot_general(
        left, right, (((1,), (1,)), ((), ())), preferred_element_type=jnp.float32
    )


def unit_factor(wide, axis):
    return lax.rsqrt(jnp.mean(wide * wide, axis=axis, keepdims=True) + epsilon)


def call(kernel, name, out_shape, scalars, arrays, scratch=(), flops=0, exps=0, moved=0):
    specs = [pl.BlockSpec(memory_space=pltpu.SMEM)] * len(scalars)
    specs += [pl.BlockSpec(memory_space=pltpu.VMEM)] * len(arrays)
    return pl.pallas_call(
        kernel,
        out_shape=tuple(jax.ShapeDtypeStruct(s, t) for s, t in out_shape),
        in_specs=specs,
        out_specs=tuple(pl.BlockSpec(memory_space=pltpu.VMEM) for _ in out_shape),
        scratch_shapes=list(scratch),
        compiler_params=pltpu.CompilerParams(vmem_limit_bytes=24 * 1024 * 1024),
        cost_estimate=pl.CostEstimate(flops=flops, bytes_accessed=moved, transcendentals=exps),
        name=name,
    )(*scalars, *arrays)


def normalize_kernel(x_ref, gain_ref, out_ref):
    wide = x_ref[...].astype(jnp.float32)
    out_ref[...] = (wide * unit_factor(wide, -1) * gain_ref[...]).astype(jnp.bfloat16)


def d_out_kernel(grad_ref, w_ref, out_ref):
    turned = contract_cols(w_ref[...], grad_ref[...]).astype(jnp.bfloat16)
    for h in range(N_SEQ):
        out_ref[h] = turned[h * HEAD_DIM : (h + 1) * HEAD_DIM]


def pick_kernel(place_ref, q_ref, k_ref, v_ref, out_ref, turned):
    odd = lax.rem(place_ref[0], 2)
    for t, ref in enumerate((q_ref, k_ref, v_ref)):
        turned[...] = ref[...].astype(jnp.float32).T
        out_ref[t * HEAD_DIM : (t + 1) * HEAD_DIM] = turned[
            pl.ds(odd * HEAD_DIM, HEAD_DIM), :
        ].astype(jnp.bfloat16)


def pick_head(place, w_qkv):
    width, columns = w_qkv.shape
    step = columns // 3 // (2 * HEAD_DIM)

    def block(t):
        return pl.BlockSpec((width, 2 * HEAD_DIM), lambda i, place: (0, t * step + place[0] // 2))

    return pl.pallas_call(
        pick_kernel,
        grid_spec=pltpu.PrefetchScalarGridSpec(
            num_scalar_prefetch=1,
            grid=(1,),
            in_specs=[block(0), block(1), block(2)],
            out_specs=pl.BlockSpec((3 * HEAD_DIM, width), lambda i, place: (0, 0)),
            scratch_shapes=[pltpu.VMEM((2 * HEAD_DIM, width), jnp.float32)],
        ),
        out_shape=jax.ShapeDtypeStruct((3 * HEAD_DIM, width), jnp.bfloat16),
        cost_estimate=pl.CostEstimate(flops=0, bytes_accessed=4 << 20, transcendentals=0),
        name="pick_head",
    )(place, w_qkv, w_qkv, w_qkv)


def message_kernel(*refs):
    place_ref, ids_ref, counts_ref, low_ref, own_ref, high_ref, w_ref, tiles_ref, grad_ref = refs[:9]
    act_ref, to_low_ref, mid_ref, to_high_ref, msg, landed = refs[9:]
    z = place_ref[0]
    for t, ref in enumerate((low_ref, own_ref, high_ref)):
        rows = matmul(ref[...], w_ref[...]).astype(jnp.bfloat16)
        msg[2 * t] = rows[:BLOCK]
        msg[2 * t + 1] = rows[BLOCK:]
    landed[...] = jnp.zeros_like(landed)
    for b in range(2):
        spots = []
        live = []
        for s in range(SLOTS):
            spots.append(jnp.clip(ids_ref[b, s] - 2 * (z - 1), 0, 5))
            mask = jnp.where(s < counts_ref[b], 1.0, 0.0)
            live.append(tiles_ref[b, s].astype(jnp.float32) * mask)
        source = jnp.concatenate([msg[spot] for spot in spots], axis=0)
        agg = matmul(jnp.concatenate(live, axis=1).astype(jnp.bfloat16), source)
        sigma = 1.0 / (1.0 + jnp.exp(-agg))
        rows = slice(b * BLOCK, (b + 1) * BLOCK)
        act_ref[rows] = agg * sigma
        d_agg = grad_ref[rows].astype(jnp.float32) * sigma * (1.0 + agg * (1.0 - sigma))
        d_agg = d_agg.astype(jnp.bfloat16)
        for s in range(SLOTS):
            landed[spots[s]] += matmul(live[s].T.astype(jnp.bfloat16), d_agg)
    for b in range(2):
        rows = slice(b * BLOCK, (b + 1) * BLOCK)
        to_low_ref[rows] = landed[b].astype(jnp.bfloat16)
        mid_ref[rows] = landed[2 + b]
        to_high_ref[rows] = landed[4 + b].astype(jnp.bfloat16)


def split_rows(core, source, keep_ref, give_ref, offset=0):
    rows = source.shape[0] // (2 * N_XY)
    for i in range(N_XY):
        for t in range(source.shape[1] // BLOCK):
            spot = slice(offset + t * rows, offset + (t + 1) * rows)
            columns = slice(t * BLOCK, (t + 1) * BLOCK)
            keep_ref[i, spot] = source[pl.ds((2 * i + core) * rows, rows), columns].astype(jnp.bfloat16)
            give_ref[i, spot] = source[pl.ds((2 * i + 1 - core) * rows, rows), columns].astype(
                jnp.bfloat16
            )


def message_grad_kernel(*refs):
    mid_ref, above_ref, below_ref, w_ref = refs[:4]
    cut_ref, d_norm_ref = refs[4:]
    total = mid_ref[...] + above_ref[...].astype(jnp.float32) + below_ref[...].astype(jnp.float32)
    d_msg = total.astype(jnp.bfloat16)
    for t in range(N_SEQ):
        columns = d_msg[:, t * BLOCK : (t + 1) * BLOCK]
        cut_ref[t] = jnp.concatenate([columns[:BLOCK], columns[BLOCK:]], axis=1)
    d_norm_ref[...] = contract_cols(d_msg, w_ref[...])


def place_of(z, j):
    return lax.rem(z - j + N_SEQ, N_SEQ)


def read_chunks(refs):
    def whole(ref):
        return lambda: ref[...]

    def halves():
        return jnp.concatenate([refs[4][...], refs[5][...]], axis=0)

    return [whole(ref) for ref in refs[:4]] + [halves] + [whole(ref) for ref in refs[6:9]]


def forward_kernel(*refs):
    z = refs[0][0]
    chunks = read_chunks(refs[1:10])
    w_ref, cut_ref = refs[10:12]
    send_ref, kv_ref, hq_ref, ku_ref, raw_ref, out_ref, stats_ref = refs[12:19]
    v_ext = refs[19]
    for h in range(N_SEQ):
        send_ref[h, HEAD_DIM:] = cut_ref[h]
    for j in range(N_SEQ):
        proj = contract_cols(w_ref[...], chunks[j]()).astype(jnp.bfloat16)
        raw_ref[j] = proj[: 2 * HEAD_DIM]
        query = proj[:HEAD_DIM].astype(jnp.float32)
        keyrow = proj[HEAD_DIM : 2 * HEAD_DIM].astype(jnp.float32)
        val = proj[2 * HEAD_DIM :]
        q_unit = (query * unit_factor(query, 0)).astype(jnp.bfloat16).astype(jnp.float32) * SCALE
        k_unit = keyrow * unit_factor(keyrow, 0)
        hq_ref[j] = q_unit.astype(jnp.bfloat16)
        ku_ref[j] = k_unit.astype(jnp.bfloat16)
        v_ext[j, :HEAD_DIM] = val
        v_ext[j, HEAD_DIM:] = jnp.ones((ONES, CHUNK), jnp.bfloat16)
        kv_ref[j] = jnp.concatenate([k_unit, val.astype(jnp.float32)], axis=0).T.astype(jnp.bfloat16)

    def step(i, carry):
        query = jnp.concatenate([hq_ref[i], jnp.zeros_like(hq_ref[i])], axis=0)
        out = jnp.zeros((HEAD_DIM + ONES, CHUNK), jnp.float32)
        for j in range(N_SEQ):
            exps = jnp.exp(matmul(kv_ref[j], query)).astype(jnp.bfloat16)
            out += matmul(v_ext[j], exps)
        inverse = 1.0 / out[HEAD_DIM : HEAD_DIM + 1]
        stats_ref[i, 0:1] = inverse
        head_out = (out[:HEAD_DIM] * inverse).astype(jnp.bfloat16)
        out_ref[i] = head_out
        send_ref[place_of(z, i), :HEAD_DIM] = head_out
        return carry

    lax.fori_loop(0, N_SEQ, step, 0)


def backward_kernel(*refs):
    place_ref = refs[0]
    chunks = read_chunks(refs[1:10])
    kv_ref, hq_ref, ku_ref, raw_ref, head_ref, stats_ref, d_ref = refs[10:17]
    stacks = refs[17:25]
    keep_ref, give_ref = refs[25:27]
    sums, dqt, grad_t, grad = refs[27:31]
    z = place_ref[0]
    sums[...] = jnp.zeros_like(sums)

    def step(i, carry):
        zero = jnp.zeros_like(hq_ref[i])
        query = jnp.concatenate([hq_ref[i], zero], axis=0)
        d_out = d_ref[place_of(z, i)]
        d_wide = d_out.astype(jnp.float32)
        d_head = jnp.concatenate([zero, d_out], axis=0)
        rows = jnp.concatenate([hq_ref[i].astype(jnp.float32), d_wide], axis=0).T
        left = lax.broadcasted_iota(jnp.int32, rows.shape, 1) < HEAD_DIM
        rhs = jnp.concatenate([jnp.where(left, 0.0, rows), jnp.where(left, rows, 0.0)], axis=0)
        rhs = rhs.astype(jnp.bfloat16)
        inverse = stats_ref[i, 0:1]
        row_dot = jnp.sum(head_ref[i].astype(jnp.float32) * d_wide, axis=0, keepdims=True)
        d_qunit = jnp.zeros((HEAD_DIM, CHUNK), jnp.float32)
        for j in range(N_SEQ):
            prob = jnp.exp(matmul(kv_ref[j], query)) * inverse
            d_scores = (prob * (matmul(kv_ref[j], d_head) - row_dot)).astype(jnp.bfloat16)
            d_qunit += matmul(ku_ref[j], d_scores)
            both = jnp.concatenate([prob.astype(jnp.bfloat16), d_scores], axis=1)
            sums[j] += matmul(both, rhs)
        dqt[i] = d_qunit * SCALE
        return carry

    lax.fori_loop(0, N_SEQ, step, 0)
    for j in range(N_SEQ):
        turned = sums[j].T
        pieces = []
        for t, d_unit in enumerate((dqt[j], turned[:HEAD_DIM])):
            wide = raw_ref[j, t * HEAD_DIM : (t + 1) * HEAD_DIM].astype(jnp.float32)
            factor = unit_factor(wide, 0)
            mean = jnp.mean(d_unit * wide, axis=0, keepdims=True)
            pieces.append(factor * d_unit - factor * factor * factor * wide * mean)
        stacked = jnp.concatenate(pieces + [turned[HEAD_DIM:]], axis=0).astype(jnp.bfloat16)
        stacks[j][...] = stacked
        term = matmul(stacked, chunks[j]())
        if j == 0:
            grad_t[: 3 * HEAD_DIM] = term
        else:
            grad_t[: 3 * HEAD_DIM] += term
    grad_t[3 * HEAD_DIM :] = jnp.zeros((HEAD_DIM, grad_t.shape[1]), jnp.float32)
    grad[...] = grad_t[...].T
    split_rows(place_ref[1], grad, keep_ref, give_ref)


def result_kernel(*refs):
    place_ref = refs[0]
    chunks = read_chunks(refs[1:10])
    home_ref, w_ref, grad_ref, x_ref, act_ref = refs[10:15]
    out_ref, keep_ref, give_ref, grad_t, grad_msg, grad_out = refs[15:]
    z = place_ref[0]
    every = jnp.concatenate([home_ref[h, :HEAD_DIM] for h in range(N_SEQ)], axis=0)
    grad_out[...] = matmul(every, grad_ref[...])
    for j in range(N_SEQ):
        folded = home_ref[place_of(z, j), HEAD_DIM:].astype(jnp.float32)
        columns = jnp.concatenate([folded[:, :BLOCK].T, folded[:, BLOCK:].T], axis=1)
        term = matmul(columns.astype(jnp.bfloat16), chunks[j]())
        if j == 0:
            grad_t[...] = term
        else:
            grad_t[...] += term
    grad_msg[...] = grad_t[...].T
    split_rows(place_ref[1], grad_msg, keep_ref, give_ref)
    split_rows(place_ref[1], grad_out, keep_ref, give_ref, grad_msg.shape[0] // (2 * N_XY))
    attn = contract_rows(every, w_ref[...])
    out_ref[...] = (x_ref[...].astype(jnp.float32) + attn + act_ref[...]).astype(jnp.bfloat16)


def pair_kernel(keep_a, got_a, keep_b, got_b, out_ref):
    cut = keep_a.shape[1]
    for i in range(N_XY):
        out_ref[i, :cut] = (keep_a[i].astype(jnp.float32) + got_a[i].astype(jnp.float32)).astype(jnp.bfloat16)
        out_ref[i, cut:] = (keep_b[i].astype(jnp.float32) + got_b[i].astype(jnp.float32)).astype(jnp.bfloat16)


def share_kernel(shares_ref, out_ref):
    total = jnp.zeros(shares_ref.shape[1:], jnp.float32)
    for i in range(N_XY):
        total += shares_ref[i].astype(jnp.float32)
    for h in range(N_SEQ):
        out_ref[h] = total.astype(jnp.bfloat16)


def finish_kernel(every_ref, w_ref, m_ref, gain_ref, qkv_ref, out_ref, msg_ref, gain_out_ref):
    rows = msg_ref.shape[0]
    hd = N_SEQ * HEAD_DIM
    nodes = N_SEQ * CHUNK
    gain_sum = jnp.zeros((rows, BLOCK), jnp.float32)
    low = slice(0, HEAD_DIM)
    high = slice(HEAD_DIM, 2 * HEAD_DIM)
    for t, (band, half) in enumerate(((0, low), (0, high), (1, low))):
        for p in range(N_SEQ // 2):
            pieces = [every_ref[h, band * rows : (band + 1) * rows, half] for h in (2 * p, 2 * p + 1)]
            block = jnp.concatenate(pieces, axis=1).astype(jnp.float32) * (1.0 / nodes)
            columns = slice(t * hd + p * BLOCK, t * hd + (p + 1) * BLOCK)
            qkv_ref[:, columns] = block
            gain_sum += block * w_ref[:, columns].astype(jnp.float32)
    total = jnp.zeros((every_ref.shape[1] - 3 * rows, BLOCK), jnp.float32)
    for h in range(N_SEQ):
        columns = slice(h * BLOCK, (h + 1) * BLOCK)
        block = every_ref[h, 2 * rows : 3 * rows].astype(jnp.float32) * (1.0 / nodes)
        msg_ref[:, columns] = block
        gain_sum += block * m_ref[:, columns].astype(jnp.float32)
        total += every_ref[h, 3 * rows :].astype(jnp.float32)
    half_rows = out_ref.shape[0]
    for t in range(N_SEQ):
        out_ref[:, t * BLOCK : (t + 1) * BLOCK] = total[t * half_rows : (t + 1) * half_rows] * (1.0 / nodes)
    gain_out_ref[...] = jnp.sum(gain_sum, axis=1, keepdims=True) / gain_ref[...]


def input_grad_kernel(*refs):
    place_ref = refs[0]
    stacks = refs[1:9]
    w_ref, d_norm_ref, x_ref, grad_ref, gain_ref = refs[9:14]
    out_ref, gathered = refs[14:]
    z = place_ref[0]
    hd = N_SEQ * HEAD_DIM
    for j in range(N_SEQ):
        head = lax.rem(z + j, N_SEQ)
        for t in range(3):
            gathered[pl.ds(t * hd + head * HEAD_DIM, HEAD_DIM), :] = stacks[j][
                t * HEAD_DIM : (t + 1) * HEAD_DIM
            ]
    d_norm = matmul(w_ref[...], gathered[...]).T + d_norm_ref[...]
    wide = x_ref[...].astype(jnp.float32)
    inv_rms = unit_factor(wide, -1)
    x_hat = wide * inv_rms
    scaled = d_norm * gain_ref[...]
    d_feat = inv_rms * (scaled - x_hat * jnp.mean(scaled * x_hat, axis=-1, keepdims=True))
    out_ref[...] = (grad_ref[...].astype(jnp.float32) + d_feat).astype(jnp.bfloat16)


def after(value, *others):
    return lax.optimization_barrier((value,) + others)[0]


def exchange(array, axis):
    return lax.all_to_all(array, axis, split_axis=0, concat_axis=0, tiled=True)


def shift(array, distance):
    return lax.ppermute(array, "z", [(i, (i + distance) % N_SEQ) for i in range(N_SEQ)])


def up(array):
    return shift(array, 1)


def down(array):
    return shift(array, -1)


def sum_over_cores(keep, give):
    got = lax.ppermute(give, "c", [(0, 1), (1, 0)])
    return (keep.astype(jnp.float32) + got.astype(jnp.float32)).astype(jnp.bfloat16)


def sum_over_chips(pair):
    return jnp.sum(exchange(pair, ("x", "y")).astype(jnp.float32), axis=0)


def on_device(
    features, out_grad, norm_gain, w_qkv, w_out, w_msg, block_ids, block_counts, edge_tiles
):
    node_rows, width = features.shape
    hd = w_out.shape[0]
    nodes = N_SEQ * node_rows
    bf16, f32 = jnp.bfloat16, jnp.float32
    z = lax.axis_index("z")
    core = lax.axis_index("c")
    place = jnp.stack([z, core]).astype(jnp.int32)
    gain = norm_gain.reshape(1, width)
    wide_shape = ((node_rows, width), f32)
    low_shape = ((node_rows, width), bf16)

    (normed,) = call(normalize_kernel, "normalize", (low_shape,), (), (features, gain), moved=1 << 20)

    a1, b1 = up(normed), down(normed)
    (d_out,) = call(
        d_out_kernel, "d_out", (((N_SEQ, HEAD_DIM, node_rows), bf16),), (), (out_grad, w_out),
        flops=2 * node_rows * width * hd, moved=2 << 20,
    )
    w_head = pick_head(place, w_qkv)
    a1, b1, d_out, w_head = lax.optimization_barrier((a1, b1, d_out, w_head))
    a2, b2 = up(a1), down(b1)

    act, to_low, mid, to_high = call(
        message_kernel, "messages", (wide_shape, low_shape, wide_shape, low_shape),
        (place, block_ids, block_counts), (a1, normed, b1, w_msg, edge_tiles, out_grad),
        [pltpu.VMEM((6, BLOCK, width), bf16), pltpu.VMEM((6, BLOCK, width), f32)],
        flops=8 * node_rows * width * width, exps=node_rows * width, moved=8 << 20,
    )
    a2, b2, to_low, to_high = lax.optimization_barrier((a2, b2, to_low, to_high))
    a3, b3 = up(a2), down(b2)
    above, below = down(to_low), up(to_high)
    a3, b3, above, below = lax.optimization_barrier((a3, b3, above, below))
    half = node_rows // 2
    c4 = (up(a3[:half]), down(b3[half:]))
    d_msg_cut, d_norm = call(
        message_grad_kernel, "message_grad", (((N_SEQ, BLOCK, CHUNK), bf16), wide_shape),
        (), (mid, above, below, w_msg), flops=2 * node_rows * width * width, moved=8 << 20,
    )
    *c4, d_msg_cut, d_norm, d_out = lax.optimization_barrier((*c4, d_msg_cut, d_norm, d_out))
    chunks = (normed, a1, a2, a3, *c4, b3, b2, b1)
    d_heads = exchange(d_out, "z")

    lanes_in = ((N_SEQ, CHUNK, 2 * HEAD_DIM), bf16)
    turned = ((N_SEQ, HEAD_DIM, CHUNK), bf16)
    send, *saved = call(
        forward_kernel, "attend_forward",
        (((N_SEQ, HEAD_DIM + BLOCK, CHUNK), bf16), lanes_in, turned, turned,
         ((N_SEQ, 2 * HEAD_DIM, CHUNK), bf16), turned, ((N_SEQ, 8, CHUNK), f32)),
        (place,), chunks + (w_head, d_msg_cut),
        [pltpu.VMEM((N_SEQ, HEAD_DIM + ONES, CHUNK), bf16)],
        flops=12 * nodes * nodes * HEAD_DIM, exps=nodes * nodes, moved=8 << 20,
    )
    send, d_heads = lax.optimization_barrier((send, d_heads))
    home = exchange(send, "z")

    rows_here = width // (2 * N_XY)
    rows_out = hd // (2 * N_XY)
    part_head = ((N_XY, 2 * rows_here, BLOCK), bf16)
    *stacks, keep, give = call(
        backward_kernel, "attend_backward",
        (((3 * HEAD_DIM, CHUNK), bf16),) * N_SEQ + (part_head, part_head),
        (place,), chunks + (*saved, d_heads),
        [
            pltpu.VMEM((N_SEQ, CHUNK, 2 * HEAD_DIM), f32),
            pltpu.VMEM((N_SEQ, HEAD_DIM, CHUNK), f32),
            pltpu.VMEM((4 * HEAD_DIM, width), f32),
            pltpu.VMEM((width, 4 * HEAD_DIM), f32),
        ],
        flops=24 * nodes * nodes * HEAD_DIM, exps=nodes * nodes, moved=8 << 20,
    )
    got = lax.ppermute(give, "c", [(0, 1), (1, 0)])

    part_out = ((N_XY, rows_here + rows_out * width // BLOCK, BLOCK), bf16)
    block_result_array, keep_out, give_out = call(
        result_kernel, "result", (low_shape, part_out, part_out), (place,),
        chunks + (after(home, keep), w_out, out_grad, features, act),
        [pltpu.VMEM((BLOCK, width), f32), pltpu.VMEM((width, BLOCK), f32), pltpu.VMEM((hd, width), f32)],
        flops=6 * node_rows * width * width, moved=10 << 20,
    )
    got_out = lax.ppermute(give_out, "c", [(0, 1), (1, 0)])
    all_rows = part_head[0][1] + part_out[0][1]
    (pair,) = call(
        pair_kernel, "pair_sum", (((N_XY, all_rows, BLOCK), bf16),), (), (keep, got, keep_out, got_out),
        moved=3 << 20,
    )
    pair, *stacks = lax.optimization_barrier((pair, *stacks))
    shares = exchange(pair, ("x", "y"))
    stacks = [stacks[0]] + [shift(stacks[j], -j) for j in range(1, N_SEQ)]
    shares, *stacks = lax.optimization_barrier((shares, *stacks))
    (mine,) = call(
        share_kernel, "share_sum", (((N_SEQ, all_rows, BLOCK), bf16),), (), (shares,), moved=2 << 20,
    )
    every = exchange(mine, "z")

    (grad_input,) = call(
        input_grad_kernel, "input_grad", (low_shape,), (place,),
        (*stacks, w_qkv, d_norm, features, out_grad, gain),
        [pltpu.VMEM((3 * hd, node_rows), bf16)],
        flops=6 * node_rows * width * hd, moved=8 << 20,
    )

    first = ((lax.axis_index("x") * 4 + lax.axis_index("y")) * 2 + core) * rows_here
    w_rows = lax.dynamic_slice_in_dim(w_qkv, first, rows_here, 0)
    m_rows = lax.dynamic_slice_in_dim(w_msg, first, rows_here, 0)
    gain_rows = lax.dynamic_slice_in_dim(norm_gain, first, rows_here, 0).reshape(rows_here, 1)
    grad_qkv, grad_out, grad_msg, grad_gain = call(
        finish_kernel, "finish",
        (((rows_here, 3 * hd), f32), ((rows_out, width), f32), ((rows_here, width), f32), ((rows_here, 1), f32)),
        (), (every, w_rows, m_rows, gain_rows), moved=2 << 20,
    )
    return block_result_array, grad_input, grad_gain.reshape(rows_here), grad_qkv, grad_out, grad_msg


def solution(mesh):
    fine = Mesh(mesh.devices.reshape(4, 4, 2, N_SEQ), ("x", "y", "c", "z"))
    dp = ("x", "y", "c")
    rows = ("x", "y", "c", "z")
    return jax.shard_map(
        on_device,
        mesh=fine,
        in_specs=(
            P(rows, None),
            P(rows, None),
            P(),
            P(),
            P(),
            P(),
            P(rows, None),
            P(rows),
            P(rows, None, None, None),
        ),
        out_specs=(
            P(rows, None),
            P(rows, None),
            P(dp),
            P(dp, None),
            P(dp, None),
            P(dp, None),
        ),
        check_vma=False,
    )
```

```python
import jax
import jax.numpy as jnp
from jax import lax
from jax.experimental import pallas as pl
from jax.experimental.pallas import tpu as pltpu
from jax.sharding import Mesh
from jax.sharding import PartitionSpec as P

HEAD_DIM = 64
BLOCK = 128
SLOTS = 4
N_SEQ = 8
N_XY = 16
CHUNK = 256
ONES = 16

exponent_divisor = 32.0
epsilon = 1e-06
SCALE = exponent_divisor / HEAD_DIM


def matmul(left, right):
    return jnp.dot(left, right, preferred_element_type=jnp.float32)


def contract_rows(left, right):
    return lax.dot_general(
        left, right, (((0,), (0,)), ((), ())), preferred_element_type=jnp.float32
    )


def contract_cols(left, right):
    return lax.dot_general(
        left, right, (((1,), (1,)), ((), ())), preferred_element_type=jnp.float32
    )


def unit_factor(wide, axis):
    return lax.rsqrt(jnp.mean(wide * wide, axis=axis, keepdims=True) + epsilon)


def call(kernel, name, out_shape, scalars, arrays, scratch=(), flops=0, exps=0, moved=0, far=()):
    specs = [pl.BlockSpec(memory_space=pltpu.SMEM)] * len(scalars)
    specs += [pl.BlockSpec(memory_space=pltpu.HBM)] * len(far)
    specs += [pl.BlockSpec(memory_space=pltpu.VMEM)] * len(arrays)
    return pl.pallas_call(
        kernel,
        out_shape=tuple(jax.ShapeDtypeStruct(s, t) for s, t in out_shape),
        in_specs=specs,
        out_specs=tuple(pl.BlockSpec(memory_space=pltpu.VMEM) for _ in out_shape),
        scratch_shapes=list(scratch),
        compiler_params=pltpu.CompilerParams(vmem_limit_bytes=60 * 1024 * 1024),
        cost_estimate=pl.CostEstimate(flops=flops, bytes_accessed=moved, transcendentals=exps),
        name=name,
    )(*scalars, *far, *arrays)


def normalize_kernel(x_ref, gain_ref, out_ref):
    wide = x_ref[...].astype(jnp.float32)
    out_ref[...] = (wide * unit_factor(wide, -1) * gain_ref[...]).astype(jnp.bfloat16)


def d_out_kernel(grad_ref, w_ref, out_ref):
    turned = contract_cols(w_ref[...], grad_ref[...]).astype(jnp.bfloat16)
    for h in range(N_SEQ):
        out_ref[h] = turned[h * HEAD_DIM : (h + 1) * HEAD_DIM]


def pick_kernel(place_ref, q_ref, k_ref, v_ref, out_ref, turned):
    odd = lax.rem(place_ref[0], 2)
    for t, ref in enumerate((q_ref, k_ref, v_ref)):
        turned[...] = ref[...].astype(jnp.float32).T
        out_ref[t * HEAD_DIM : (t + 1) * HEAD_DIM] = turned[
            pl.ds(odd * HEAD_DIM, HEAD_DIM), :
        ].astype(jnp.bfloat16)


def pick_head(place, w_qkv):
    width, columns = w_qkv.shape
    step = columns // 3 // (2 * HEAD_DIM)

    def block(t):
        return pl.BlockSpec((width, 2 * HEAD_DIM), lambda i, place: (0, t * step + place[0] // 2))

    return pl.pallas_call(
        pick_kernel,
        grid_spec=pltpu.PrefetchScalarGridSpec(
            num_scalar_prefetch=1,
            grid=(1,),
            in_specs=[block(0), block(1), block(2)],
            out_specs=pl.BlockSpec((3 * HEAD_DIM, width), lambda i, place: (0, 0)),
            scratch_shapes=[pltpu.VMEM((2 * HEAD_DIM, width), jnp.float32)],
        ),
        out_shape=jax.ShapeDtypeStruct((3 * HEAD_DIM, width), jnp.bfloat16),
        cost_estimate=pl.CostEstimate(flops=0, bytes_accessed=4 << 20, transcendentals=0),
        name="pick_head",
    )(place, w_qkv, w_qkv, w_qkv)


def message_kernel(*refs):
    place_ref, ids_ref, counts_ref, low_ref, own_ref, high_ref, w_ref, tiles_ref, grad_ref = refs[:9]
    act_ref, to_low_ref, mid_ref, to_high_ref, msg, landed = refs[9:]
    z = place_ref[0]
    for t, ref in enumerate((low_ref, own_ref, high_ref)):
        rows = matmul(ref[...], w_ref[...]).astype(jnp.bfloat16)
        msg[2 * t] = rows[:BLOCK]
        msg[2 * t + 1] = rows[BLOCK:]
    landed[...] = jnp.zeros_like(landed)
    for b in range(2):
        spots = []
        live = []
        for s in range(SLOTS):
            spots.append(jnp.clip(ids_ref[b, s] - 2 * (z - 1), 0, 5))
            mask = jnp.where(s < counts_ref[b], 1.0, 0.0)
            live.append(tiles_ref[b, s].astype(jnp.float32) * mask)
        source = jnp.concatenate([msg[spot] for spot in spots], axis=0)
        agg = matmul(jnp.concatenate(live, axis=1).astype(jnp.bfloat16), source)
        sigma = 1.0 / (1.0 + jnp.exp(-agg))
        rows = slice(b * BLOCK, (b + 1) * BLOCK)
        act_ref[rows] = agg * sigma
        d_agg = grad_ref[rows].astype(jnp.float32) * sigma * (1.0 + agg * (1.0 - sigma))
        d_agg = d_agg.astype(jnp.bfloat16)
        for s in range(SLOTS):
            landed[spots[s]] += matmul(live[s].T.astype(jnp.bfloat16), d_agg)
    for b in range(2):
        rows = slice(b * BLOCK, (b + 1) * BLOCK)
        to_low_ref[rows] = landed[b].astype(jnp.bfloat16)
        mid_ref[rows] = landed[2 + b]
        to_high_ref[rows] = landed[4 + b].astype(jnp.bfloat16)


def split_rows(core, source, keep_ref, give_ref, offset=0):
    rows = source.shape[0] // (2 * N_XY)
    for i in range(N_XY):
        for t in range(source.shape[1] // BLOCK):
            spot = slice(offset + t * rows, offset + (t + 1) * rows)
            columns = slice(t * BLOCK, (t + 1) * BLOCK)
            keep_ref[i, spot] = source[pl.ds((2 * i + core) * rows, rows), columns].astype(jnp.bfloat16)
            give_ref[i, spot] = source[pl.ds((2 * i + 1 - core) * rows, rows), columns].astype(
                jnp.bfloat16
            )


def message_grad_kernel(*refs):
    mid_ref, above_ref, below_ref, w_ref = refs[:4]
    cut_ref, d_norm_ref = refs[4:]
    total = mid_ref[...] + above_ref[...].astype(jnp.float32) + below_ref[...].astype(jnp.float32)
    d_msg = total.astype(jnp.bfloat16)
    for t in range(N_SEQ):
        columns = d_msg[:, t * BLOCK : (t + 1) * BLOCK]
        cut_ref[t] = jnp.concatenate([columns[:BLOCK], columns[BLOCK:]], axis=1)
    d_norm_ref[...] = contract_cols(d_msg, w_ref[...])


def place_of(z, j):
    return lax.rem(z - j + N_SEQ, N_SEQ)


def fetch_chunks(refs, held, sems):
    half = CHUNK // 2
    targets = [held.at[j] for j in range(4)]
    targets += [held.at[4, pl.ds(0, half)], held.at[4, pl.ds(half, half)]]
    targets += [held.at[j] for j in range(5, N_SEQ)]
    copies = [pltpu.make_async_copy(ref, to, sems.at[i]) for i, (ref, to) in enumerate(zip(refs, targets))]
    for copy in copies:
        copy.start()

    def wait(j):
        for copy in copies[j + (j > 4) : j + 1 + (j >= 4)]:
            copy.wait()

    return wait


def forward_kernel(*refs):
    z = refs[0][0]
    cut_ref, w_ref = refs[10:12]
    send_ref, kv_ref, hq_ref, ku_ref, raw_ref, out_ref, stats_ref = refs[12:19]
    v_ext, held, sems = refs[19:22]
    wait = fetch_chunks(refs[1:10], held, sems)
    pass_on = pltpu.make_async_copy(cut_ref, send_ref.at[:, pl.ds(HEAD_DIM, BLOCK)], sems.at[9])
    pass_on.start()
    for j in range(N_SEQ):
        wait(j)
        proj = contract_cols(w_ref[...], held[j]).astype(jnp.bfloat16)
        raw_ref[j] = proj[: 2 * HEAD_DIM]
        query = proj[:HEAD_DIM].astype(jnp.float32)
        keyrow = proj[HEAD_DIM : 2 * HEAD_DIM].astype(jnp.float32)
        val = proj[2 * HEAD_DIM :]
        q_unit = (query * unit_factor(query, 0)).astype(jnp.bfloat16).astype(jnp.float32) * SCALE
        k_unit = keyrow * unit_factor(keyrow, 0)
        hq_ref[j] = q_unit.astype(jnp.bfloat16)
        ku_ref[j] = k_unit.astype(jnp.bfloat16)
        v_ext[j, :HEAD_DIM] = val
        v_ext[j, HEAD_DIM:] = jnp.ones((ONES, CHUNK), jnp.bfloat16)
        kv_ref[j] = jnp.concatenate([k_unit, val.astype(jnp.float32)], axis=0).T.astype(jnp.bfloat16)

    def step(i, carry):
        query = jnp.concatenate([hq_ref[i], jnp.zeros_like(hq_ref[i])], axis=0)
        keys = kv_ref[...].reshape(N_SEQ * CHUNK, 2 * HEAD_DIM)
        exps = jnp.exp(matmul(keys, query)).astype(jnp.bfloat16)
        out = matmul(jnp.concatenate([v_ext[j] for j in range(N_SEQ)], axis=1), exps)
        inverse = 1.0 / out[HEAD_DIM : HEAD_DIM + 1]
        stats_ref[i, 0:1] = inverse
        head_out = (out[:HEAD_DIM] * inverse).astype(jnp.bfloat16)
        out_ref[i] = head_out
        send_ref[place_of(z, i), :HEAD_DIM] = head_out
        return carry

    lax.fori_loop(0, N_SEQ, step, 0)
    pass_on.wait()


def backward_kernel(*refs):
    place_ref = refs[0]
    kv_ref, hq_ref, ku_ref, raw_ref, head_ref, stats_ref, d_ref = refs[10:17]
    stacks = refs[17:25]
    keep_ref, give_ref = refs[25:27]
    sums, dqt, grad_t, grad, held, sems = refs[27:33]
    wait = fetch_chunks(refs[1:10], held, sems)
    z = place_ref[0]
    sums[...] = jnp.zeros_like(sums)

    def step(i, carry):
        zero = jnp.zeros_like(hq_ref[i])
        query = jnp.concatenate([hq_ref[i], zero], axis=0)
        d_out = d_ref[place_of(z, i)]
        d_wide = d_out.astype(jnp.float32)
        d_head = jnp.concatenate([zero, d_out], axis=0)
        rows = jnp.concatenate([hq_ref[i].astype(jnp.float32), d_wide], axis=0).T
        left = lax.broadcasted_iota(jnp.int32, rows.shape, 1) < HEAD_DIM
        rhs = jnp.concatenate([jnp.where(left, 0.0, rows), jnp.where(left, rows, 0.0)], axis=0)
        rhs = rhs.astype(jnp.bfloat16)
        inverse = stats_ref[i, 0:1]
        row_dot = jnp.sum(head_ref[i].astype(jnp.float32) * d_wide, axis=0, keepdims=True)
        keys = kv_ref[...].reshape(N_SEQ * CHUNK, 2 * HEAD_DIM)
        prob = jnp.exp(matmul(keys, query)) * inverse
        d_scores = (prob * (matmul(keys, d_head) - row_dot)).astype(jnp.bfloat16)
        d_qunit = matmul(jnp.concatenate([ku_ref[j] for j in range(N_SEQ)], axis=1), d_scores)
        both = jnp.concatenate([prob.astype(jnp.bfloat16), d_scores], axis=1)
        sums[...] += matmul(both, rhs).reshape(N_SEQ, CHUNK, 2 * HEAD_DIM)
        dqt[i] = d_qunit * SCALE
        return carry

    lax.fori_loop(0, N_SEQ, step, 0)
    for j in range(N_SEQ):
        turned = sums[j].T
        pieces = []
        for t, d_unit in enumerate((dqt[j], turned[:HEAD_DIM])):
            wide = raw_ref[j, t * HEAD_DIM : (t + 1) * HEAD_DIM].astype(jnp.float32)
            factor = unit_factor(wide, 0)
            mean = jnp.mean(d_unit * wide, axis=0, keepdims=True)
            pieces.append(factor * d_unit - factor * factor * factor * wide * mean)
        stacked = jnp.concatenate(pieces + [turned[HEAD_DIM:]], axis=0).astype(jnp.bfloat16)
        stacks[j][...] = stacked
        wait(j)
        term = matmul(stacked, held[j])
        if j == 0:
            grad_t[: 3 * HEAD_DIM] = term
        else:
            grad_t[: 3 * HEAD_DIM] += term
    grad_t[3 * HEAD_DIM :] = jnp.zeros((HEAD_DIM, grad_t.shape[1]), jnp.float32)
    grad[...] = grad_t[...].T
    split_rows(place_ref[1], grad, keep_ref, give_ref)


def result_kernel(*refs):
    place_ref = refs[0]
    home_ref, w_ref, grad_ref, x_ref, act_ref = refs[10:15]
    out_ref, keep_ref, give_ref, grad_t, grad_msg, grad_out, held, sems = refs[15:]
    wait = fetch_chunks(refs[1:10], held, sems)
    z = place_ref[0]
    every = jnp.concatenate([home_ref[h, :HEAD_DIM] for h in range(N_SEQ)], axis=0)
    grad_out[...] = matmul(every, grad_ref[...])
    for j in range(N_SEQ):
        folded = home_ref[place_of(z, j), HEAD_DIM:].astype(jnp.float32)
        columns = jnp.concatenate([folded[:, :BLOCK].T, folded[:, BLOCK:].T], axis=1)
        wait(j)
        term = matmul(columns.astype(jnp.bfloat16), held[j])
        if j == 0:
            grad_t[...] = term
        else:
            grad_t[...] += term
    grad_msg[...] = grad_t[...].T
    split_rows(place_ref[1], grad_msg, keep_ref, give_ref)
    split_rows(place_ref[1], grad_out, keep_ref, give_ref, grad_msg.shape[0] // (2 * N_XY))
    attn = contract_rows(every, w_ref[...])
    out_ref[...] = (x_ref[...].astype(jnp.float32) + attn + act_ref[...]).astype(jnp.bfloat16)


def pair_kernel(keep_a, got_a, keep_b, got_b, out_ref):
    cut = keep_a.shape[1]
    for i in range(N_XY):
        out_ref[i, :cut] = (keep_a[i].astype(jnp.float32) + got_a[i].astype(jnp.float32)).astype(jnp.bfloat16)
        out_ref[i, cut:] = (keep_b[i].astype(jnp.float32) + got_b[i].astype(jnp.float32)).astype(jnp.bfloat16)


def share_kernel(shares_ref, out_ref):
    total = jnp.zeros(shares_ref.shape[1:], jnp.float32)
    for i in range(N_XY):
        total += shares_ref[i].astype(jnp.float32)
    for h in range(N_SEQ):
        out_ref[h] = total.astype(jnp.bfloat16)


def finish_kernel(every_ref, w_ref, m_ref, gain_ref, qkv_ref, out_ref, msg_ref, gain_out_ref):
    rows = msg_ref.shape[0]
    hd = N_SEQ * HEAD_DIM
    nodes = N_SEQ * CHUNK
    gain_sum = jnp.zeros((rows, BLOCK), jnp.float32)
    low = slice(0, HEAD_DIM)
    high = slice(HEAD_DIM, 2 * HEAD_DIM)
    for t, (band, half) in enumerate(((0, low), (0, high), (1, low))):
        for p in range(N_SEQ // 2):
            pieces = [every_ref[h, band * rows : (band + 1) * rows, half] for h in (2 * p, 2 * p + 1)]
            block = jnp.concatenate(pieces, axis=1).astype(jnp.float32) * (1.0 / nodes)
            columns = slice(t * hd + p * BLOCK, t * hd + (p + 1) * BLOCK)
            qkv_ref[:, columns] = block
            gain_sum += block * w_ref[:, columns].astype(jnp.float32)
    total = jnp.zeros((every_ref.shape[1] - 3 * rows, BLOCK), jnp.float32)
    for h in range(N_SEQ):
        columns = slice(h * BLOCK, (h + 1) * BLOCK)
        block = every_ref[h, 2 * rows : 3 * rows].astype(jnp.float32) * (1.0 / nodes)
        msg_ref[:, columns] = block
        gain_sum += block * m_ref[:, columns].astype(jnp.float32)
        total += every_ref[h, 3 * rows :].astype(jnp.float32)
    half_rows = out_ref.shape[0]
    for t in range(N_SEQ):
        out_ref[:, t * BLOCK : (t + 1) * BLOCK] = total[t * half_rows : (t + 1) * half_rows] * (1.0 / nodes)
    gain_out_ref[...] = jnp.sum(gain_sum, axis=1, keepdims=True) / gain_ref[...]


def input_grad_kernel(*refs):
    place_ref = refs[0]
    stacks = refs[1:9]
    w_ref, d_norm_ref, x_ref, grad_ref, gain_ref = refs[9:14]
    out_ref, gathered = refs[14:]
    z = place_ref[0]
    hd = N_SEQ * HEAD_DIM
    for j in range(N_SEQ):
        head = lax.rem(z + j, N_SEQ)
        for t in range(3):
            gathered[pl.ds(t * hd + head * HEAD_DIM, HEAD_DIM), :] = stacks[j][
                t * HEAD_DIM : (t + 1) * HEAD_DIM
            ]
    d_norm = matmul(w_ref[...], gathered[...]).T + d_norm_ref[...]
    wide = x_ref[...].astype(jnp.float32)
    inv_rms = unit_factor(wide, -1)
    x_hat = wide * inv_rms
    scaled = d_norm * gain_ref[...]
    d_feat = inv_rms * (scaled - x_hat * jnp.mean(scaled * x_hat, axis=-1, keepdims=True))
    out_ref[...] = (grad_ref[...].astype(jnp.float32) + d_feat).astype(jnp.bfloat16)


def after(value, *others):
    return lax.optimization_barrier((value,) + others)[0]


def exchange(array, axis):
    return lax.all_to_all(array, axis, split_axis=0, concat_axis=0, tiled=True)


def shift(array, distance):
    return lax.ppermute(array, "z", [(i, (i + distance) % N_SEQ) for i in range(N_SEQ)])


def up(array):
    return shift(array, 1)


def down(array):
    return shift(array, -1)


def sum_over_cores(keep, give):
    got = lax.ppermute(give, "c", [(0, 1), (1, 0)])
    return (keep.astype(jnp.float32) + got.astype(jnp.float32)).astype(jnp.bfloat16)


def sum_over_chips(pair):
    return jnp.sum(exchange(pair, ("x", "y")).astype(jnp.float32), axis=0)


def on_device(
    features, out_grad, norm_gain, w_qkv, w_out, w_msg, block_ids, block_counts, edge_tiles
):
    node_rows, width = features.shape
    hd = w_out.shape[0]
    nodes = N_SEQ * node_rows
    bf16, f32 = jnp.bfloat16, jnp.float32
    z = lax.axis_index("z")
    core = lax.axis_index("c")
    place = jnp.stack([z, core]).astype(jnp.int32)
    gain = norm_gain.reshape(1, width)
    wide_shape = ((node_rows, width), f32)
    low_shape = ((node_rows, width), bf16)

    (normed,) = call(normalize_kernel, "normalize", (low_shape,), (), (features, gain), moved=1 << 20)

    a1, b1 = up(normed), down(normed)
    (d_out,) = call(
        d_out_kernel, "d_out", (((N_SEQ, HEAD_DIM, node_rows), bf16),), (), (out_grad, w_out),
        flops=2 * node_rows * width * hd, moved=2 << 20,
    )
    w_head = pick_head(place, w_qkv)
    a1, b1, d_out, w_head = lax.optimization_barrier((a1, b1, d_out, w_head))
    a2, b2 = up(a1), down(b1)

    act, to_low, mid, to_high = call(
        message_kernel, "messages", (wide_shape, low_shape, wide_shape, low_shape),
        (place, block_ids, block_counts), (a1, normed, b1, w_msg, edge_tiles, out_grad),
        [pltpu.VMEM((6, BLOCK, width), bf16), pltpu.VMEM((6, BLOCK, width), f32)],
        flops=8 * node_rows * width * width, exps=node_rows * width, moved=8 << 20,
    )
    a2, b2, to_low, to_high = lax.optimization_barrier((a2, b2, to_low, to_high))
    a3, b3 = up(a2), down(b2)
    above, below = down(to_low), up(to_high)
    a3, b3, above, below = lax.optimization_barrier((a3, b3, above, below))
    half = node_rows // 2
    c4 = (up(a3[:half]), down(b3[half:]))
    d_msg_cut, d_norm = call(
        message_grad_kernel, "message_grad", (((N_SEQ, BLOCK, CHUNK), bf16), wide_shape),
        (), (mid, above, below, w_msg), flops=2 * node_rows * width * width, moved=8 << 20,
    )
    *c4, d_msg_cut, d_norm, d_out = lax.optimization_barrier((*c4, d_msg_cut, d_norm, d_out))
    chunks = (normed, a1, a2, a3, *c4, b3, b2, b1)
    d_heads = exchange(d_out, "z")

    held = pltpu.VMEM((N_SEQ, CHUNK, width), bf16)
    lanes_in = ((N_SEQ, CHUNK, 2 * HEAD_DIM), bf16)
    turned = ((N_SEQ, HEAD_DIM, CHUNK), bf16)
    send, *saved = call(
        forward_kernel, "attend_forward",
        (((N_SEQ, HEAD_DIM + BLOCK, CHUNK), bf16), lanes_in, turned, turned,
         ((N_SEQ, 2 * HEAD_DIM, CHUNK), bf16), turned, ((N_SEQ, 8, CHUNK), f32)),
        (place,), (w_head,),
        [pltpu.VMEM((N_SEQ, HEAD_DIM + ONES, CHUNK), bf16), held, pltpu.SemaphoreType.DMA((10,))],
        flops=12 * nodes * nodes * HEAD_DIM, exps=nodes * nodes, moved=8 << 20, far=chunks + (d_msg_cut,),
    )
    send, d_heads = lax.optimization_barrier((send, d_heads))
    home = exchange(send, "z")

    rows_here = width // (2 * N_XY)
    rows_out = hd // (2 * N_XY)
    part_head = ((N_XY, 2 * rows_here, BLOCK), bf16)
    *stacks, keep, give = call(
        backward_kernel, "attend_backward",
        (((3 * HEAD_DIM, CHUNK), bf16),) * N_SEQ + (part_head, part_head),
        (place,), (*saved, d_heads),
        [
            pltpu.VMEM((N_SEQ, CHUNK, 2 * HEAD_DIM), f32),
            pltpu.VMEM((N_SEQ, HEAD_DIM, CHUNK), f32),
            pltpu.VMEM((4 * HEAD_DIM, width), f32),
            pltpu.VMEM((width, 4 * HEAD_DIM), f32),
            held,
            pltpu.SemaphoreType.DMA((9,)),
        ],
        flops=24 * nodes * nodes * HEAD_DIM, exps=nodes * nodes, moved=8 << 20, far=chunks,
    )
    got = lax.ppermute(give, "c", [(0, 1), (1, 0)])

    part_out = ((N_XY, rows_here + rows_out * width // BLOCK, BLOCK), bf16)
    block_result_array, keep_out, give_out = call(
        result_kernel, "result", (low_shape, part_out, part_out), (place,),
        (after(home, keep), w_out, out_grad, features, act),
        [
            pltpu.VMEM((BLOCK, width), f32), pltpu.VMEM((width, BLOCK), f32), pltpu.VMEM((hd, width), f32),
            held, pltpu.SemaphoreType.DMA((9,)),
        ],
        flops=6 * node_rows * width * width, moved=10 << 20, far=chunks,
    )
    got_out = lax.ppermute(give_out, "c", [(0, 1), (1, 0)])
    all_rows = part_head[0][1] + part_out[0][1]
    (pair,) = call(
        pair_kernel, "pair_sum", (((N_XY, all_rows, BLOCK), bf16),), (), (keep, got, keep_out, got_out),
        moved=3 << 20,
    )
    pair, *stacks = lax.optimization_barrier((pair, *stacks))
    shares = exchange(pair, ("x", "y"))
    stacks = [stacks[0]] + [shift(stacks[j], -j) for j in range(1, N_SEQ)]
    shares, *stacks[1:5] = lax.optimization_barrier((shares, *stacks[1:5]))
    (mine,) = call(
        share_kernel, "share_sum", (((N_SEQ, all_rows, BLOCK), bf16),), (), (shares,), moved=2 << 20,
    )
    every = exchange(mine, "z")

    (grad_input,) = call(
        input_grad_kernel, "input_grad", (low_shape,), (place,),
        (*stacks, w_qkv, d_norm, features, out_grad, gain),
        [pltpu.VMEM((3 * hd, node_rows), bf16)],
        flops=6 * node_rows * width * hd, moved=8 << 20,
    )

    every, grad_input = lax.optimization_barrier((every, grad_input))
    first = ((lax.axis_index("x") * 4 + lax.axis_index("y")) * 2 + core) * rows_here
    w_rows = lax.dynamic_slice_in_dim(w_qkv, first, rows_here, 0)
    m_rows = lax.dynamic_slice_in_dim(w_msg, first, rows_here, 0)
    gain_rows = lax.dynamic_slice_in_dim(norm_gain, first, rows_here, 0).reshape(rows_here, 1)
    grad_qkv, grad_out, grad_msg, grad_gain = call(
        finish_kernel, "finish",
        (((rows_here, 3 * hd), f32), ((rows_out, width), f32), ((rows_here, width), f32), ((rows_here, 1), f32)),
        (), (every, w_rows, m_rows, gain_rows), moved=2 << 20,
    )
    return block_result_array, grad_input, grad_gain.reshape(rows_here), grad_qkv, grad_out, grad_msg


def solution(mesh):
    fine = Mesh(mesh.devices.reshape(4, 4, 2, N_SEQ), ("x", "y", "c", "z"))
    dp = ("x", "y", "c")
    rows = ("x", "y", "c", "z")
    return jax.shard_map(
        on_device,
        mesh=fine,
        in_specs=(
            P(rows, None),
            P(rows, None),
            P(),
            P(),
            P(),
            P(),
            P(rows, None),
            P(rows),
            P(rows, None, None, None),
        ),
        out_specs=(
            P(rows, None),
            P(rows, None),
            P(dp),
            P(dp, None),
            P(dp, None),
            P(dp, None),
        ),
        check_vma=False,
    )
```

```python
import jax
import jax.numpy as jnp
from jax import lax
from jax.experimental import pallas as pl
from jax.experimental.pallas import tpu as pltpu
from jax.sharding import Mesh
from jax.sharding import PartitionSpec as P

HEAD_DIM = 64
BLOCK = 128
SLOTS = 4
N_SEQ = 8
N_XY = 16
CHUNK = 256
ONES = 16

exponent_divisor = 32.0
epsilon = 1e-06
SCALE = exponent_divisor / HEAD_DIM


def matmul(left, right):
    return jnp.dot(left, right, preferred_element_type=jnp.float32)


def contract_rows(left, right):
    return lax.dot_general(
        left, right, (((0,), (0,)), ((), ())), preferred_element_type=jnp.float32
    )


def contract_cols(left, right):
    return lax.dot_general(
        left, right, (((1,), (1,)), ((), ())), preferred_element_type=jnp.float32
    )


def unit_factor(wide, axis):
    return lax.rsqrt(jnp.mean(wide * wide, axis=axis, keepdims=True) + epsilon)


def call(kernel, name, out_shape, scalars, arrays, scratch=(), flops=0, exps=0, moved=0, far=()):
    specs = [pl.BlockSpec(memory_space=pltpu.SMEM)] * len(scalars)
    specs += [pl.BlockSpec(memory_space=pltpu.HBM)] * len(far)
    specs += [pl.BlockSpec(memory_space=pltpu.VMEM)] * len(arrays)
    return pl.pallas_call(
        kernel,
        out_shape=tuple(jax.ShapeDtypeStruct(s, t) for s, t in out_shape),
        in_specs=specs,
        out_specs=tuple(pl.BlockSpec(memory_space=pltpu.VMEM) for _ in out_shape),
        scratch_shapes=list(scratch),
        compiler_params=pltpu.CompilerParams(vmem_limit_bytes=62 * 1024 * 1024),
        cost_estimate=pl.CostEstimate(flops=flops, bytes_accessed=moved, transcendentals=exps),
        name=name,
    )(*scalars, *far, *arrays)


def normalize_kernel(x_ref, gain_ref, out_ref):
    wide = x_ref[...].astype(jnp.float32)
    out_ref[...] = (wide * unit_factor(wide, -1) * gain_ref[...]).astype(jnp.bfloat16)


def d_out_kernel(grad_ref, w_ref, out_ref):
    turned = contract_cols(w_ref[...], grad_ref[...]).astype(jnp.bfloat16)
    for h in range(N_SEQ):
        out_ref[h] = turned[h * HEAD_DIM : (h + 1) * HEAD_DIM]


def pick_kernel(place_ref, q_ref, k_ref, v_ref, out_ref, turned):
    odd = lax.rem(place_ref[0], 2)
    for t, ref in enumerate((q_ref, k_ref, v_ref)):
        turned[...] = ref[...].astype(jnp.float32).T
        out_ref[t * HEAD_DIM : (t + 1) * HEAD_DIM] = turned[
            pl.ds(odd * HEAD_DIM, HEAD_DIM), :
        ].astype(jnp.bfloat16)


def pick_head(place, w_qkv):
    width, columns = w_qkv.shape
    step = columns // 3 // (2 * HEAD_DIM)

    def block(t):
        return pl.BlockSpec((width, 2 * HEAD_DIM), lambda i, place: (0, t * step + place[0] // 2))

    return pl.pallas_call(
        pick_kernel,
        grid_spec=pltpu.PrefetchScalarGridSpec(
            num_scalar_prefetch=1,
            grid=(1,),
            in_specs=[block(0), block(1), block(2)],
            out_specs=pl.BlockSpec((3 * HEAD_DIM, width), lambda i, place: (0, 0)),
            scratch_shapes=[pltpu.VMEM((2 * HEAD_DIM, width), jnp.float32)],
        ),
        out_shape=jax.ShapeDtypeStruct((3 * HEAD_DIM, width), jnp.bfloat16),
        cost_estimate=pl.CostEstimate(flops=0, bytes_accessed=4 << 20, transcendentals=0),
        name="pick_head",
    )(place, w_qkv, w_qkv, w_qkv)


def message_kernel(*refs):
    place_ref, ids_ref, counts_ref, low_ref, own_ref, high_ref, w_ref, tiles_ref, grad_ref = refs[:9]
    act_ref, to_low_ref, mid_ref, to_high_ref, msg, landed = refs[9:]
    z = place_ref[0]
    for t, ref in enumerate((low_ref, own_ref, high_ref)):
        rows = matmul(ref[...], w_ref[...]).astype(jnp.bfloat16)
        msg[2 * t] = rows[:BLOCK]
        msg[2 * t + 1] = rows[BLOCK:]
    landed[...] = jnp.zeros_like(landed)
    for b in range(2):
        spots = []
        live = []
        for s in range(SLOTS):
            spots.append(jnp.clip(ids_ref[b, s] - 2 * (z - 1), 0, 5))
            mask = jnp.where(s < counts_ref[b], 1.0, 0.0)
            live.append(tiles_ref[b, s].astype(jnp.float32) * mask)
        source = jnp.concatenate([msg[spot] for spot in spots], axis=0)
        agg = matmul(jnp.concatenate(live, axis=1).astype(jnp.bfloat16), source)
        sigma = 1.0 / (1.0 + jnp.exp(-agg))
        rows = slice(b * BLOCK, (b + 1) * BLOCK)
        act_ref[rows] = agg * sigma
        d_agg = grad_ref[rows].astype(jnp.float32) * sigma * (1.0 + agg * (1.0 - sigma))
        d_agg = d_agg.astype(jnp.bfloat16)
        for s in range(SLOTS):
            landed[spots[s]] += matmul(live[s].T.astype(jnp.bfloat16), d_agg)
    for b in range(2):
        rows = slice(b * BLOCK, (b + 1) * BLOCK)
        to_low_ref[rows] = landed[b].astype(jnp.bfloat16)
        mid_ref[rows] = landed[2 + b]
        to_high_ref[rows] = landed[4 + b].astype(jnp.bfloat16)


def split_rows(core, source, keep_ref, give_ref, offset=0):
    rows = source.shape[0] // (2 * N_XY)
    for i in range(N_XY):
        for t in range(source.shape[1] // BLOCK):
            spot = slice(offset + t * rows, offset + (t + 1) * rows)
            columns = slice(t * BLOCK, (t + 1) * BLOCK)
            keep_ref[i, spot] = source[pl.ds((2 * i + core) * rows, rows), columns].astype(jnp.bfloat16)
            give_ref[i, spot] = source[pl.ds((2 * i + 1 - core) * rows, rows), columns].astype(
                jnp.bfloat16
            )


def message_grad_kernel(*refs):
    mid_ref, above_ref, below_ref, w_ref = refs[:4]
    cut_ref, d_norm_ref = refs[4:]
    total = mid_ref[...] + above_ref[...].astype(jnp.float32) + below_ref[...].astype(jnp.float32)
    d_msg = total.astype(jnp.bfloat16)
    for t in range(N_SEQ):
        columns = d_msg[:, t * BLOCK : (t + 1) * BLOCK]
        cut_ref[t] = jnp.concatenate([columns[:BLOCK], columns[BLOCK:]], axis=1)
    d_norm_ref[...] = contract_cols(d_msg, w_ref[...])


def place_of(z, j):
    return lax.rem(z - j + N_SEQ, N_SEQ)


def fetch_chunks(refs, held, sems):
    half = CHUNK // 2
    targets = [held.at[j] for j in range(4)]
    targets += [held.at[4, pl.ds(0, half)], held.at[4, pl.ds(half, half)]]
    targets += [held.at[j] for j in range(5, N_SEQ)]
    copies = [pltpu.make_async_copy(ref, to, sems.at[i]) for i, (ref, to) in enumerate(zip(refs, targets))]
    for copy in copies:
        copy.start()

    def wait(j):
        for copy in copies[j + (j > 4) : j + 1 + (j >= 4)]:
            copy.wait()

    return wait


def forward_kernel(*refs):
    z = refs[0][0]
    cut_ref, w_ref = refs[10:12]
    send_ref, kv_ref, hq_ref, ku_ref, raw_ref, out_ref, stats_ref = refs[12:19]
    v_ext, held, sems = refs[19:22]
    wait = fetch_chunks(refs[1:10], held, sems)
    pass_on = pltpu.make_async_copy(cut_ref, send_ref.at[:, pl.ds(HEAD_DIM, BLOCK)], sems.at[9])
    pass_on.start()
    for j in range(N_SEQ):
        wait(j)
        proj = contract_cols(w_ref[...], held[j]).astype(jnp.bfloat16)
        raw_ref[j] = proj[: 2 * HEAD_DIM]
        query = proj[:HEAD_DIM].astype(jnp.float32)
        keyrow = proj[HEAD_DIM : 2 * HEAD_DIM].astype(jnp.float32)
        val = proj[2 * HEAD_DIM :]
        q_unit = (query * unit_factor(query, 0)).astype(jnp.bfloat16).astype(jnp.float32) * SCALE
        k_unit = keyrow * unit_factor(keyrow, 0)
        hq_ref[j] = q_unit.astype(jnp.bfloat16)
        ku_ref[j] = k_unit.astype(jnp.bfloat16)
        v_ext[j, :HEAD_DIM] = val
        v_ext[j, HEAD_DIM:] = jnp.ones((ONES, CHUNK), jnp.bfloat16)
        kv_ref[j] = jnp.concatenate([k_unit, val.astype(jnp.float32)], axis=0).T.astype(jnp.bfloat16)

    def step(i, carry):
        query = jnp.concatenate([hq_ref[i], jnp.zeros_like(hq_ref[i])], axis=0)
        keys = kv_ref[...].reshape(N_SEQ * CHUNK, 2 * HEAD_DIM)
        exps = jnp.exp(matmul(keys, query)).astype(jnp.bfloat16)
        out = matmul(jnp.concatenate([v_ext[j] for j in range(N_SEQ)], axis=1), exps)
        inverse = 1.0 / out[HEAD_DIM : HEAD_DIM + 1]
        stats_ref[i, 0:1] = inverse
        head_out = (out[:HEAD_DIM] * inverse).astype(jnp.bfloat16)
        out_ref[i] = head_out
        send_ref[place_of(z, i), :HEAD_DIM] = head_out
        return carry

    lax.fori_loop(0, N_SEQ, step, 0)
    pass_on.wait()


def backward_kernel(*refs):
    z = refs[0][0]
    kv_ref, hq_ref, ku_ref, raw_ref, head_ref, stats_ref, d_ref = refs[1:8]
    stack_ref, sums, dqt = refs[8:]
    sums[...] = jnp.zeros_like(sums)

    def step(i, carry):
        zero = jnp.zeros_like(hq_ref[i])
        query = jnp.concatenate([hq_ref[i], zero], axis=0)
        d_out = d_ref[place_of(z, i)]
        d_wide = d_out.astype(jnp.float32)
        d_head = jnp.concatenate([zero, d_out], axis=0)
        rows = jnp.concatenate([hq_ref[i].astype(jnp.float32), d_wide], axis=0).T
        left = lax.broadcasted_iota(jnp.int32, rows.shape, 1) < HEAD_DIM
        rhs = jnp.concatenate([jnp.where(left, 0.0, rows), jnp.where(left, rows, 0.0)], axis=0)
        rhs = rhs.astype(jnp.bfloat16)
        inverse = stats_ref[i, 0:1]
        row_dot = jnp.sum(head_ref[i].astype(jnp.float32) * d_wide, axis=0, keepdims=True)
        keys = kv_ref[...].reshape(N_SEQ * CHUNK, 2 * HEAD_DIM)
        prob = jnp.exp(matmul(keys, query)) * inverse
        d_scores = (prob * (matmul(keys, d_head) - row_dot)).astype(jnp.bfloat16)
        d_qunit = matmul(jnp.concatenate([ku_ref[j] for j in range(N_SEQ)], axis=1), d_scores)
        both = jnp.concatenate([prob.astype(jnp.bfloat16), d_scores], axis=1)
        sums[...] += matmul(both, rhs).reshape(N_SEQ, CHUNK, 2 * HEAD_DIM)
        dqt[i] = d_qunit * SCALE
        return carry

    lax.fori_loop(0, N_SEQ, step, 0)
    for j in range(N_SEQ):
        turned = sums[j].T
        pieces = []
        for t, d_unit in enumerate((dqt[j], turned[:HEAD_DIM])):
            wide = raw_ref[j, t * HEAD_DIM : (t + 1) * HEAD_DIM].astype(jnp.float32)
            factor = unit_factor(wide, 0)
            mean = jnp.mean(d_unit * wide, axis=0, keepdims=True)
            pieces.append(factor * d_unit - factor * factor * factor * wide * mean)
        stacked = jnp.concatenate(pieces + [turned[HEAD_DIM:]], axis=0).astype(jnp.bfloat16)
        stack_ref[place_of(z, j)] = stacked


def result_kernel(*refs):
    place_ref = refs[0]
    home_ref, stack_ref, w_ref, grad_ref, x_ref, act_ref = refs[10:16]
    out_ref, keep_ref, give_ref, grad_t, grad_node, grad_out, held, sems = refs[16:]
    wait = fetch_chunks(refs[1:10], held, sems)
    z = place_ref[0]
    every = jnp.concatenate([home_ref[h, :HEAD_DIM] for h in range(N_SEQ)], axis=0)
    grad_out[...] = matmul(every, grad_ref[...])
    for j in range(N_SEQ):
        folded = home_ref[place_of(z, j), HEAD_DIM:].astype(jnp.float32)
        columns = jnp.concatenate([folded[:, :BLOCK].T, folded[:, BLOCK:].T], axis=1)
        d_head = stack_ref[place_of(z, j)]
        pad = jnp.zeros((HEAD_DIM, CHUNK), jnp.bfloat16)
        both = jnp.concatenate([d_head, pad, columns.astype(jnp.bfloat16)], axis=0)
        wait(j)
        term = matmul(both, held[j])
        if j == 0:
            grad_t[...] = term
        else:
            grad_t[...] += term
    grad_node[...] = grad_t[...].T
    split_rows(place_ref[1], grad_node, keep_ref, give_ref)
    split_rows(place_ref[1], grad_out, keep_ref, give_ref, 3 * (grad_node.shape[0] // (2 * N_XY)))
    attn = contract_rows(every, w_ref[...])
    out_ref[...] = (x_ref[...].astype(jnp.float32) + attn + act_ref[...]).astype(jnp.bfloat16)


def share_kernel(shares_ref, out_ref):
    total = jnp.zeros(shares_ref.shape[1:], jnp.float32)
    for i in range(N_XY):
        total += shares_ref[i].astype(jnp.float32)
    for h in range(N_SEQ):
        out_ref[h] = total.astype(jnp.bfloat16)


def finish_kernel(every_ref, w_ref, m_ref, gain_ref, qkv_ref, out_ref, msg_ref, gain_out_ref):
    rows = msg_ref.shape[0]
    hd = N_SEQ * HEAD_DIM
    nodes = N_SEQ * CHUNK
    gain_sum = jnp.zeros((rows, BLOCK), jnp.float32)
    low = slice(0, HEAD_DIM)
    high = slice(HEAD_DIM, 2 * HEAD_DIM)
    for t, (band, half) in enumerate(((0, low), (0, high), (1, low))):
        for p in range(N_SEQ // 2):
            pieces = [every_ref[h, band * rows : (band + 1) * rows, half] for h in (2 * p, 2 * p + 1)]
            block = jnp.concatenate(pieces, axis=1).astype(jnp.float32) * (1.0 / nodes)
            columns = slice(t * hd + p * BLOCK, t * hd + (p + 1) * BLOCK)
            qkv_ref[:, columns] = block
            gain_sum += block * w_ref[:, columns].astype(jnp.float32)
    total = jnp.zeros((every_ref.shape[1] - 3 * rows, BLOCK), jnp.float32)
    for h in range(N_SEQ):
        columns = slice(h * BLOCK, (h + 1) * BLOCK)
        block = every_ref[h, 2 * rows : 3 * rows].astype(jnp.float32) * (1.0 / nodes)
        msg_ref[:, columns] = block
        gain_sum += block * m_ref[:, columns].astype(jnp.float32)
        total += every_ref[h, 3 * rows :].astype(jnp.float32)
    half_rows = out_ref.shape[0]
    for t in range(N_SEQ):
        out_ref[:, t * BLOCK : (t + 1) * BLOCK] = total[t * half_rows : (t + 1) * half_rows] * (1.0 / nodes)
    gain_out_ref[...] = jnp.sum(gain_sum.T, axis=0, keepdims=True) / gain_ref[...]


def input_grad_kernel(*refs):
    stack_ref, w_ref, d_norm_ref, x_ref, grad_ref, gain_ref, out_ref = refs
    parts = [
        stack_ref[h, t * HEAD_DIM : (t + 1) * HEAD_DIM] for t in range(3) for h in range(N_SEQ)
    ]
    d_norm = matmul(w_ref[...], jnp.concatenate(parts, axis=0)).T + d_norm_ref[...]
    wide = x_ref[...].astype(jnp.float32)
    inv_rms = unit_factor(wide, -1)
    x_hat = wide * inv_rms
    scaled = d_norm * gain_ref[...]
    d_feat = inv_rms * (scaled - x_hat * jnp.mean(scaled * x_hat, axis=-1, keepdims=True))
    out_ref[...] = (grad_ref[...].astype(jnp.float32) + d_feat).astype(jnp.bfloat16)


def after(value, *others):
    return lax.optimization_barrier((value,) + others)[0]


def exchange(array, axis):
    return lax.all_to_all(array, axis, split_axis=0, concat_axis=0, tiled=True)


def shift(array, distance):
    return lax.ppermute(array, "z", [(i, (i + distance) % N_SEQ) for i in range(N_SEQ)])


def up(array):
    return shift(array, 1)


def down(array):
    return shift(array, -1)


def sum_over_cores(keep, give):
    got = lax.ppermute(give, "c", [(0, 1), (1, 0)])
    return (keep.astype(jnp.float32) + got.astype(jnp.float32)).astype(jnp.bfloat16)


def sum_over_chips(pair):
    return jnp.sum(exchange(pair, ("x", "y")).astype(jnp.float32), axis=0)


def on_device(
    features, out_grad, norm_gain, w_qkv, w_out, w_msg, block_ids, block_counts, edge_tiles
):
    node_rows, width = features.shape
    hd = w_out.shape[0]
    nodes = N_SEQ * node_rows
    bf16, f32 = jnp.bfloat16, jnp.float32
    z = lax.axis_index("z")
    core = lax.axis_index("c")
    place = jnp.stack([z, core]).astype(jnp.int32)
    gain = norm_gain.reshape(1, width)
    wide_shape = ((node_rows, width), f32)
    low_shape = ((node_rows, width), bf16)

    (normed,) = call(normalize_kernel, "normalize", (low_shape,), (), (features, gain), moved=1 << 20)

    a1, b1 = up(normed), down(normed)
    (d_out,) = call(
        d_out_kernel, "d_out", (((N_SEQ, HEAD_DIM, node_rows), bf16),), (), (out_grad, w_out),
        flops=2 * node_rows * width * hd, moved=2 << 20,
    )
    w_head = pick_head(place, w_qkv)
    a1, b1, d_out, w_head = lax.optimization_barrier((a1, b1, d_out, w_head))
    a2, b2 = up(a1), down(b1)

    act, to_low, mid, to_high = call(
        message_kernel, "messages", (wide_shape, low_shape, wide_shape, low_shape),
        (place, block_ids, block_counts), (a1, normed, b1, w_msg, edge_tiles, out_grad),
        [pltpu.VMEM((6, BLOCK, width), bf16), pltpu.VMEM((6, BLOCK, width), f32)],
        flops=8 * node_rows * width * width, exps=node_rows * width, moved=8 << 20,
    )
    a2, b2, to_low, to_high = lax.optimization_barrier((a2, b2, to_low, to_high))
    a3, b3 = up(a2), down(b2)
    above, below = down(to_low), up(to_high)
    a3, b3, above, below = lax.optimization_barrier((a3, b3, above, below))
    half = node_rows // 2
    c4 = (up(a3[:half]), down(b3[half:]))
    d_msg_cut, d_norm = call(
        message_grad_kernel, "message_grad", (((N_SEQ, BLOCK, CHUNK), bf16), wide_shape),
        (), (mid, above, below, w_msg), flops=2 * node_rows * width * width, moved=8 << 20,
    )
    *c4, d_msg_cut, d_norm, d_out = lax.optimization_barrier((*c4, d_msg_cut, d_norm, d_out))
    chunks = (normed, a1, a2, a3, *c4, b3, b2, b1)
    d_heads = exchange(d_out, "z")

    held = pltpu.VMEM((N_SEQ, CHUNK, width), bf16)
    lanes_in = ((N_SEQ, CHUNK, 2 * HEAD_DIM), bf16)
    turned = ((N_SEQ, HEAD_DIM, CHUNK), bf16)
    send, *saved = call(
        forward_kernel, "attend_forward",
        (((N_SEQ, HEAD_DIM + BLOCK, CHUNK), bf16), lanes_in, turned, turned,
         ((N_SEQ, 2 * HEAD_DIM, CHUNK), bf16), turned, ((N_SEQ, 8, CHUNK), f32)),
        (place,), (w_head,),
        [pltpu.VMEM((N_SEQ, HEAD_DIM + ONES, CHUNK), bf16), held, pltpu.SemaphoreType.DMA((10,))],
        flops=12 * nodes * nodes * HEAD_DIM, exps=nodes * nodes, moved=8 << 20, far=chunks + (d_msg_cut,),
    )
    send, d_heads = lax.optimization_barrier((send, d_heads))
    home = exchange(send, "z")

    rows_here = width // (2 * N_XY)
    rows_out = hd // (2 * N_XY)
    (stack,) = call(
        backward_kernel, "attend_backward", (((N_SEQ, 3 * HEAD_DIM, CHUNK), bf16),),
        (place,), (*saved, d_heads),
        [pltpu.VMEM((N_SEQ, CHUNK, 2 * HEAD_DIM), f32), pltpu.VMEM((N_SEQ, HEAD_DIM, CHUNK), f32)],
        flops=24 * nodes * nodes * HEAD_DIM, exps=nodes * nodes, moved=4 << 20,
    )
    stack, home = lax.optimization_barrier((stack, home))
    stack_home = exchange(stack, "z")

    all_rows = 3 * rows_here + rows_out * width // BLOCK
    part = ((N_XY, all_rows, BLOCK), bf16)
    block_result_array, keep, give = call(
        result_kernel, "result", (low_shape, part, part), (place,),
        (home, stack, w_out, out_grad, features, act),
        [
            pltpu.VMEM((3 * BLOCK, width), f32), pltpu.VMEM((width, 3 * BLOCK), f32),
            pltpu.VMEM((hd, width), f32), held, pltpu.SemaphoreType.DMA((9,)),
        ],
        flops=8 * node_rows * width * width, moved=10 << 20, far=chunks,
    )
    got = lax.ppermute(give, "c", [(0, 1), (1, 0)])
    pair = (keep.astype(f32) + got.astype(f32)).astype(bf16)
    pair, stack_home = lax.optimization_barrier((pair, stack_home))
    shares = exchange(pair, ("x", "y"))
    (mine,) = call(
        share_kernel, "share_sum", (((N_SEQ, all_rows, BLOCK), bf16),), (), (shares,), moved=2 << 20,
    )
    every = exchange(mine, "z")

    (grad_input,) = call(
        input_grad_kernel, "input_grad", (low_shape,), (),
        (after(stack_home, mine), w_qkv, d_norm, features, out_grad, gain),
        flops=6 * node_rows * width * hd, moved=8 << 20,
    )

    every, grad_input = lax.optimization_barrier((every, grad_input))
    first = ((lax.axis_index("x") * 4 + lax.axis_index("y")) * 2 + core) * rows_here
    w_rows = lax.dynamic_slice_in_dim(w_qkv, first, rows_here, 0)
    m_rows = lax.dynamic_slice_in_dim(w_msg, first, rows_here, 0)
    gain_rows = lax.dynamic_slice_in_dim(norm_gain, first, rows_here, 0).reshape(1, rows_here)
    grad_qkv, grad_out, grad_msg, grad_gain = call(
        finish_kernel, "finish",
        (((rows_here, 3 * hd), f32), ((rows_out, width), f32), ((rows_here, width), f32), ((1, rows_here), f32)),
        (), (every, w_rows, m_rows, gain_rows), moved=2 << 20,
    )
    return block_result_array, grad_input, grad_gain.reshape(rows_here), grad_qkv, grad_out, grad_msg


def solution(mesh):
    fine = Mesh(mesh.devices.reshape(4, 4, 2, N_SEQ), ("x", "y", "c", "z"))
    dp = ("x", "y", "c")
    rows = ("x", "y", "c", "z")
    return jax.shard_map(
        on_device,
        mesh=fine,
        in_specs=(
            P(rows, None),
            P(rows, None),
            P(),
            P(),
            P(),
            P(),
            P(rows, None),
            P(rows),
            P(rows, None, None, None),
        ),
        out_specs=(
            P(rows, None),
            P(rows, None),
            P(dp),
            P(dp, None),
            P(dp, None),
            P(dp, None),
        ),
        check_vma=False,
    )
```

```python
import jax
import jax.numpy as jnp
from jax import lax
from jax.experimental import pallas as pl
from jax.experimental.pallas import tpu as pltpu
from jax.sharding import Mesh
from jax.sharding import PartitionSpec as P

HEAD_DIM = 64
BLOCK = 128
SLOTS = 4
N_SEQ = 8
N_XY = 16
CHUNK = 256
ONES = 16

exponent_divisor = 32.0
epsilon = 1e-06
SCALE = exponent_divisor / HEAD_DIM


def matmul(left, right):
    return jnp.dot(left, right, preferred_element_type=jnp.float32)


def contract_rows(left, right):
    return lax.dot_general(
        left, right, (((0,), (0,)), ((), ())), preferred_element_type=jnp.float32
    )


def contract_cols(left, right):
    return lax.dot_general(
        left, right, (((1,), (1,)), ((), ())), preferred_element_type=jnp.float32
    )


def unit_factor(wide, axis):
    return lax.rsqrt(jnp.mean(wide * wide, axis=axis, keepdims=True) + epsilon)


def call(kernel, name, out_shape, scalars, arrays, scratch=(), flops=0, exps=0, moved=0, far=()):
    specs = [pl.BlockSpec(memory_space=pltpu.SMEM)] * len(scalars)
    specs += [pl.BlockSpec(memory_space=pltpu.HBM)] * len(far)
    specs += [pl.BlockSpec(memory_space=pltpu.VMEM)] * len(arrays)
    return pl.pallas_call(
        kernel,
        out_shape=tuple(jax.ShapeDtypeStruct(s, t) for s, t in out_shape),
        in_specs=specs,
        out_specs=tuple(pl.BlockSpec(memory_space=pltpu.VMEM) for _ in out_shape),
        scratch_shapes=list(scratch),
        compiler_params=pltpu.CompilerParams(vmem_limit_bytes=62 * 1024 * 1024),
        cost_estimate=pl.CostEstimate(flops=flops, bytes_accessed=moved, transcendentals=exps),
        name=name,
    )(*scalars, *far, *arrays)


def normalize_kernel(x_ref, gain_ref, out_ref):
    wide = x_ref[...].astype(jnp.float32)
    out_ref[...] = (wide * unit_factor(wide, -1) * gain_ref[...]).astype(jnp.bfloat16)


def normalize_half(features, gain, half):
    width = features.shape[1]
    return pl.pallas_call(
        normalize_kernel,
        grid=(1,),
        in_specs=[
            pl.BlockSpec((BLOCK, width), lambda i: (half, 0)),
            pl.BlockSpec((1, width), lambda i: (0, 0)),
        ],
        out_specs=pl.BlockSpec((BLOCK, width), lambda i: (0, 0)),
        out_shape=jax.ShapeDtypeStruct((BLOCK, width), jnp.bfloat16),
        cost_estimate=pl.CostEstimate(flops=0, bytes_accessed=1 << 19, transcendentals=0),
        name="normalize",
    )(features, gain)


def d_out_kernel(grad_ref, w_ref, out_ref):
    turned = contract_cols(w_ref[...], grad_ref[...]).astype(jnp.bfloat16)
    for h in range(N_SEQ):
        out_ref[h] = turned[h * HEAD_DIM : (h + 1) * HEAD_DIM]


def pick_kernel(place_ref, q_ref, k_ref, v_ref, out_ref, turned):
    odd = lax.rem(place_ref[0], 2)
    for t, ref in enumerate((q_ref, k_ref, v_ref)):
        turned[...] = ref[...].astype(jnp.float32).T
        out_ref[t * HEAD_DIM : (t + 1) * HEAD_DIM] = turned[
            pl.ds(odd * HEAD_DIM, HEAD_DIM), :
        ].astype(jnp.bfloat16)


def pick_head(place, w_qkv):
    width, columns = w_qkv.shape
    step = columns // 3 // (2 * HEAD_DIM)

    def block(t):
        return pl.BlockSpec((width, 2 * HEAD_DIM), lambda i, place: (0, t * step + place[0] // 2))

    return pl.pallas_call(
        pick_kernel,
        grid_spec=pltpu.PrefetchScalarGridSpec(
            num_scalar_prefetch=1,
            grid=(1,),
            in_specs=[block(0), block(1), block(2)],
            out_specs=pl.BlockSpec((3 * HEAD_DIM, width), lambda i, place: (0, 0)),
            scratch_shapes=[pltpu.VMEM((2 * HEAD_DIM, width), jnp.float32)],
        ),
        out_shape=jax.ShapeDtypeStruct((3 * HEAD_DIM, width), jnp.bfloat16),
        cost_estimate=pl.CostEstimate(flops=0, bytes_accessed=4 << 20, transcendentals=0),
        name="pick_head",
    )(place, w_qkv, w_qkv, w_qkv)


def message_kernel(*refs):
    place_ref, ids_ref, counts_ref = refs[:3]
    blocks = refs[3:9]
    w_ref, tiles_ref, grad_ref = refs[9:12]
    act_ref, to_low_ref, mid_ref, to_high_ref, msg, landed = refs[12:]
    z = place_ref[0]
    for t in range(3):
        both = jnp.concatenate([blocks[2 * t][...], blocks[2 * t + 1][...]], axis=0)
        rows = matmul(both, w_ref[...]).astype(jnp.bfloat16)
        msg[2 * t] = rows[:BLOCK]
        msg[2 * t + 1] = rows[BLOCK:]
    landed[...] = jnp.zeros_like(landed)
    for b in range(2):
        spots = []
        live = []
        for s in range(SLOTS):
            spots.append(jnp.clip(ids_ref[b, s] - 2 * (z - 1), 0, 5))
            mask = jnp.where(s < counts_ref[b], 1.0, 0.0)
            live.append(tiles_ref[b, s].astype(jnp.float32) * mask)
        source = jnp.concatenate([msg[spot] for spot in spots], axis=0)
        agg = matmul(jnp.concatenate(live, axis=1).astype(jnp.bfloat16), source)
        sigma = 1.0 / (1.0 + jnp.exp(-agg))
        rows = slice(b * BLOCK, (b + 1) * BLOCK)
        act_ref[rows] = agg * sigma
        d_agg = grad_ref[rows].astype(jnp.float32) * sigma * (1.0 + agg * (1.0 - sigma))
        d_agg = d_agg.astype(jnp.bfloat16)
        for s in range(SLOTS):
            landed[spots[s]] += matmul(live[s].T.astype(jnp.bfloat16), d_agg)
    for b in range(2):
        rows = slice(b * BLOCK, (b + 1) * BLOCK)
        to_low_ref[rows] = landed[b].astype(jnp.bfloat16)
        mid_ref[rows] = landed[2 + b]
        to_high_ref[rows] = landed[4 + b].astype(jnp.bfloat16)


def split_rows(core, source, keep_ref, give_ref, offset=0):
    rows = source.shape[0] // (2 * N_XY)
    for i in range(N_XY):
        for t in range(source.shape[1] // BLOCK):
            spot = slice(offset + t * rows, offset + (t + 1) * rows)
            columns = slice(t * BLOCK, (t + 1) * BLOCK)
            keep_ref[i, spot] = source[pl.ds((2 * i + core) * rows, rows), columns].astype(jnp.bfloat16)
            give_ref[i, spot] = source[pl.ds((2 * i + 1 - core) * rows, rows), columns].astype(
                jnp.bfloat16
            )


def merge_kernel(heads_ref, mid_ref, above_ref, below_ref, send_ref, d_msg_ref):
    total = mid_ref[...] + above_ref[...].astype(jnp.float32) + below_ref[...].astype(jnp.float32)
    d_msg = total.astype(jnp.bfloat16)
    d_msg_ref[...] = d_msg
    for t in range(N_SEQ):
        columns = d_msg[:, t * BLOCK : (t + 1) * BLOCK]
        send_ref[t, :HEAD_DIM] = heads_ref[t]
        send_ref[t, HEAD_DIM:] = jnp.concatenate([columns[:BLOCK], columns[BLOCK:]], axis=1)


def place_of(z, j):
    return lax.rem(z - j + N_SEQ, N_SEQ)


def fetch_chunks(refs, held, sems):
    copies = [
        pltpu.make_async_copy(ref, held.at[i // 2, pl.ds(i % 2 * BLOCK, BLOCK)], sems.at[i])
        for i, ref in enumerate(refs)
    ]
    for copy in copies:
        copy.start()

    def wait(j):
        copies[2 * j].wait()
        copies[2 * j + 1].wait()

    return wait


def forward_kernel(*refs):
    z = refs[0][0]
    w_ref = refs[17]
    out_ref, kv_ref, hq_ref, ku_ref, raw_ref, stats_ref = refs[18:24]
    v_ext, held, sems = refs[24:]
    wait = fetch_chunks(refs[1:17], held, sems)
    for j in range(N_SEQ):
        wait(j)
        proj = contract_cols(w_ref[...], held[j]).astype(jnp.bfloat16)
        raw_ref[j] = proj[: 2 * HEAD_DIM]
        query = proj[:HEAD_DIM].astype(jnp.float32)
        keyrow = proj[HEAD_DIM : 2 * HEAD_DIM].astype(jnp.float32)
        val = proj[2 * HEAD_DIM :]
        q_unit = (query * unit_factor(query, 0)).astype(jnp.bfloat16).astype(jnp.float32) * SCALE
        k_unit = keyrow * unit_factor(keyrow, 0)
        hq_ref[j] = q_unit.astype(jnp.bfloat16)
        ku_ref[j] = k_unit.astype(jnp.bfloat16)
        v_ext[j, :HEAD_DIM] = val
        v_ext[j, HEAD_DIM:] = jnp.ones((ONES, CHUNK), jnp.bfloat16)
        kv_ref[j] = jnp.concatenate([k_unit, val.astype(jnp.float32)], axis=0).T.astype(jnp.bfloat16)

    def step(i, carry):
        query = jnp.concatenate([hq_ref[i], jnp.zeros_like(hq_ref[i])], axis=0)
        keys = kv_ref[...].reshape(N_SEQ * CHUNK, 2 * HEAD_DIM)
        exps = jnp.exp(matmul(keys, query)).astype(jnp.bfloat16)
        out = matmul(jnp.concatenate([v_ext[j] for j in range(N_SEQ)], axis=1), exps)
        inverse = 1.0 / out[HEAD_DIM : HEAD_DIM + 1]
        stats_ref[i, 0:1] = inverse
        head_out = (out[:HEAD_DIM] * inverse).astype(jnp.bfloat16)
        out_ref[place_of(z, i)] = head_out
        return carry

    lax.fori_loop(0, N_SEQ, step, 0)


def backward_kernel(*refs):
    z = refs[0][0]
    head_ref, kv_ref, hq_ref, ku_ref, raw_ref, stats_ref, d_ref = refs[1:8]
    stack_ref, sums, dqt = refs[8:]
    sums[...] = jnp.zeros_like(sums)

    def step(i, carry):
        zero = jnp.zeros_like(hq_ref[i])
        query = jnp.concatenate([hq_ref[i], zero], axis=0)
        d_out = d_ref[place_of(z, i)]
        d_wide = d_out.astype(jnp.float32)
        d_head = jnp.concatenate([zero, d_out], axis=0)
        rows = jnp.concatenate([hq_ref[i].astype(jnp.float32), d_wide], axis=0).T
        left = lax.broadcasted_iota(jnp.int32, rows.shape, 1) < HEAD_DIM
        rhs = jnp.concatenate([jnp.where(left, 0.0, rows), jnp.where(left, rows, 0.0)], axis=0)
        rhs = rhs.astype(jnp.bfloat16)
        inverse = stats_ref[i, 0:1]
        row_dot = jnp.sum(head_ref[place_of(z, i)].astype(jnp.float32) * d_wide, axis=0, keepdims=True)
        keys = kv_ref[...].reshape(N_SEQ * CHUNK, 2 * HEAD_DIM)
        prob = jnp.exp(matmul(keys, query)) * inverse
        d_scores = (prob * (matmul(keys, d_head) - row_dot)).astype(jnp.bfloat16)
        d_qunit = matmul(jnp.concatenate([ku_ref[j] for j in range(N_SEQ)], axis=1), d_scores)
        both = jnp.concatenate([prob.astype(jnp.bfloat16), d_scores], axis=1)
        sums[...] += matmul(both, rhs).reshape(N_SEQ, CHUNK, 2 * HEAD_DIM)
        dqt[i] = d_qunit * SCALE
        return carry

    lax.fori_loop(0, N_SEQ, step, 0)
    for j in range(N_SEQ):
        turned = sums[j].T
        pieces = []
        for t, d_unit in enumerate((dqt[j], turned[:HEAD_DIM])):
            wide = raw_ref[j, t * HEAD_DIM : (t + 1) * HEAD_DIM].astype(jnp.float32)
            factor = unit_factor(wide, 0)
            mean = jnp.mean(d_unit * wide, axis=0, keepdims=True)
            pieces.append(factor * d_unit - factor * factor * factor * wide * mean)
        stacked = jnp.concatenate(pieces + [turned[HEAD_DIM:]], axis=0).astype(jnp.bfloat16)
        stack_ref[place_of(z, j)] = stacked


def result_kernel(*refs):
    place_ref = refs[0]
    home_ref, stack_ref, w_ref, grad_ref, x_ref, act_ref = refs[17:23]
    out_ref, keep_ref, give_ref, grad_t, grad_node, grad_out, held, sems = refs[23:]
    wait = fetch_chunks(refs[1:17], held, sems)
    z = place_ref[0]
    every = jnp.concatenate([home_ref[h, :HEAD_DIM] for h in range(N_SEQ)], axis=0)
    grad_out[...] = matmul(every, grad_ref[...])
    for j in range(N_SEQ):
        folded = home_ref[place_of(z, j), HEAD_DIM:].astype(jnp.float32)
        columns = jnp.concatenate([folded[:, :BLOCK].T, folded[:, BLOCK:].T], axis=1)
        d_head = stack_ref[place_of(z, j)]
        pad = jnp.zeros((HEAD_DIM, CHUNK), jnp.bfloat16)
        both = jnp.concatenate([d_head, pad, columns.astype(jnp.bfloat16)], axis=0)
        wait(j)
        term = matmul(both, held[j])
        if j == 0:
            grad_t[...] = term
        else:
            grad_t[...] += term
    grad_node[...] = grad_t[...].T
    split_rows(place_ref[1], grad_node, keep_ref, give_ref)
    split_rows(place_ref[1], grad_out, keep_ref, give_ref, 3 * (grad_node.shape[0] // (2 * N_XY)))
    attn = contract_rows(every, w_ref[...])
    out_ref[...] = (x_ref[...].astype(jnp.float32) + attn + act_ref[...]).astype(jnp.bfloat16)


def share_kernel(shares_ref, out_ref):
    total = jnp.zeros(shares_ref.shape[1:], jnp.float32)
    for i in range(N_XY):
        total += shares_ref[i].astype(jnp.float32)
    for h in range(N_SEQ):
        out_ref[h] = total.astype(jnp.bfloat16)


def finish_kernel(every_ref, w_ref, m_ref, gain_ref, qkv_ref, out_ref, msg_ref, gain_out_ref):
    rows = msg_ref.shape[0]
    hd = N_SEQ * HEAD_DIM
    nodes = N_SEQ * CHUNK
    gain_sum = jnp.zeros((rows, BLOCK), jnp.float32)
    low = slice(0, HEAD_DIM)
    high = slice(HEAD_DIM, 2 * HEAD_DIM)
    for t, (band, half) in enumerate(((0, low), (0, high), (1, low))):
        for p in range(N_SEQ // 2):
            pieces = [every_ref[h, band * rows : (band + 1) * rows, half] for h in (2 * p, 2 * p + 1)]
            block = jnp.concatenate(pieces, axis=1).astype(jnp.float32) * (1.0 / nodes)
            columns = slice(t * hd + p * BLOCK, t * hd + (p + 1) * BLOCK)
            qkv_ref[:, columns] = block
            gain_sum += block * w_ref[:, columns].astype(jnp.float32)
    total = jnp.zeros((every_ref.shape[1] - 3 * rows, BLOCK), jnp.float32)
    for h in range(N_SEQ):
        columns = slice(h * BLOCK, (h + 1) * BLOCK)
        block = every_ref[h, 2 * rows : 3 * rows].astype(jnp.float32) * (1.0 / nodes)
        msg_ref[:, columns] = block
        gain_sum += block * m_ref[:, columns].astype(jnp.float32)
        total += every_ref[h, 3 * rows :].astype(jnp.float32)
    half_rows = out_ref.shape[0]
    for t in range(N_SEQ):
        out_ref[:, t * BLOCK : (t + 1) * BLOCK] = total[t * half_rows : (t + 1) * half_rows] * (1.0 / nodes)
    gain_out_ref[...] = jnp.sum(gain_sum.T, axis=0, keepdims=True) / gain_ref[...]


def input_grad_kernel(*refs):
    stack_ref, w_ref, d_msg_ref, w_msg_ref, x_ref, grad_ref, gain_ref, out_ref = refs
    parts = [
        stack_ref[h, t * HEAD_DIM : (t + 1) * HEAD_DIM] for t in range(3) for h in range(N_SEQ)
    ]
    d_norm = matmul(w_ref[...], jnp.concatenate(parts, axis=0)).T
    d_norm += contract_cols(d_msg_ref[...], w_msg_ref[...])
    wide = x_ref[...].astype(jnp.float32)
    inv_rms = unit_factor(wide, -1)
    x_hat = wide * inv_rms
    scaled = d_norm * gain_ref[...]
    d_feat = inv_rms * (scaled - x_hat * jnp.mean(scaled * x_hat, axis=-1, keepdims=True))
    out_ref[...] = (grad_ref[...].astype(jnp.float32) + d_feat).astype(jnp.bfloat16)


def after(value, *others):
    return lax.optimization_barrier((value,) + others)[0]


def exchange(array, axis):
    return lax.all_to_all(array, axis, split_axis=0, concat_axis=0, tiled=True)


def shift(array, distance):
    return lax.ppermute(array, "z", [(i, (i + distance) % N_SEQ) for i in range(N_SEQ)])


def up(array):
    return shift(array, 1)


def down(array):
    return shift(array, -1)


def sum_over_cores(keep, give):
    got = lax.ppermute(give, "c", [(0, 1), (1, 0)])
    return (keep.astype(jnp.float32) + got.astype(jnp.float32)).astype(jnp.bfloat16)


def sum_over_chips(pair):
    return jnp.sum(exchange(pair, ("x", "y")).astype(jnp.float32), axis=0)


def on_device(
    features, out_grad, norm_gain, w_qkv, w_out, w_msg, block_ids, block_counts, edge_tiles
):
    node_rows, width = features.shape
    hd = w_out.shape[0]
    nodes = N_SEQ * node_rows
    bf16, f32 = jnp.bfloat16, jnp.float32
    z = lax.axis_index("z")
    core = lax.axis_index("c")
    place = jnp.stack([z, core]).astype(jnp.int32)
    gain = norm_gain.reshape(1, width)
    wide_shape = ((node_rows, width), f32)
    low_shape = ((node_rows, width), bf16)

    n_a = normalize_half(features, gain, 0)
    a_up, a_down = [n_a, up(n_a)], [n_a, down(n_a)]
    n_b = normalize_half(features, gain, 1)
    b_up, b_down = [n_b, up(n_b)], [n_b, down(n_b)]
    w_head = pick_head(place, w_qkv)
    (d_out,) = call(
        d_out_kernel, "d_out", (((N_SEQ, HEAD_DIM, node_rows), bf16),), (), (out_grad, w_out),
        flops=2 * node_rows * width * hd, moved=2 << 20,
    )
    a_up[1], a_down[1], d_out, w_head = lax.optimization_barrier((a_up[1], a_down[1], d_out, w_head))
    a_up.append(up(a_up[1]))
    a_down.append(down(a_down[1]))
    b_up.append(up(b_up[1]))
    b_down.append(down(b_down[1]))
    a_up.append(up(a_up[2]))
    a_down.append(down(a_down[2]))
    act, to_low, mid, to_high = call(
        message_kernel, "messages", (wide_shape, low_shape, wide_shape, low_shape),
        (place, block_ids, block_counts),
        (after(a_up[1], a_up[3], a_down[3]), b_up[1], n_a, n_b, a_down[1], b_down[1], w_msg, edge_tiles, out_grad),
        [pltpu.VMEM((6, BLOCK, width), bf16), pltpu.VMEM((6, BLOCK, width), f32)],
        flops=8 * node_rows * width * width, exps=node_rows * width, moved=8 << 20,
    )
    b_up.append(up(b_up[2]))
    b_down.append(down(b_down[2]))
    c4 = [up(a_up[3]), down(b_down[3])]
    *c4, to_low, to_high, d_out = lax.optimization_barrier((*c4, to_low, to_high, d_out))
    above, below = down(to_low), up(to_high)
    pairs = list(zip(a_up, b_up)) + [c4] + list(zip(a_down, b_down))[:0:-1]
    chunks = tuple(half for pair in pairs for half in pair)
    d_heads = exchange(d_out, "z")

    held = pltpu.VMEM((N_SEQ, CHUNK, width), bf16)
    lanes_in = ((N_SEQ, CHUNK, 2 * HEAD_DIM), bf16)
    turned = ((N_SEQ, HEAD_DIM, CHUNK), bf16)
    heads, *saved = call(
        forward_kernel, "attend_forward",
        (turned, lanes_in, turned, turned, ((N_SEQ, 2 * HEAD_DIM, CHUNK), bf16), ((N_SEQ, 8, CHUNK), f32)),
        (place,), (w_head,),
        [pltpu.VMEM((N_SEQ, HEAD_DIM + ONES, CHUNK), bf16), held, pltpu.SemaphoreType.DMA((16,))],
        flops=12 * nodes * nodes * HEAD_DIM, exps=nodes * nodes, moved=8 << 20, far=chunks,
    )
    send, d_msg = call(
        merge_kernel, "merge", (((N_SEQ, HEAD_DIM + BLOCK, CHUNK), bf16), low_shape), (),
        (heads, mid, above, below), moved=4 << 20,
    )
    send, d_heads = lax.optimization_barrier((send, d_heads))
    home = exchange(send, "z")

    rows_here = width // (2 * N_XY)
    rows_out = hd // (2 * N_XY)
    (stack,) = call(
        backward_kernel, "attend_backward", (((N_SEQ, 3 * HEAD_DIM, CHUNK), bf16),),
        (place,), (heads, *saved, d_heads),
        [pltpu.VMEM((N_SEQ, CHUNK, 2 * HEAD_DIM), f32), pltpu.VMEM((N_SEQ, HEAD_DIM, CHUNK), f32)],
        flops=24 * nodes * nodes * HEAD_DIM, exps=nodes * nodes, moved=4 << 20,
    )
    stack, home = lax.optimization_barrier((stack, home))
    stack_home = exchange(stack, "z")

    all_rows = 3 * rows_here + rows_out * width // BLOCK
    part = ((N_XY, all_rows, BLOCK), bf16)
    block_result_array, keep, give = call(
        result_kernel, "result", (low_shape, part, part), (place,),
        (home, stack, w_out, out_grad, features, act),
        [
            pltpu.VMEM((3 * BLOCK, width), f32), pltpu.VMEM((width, 3 * BLOCK), f32),
            pltpu.VMEM((hd, width), f32), held, pltpu.SemaphoreType.DMA((16,)),
        ],
        flops=8 * node_rows * width * width, moved=10 << 20, far=chunks,
    )
    got = lax.ppermute(give, "c", [(0, 1), (1, 0)])
    pair = (keep.astype(f32) + got.astype(f32)).astype(bf16)
    pair, stack_home = lax.optimization_barrier((pair, stack_home))
    shares = exchange(pair, ("x", "y"))
    (mine,) = call(
        share_kernel, "share_sum", (((N_SEQ, all_rows, BLOCK), bf16),), (), (shares,), moved=2 << 20,
    )
    every = exchange(mine, "z")

    (grad_input,) = call(
        input_grad_kernel, "input_grad", (low_shape,), (),
        (after(stack_home, mine), w_qkv, d_msg, w_msg, features, out_grad, gain),
        flops=6 * node_rows * width * hd, moved=8 << 20,
    )

    every, grad_input = lax.optimization_barrier((every, grad_input))
    first = ((lax.axis_index("x") * 4 + lax.axis_index("y")) * 2 + core) * rows_here
    w_rows = lax.dynamic_slice_in_dim(w_qkv, first, rows_here, 0)
    m_rows = lax.dynamic_slice_in_dim(w_msg, first, rows_here, 0)
    gain_rows = lax.dynamic_slice_in_dim(norm_gain, first, rows_here, 0).reshape(1, rows_here)
    grad_qkv, grad_out, grad_msg, grad_gain = call(
        finish_kernel, "finish",
        (((rows_here, 3 * hd), f32), ((rows_out, width), f32), ((rows_here, width), f32), ((1, rows_here), f32)),
        (), (every, w_rows, m_rows, gain_rows), moved=2 << 20,
    )
    return block_result_array, grad_input, grad_gain.reshape(rows_here), grad_qkv, grad_out, grad_msg


def solution(mesh):
    fine = Mesh(mesh.devices.reshape(4, 4, 2, N_SEQ), ("x", "y", "c", "z"))
    dp = ("x", "y", "c")
    rows = ("x", "y", "c", "z")
    return jax.shard_map(
        on_device,
        mesh=fine,
        in_specs=(
            P(rows, None),
            P(rows, None),
            P(),
            P(),
            P(),
            P(),
            P(rows, None),
            P(rows),
            P(rows, None, None, None),
        ),
        out_specs=(
            P(rows, None),
            P(rows, None),
            P(dp),
            P(dp, None),
            P(dp, None),
            P(dp, None),
        ),
        check_vma=False,
    )
```

```python
import jax
import jax.numpy as jnp
from jax import lax
from jax.experimental import pallas as pl
from jax.experimental.pallas import tpu as pltpu
from jax.sharding import Mesh
from jax.sharding import PartitionSpec as P

HEAD_DIM = 64
BLOCK = 128
SLOTS = 4
N_SEQ = 8
N_XY = 16
CHUNK = 256
ONES = 16

exponent_divisor = 32.0
epsilon = 1e-06
SCALE = exponent_divisor / HEAD_DIM


def matmul(left, right):
    return jnp.dot(left, right, preferred_element_type=jnp.float32)


def contract_rows(left, right):
    return lax.dot_general(
        left, right, (((0,), (0,)), ((), ())), preferred_element_type=jnp.float32
    )


def contract_cols(left, right):
    return lax.dot_general(
        left, right, (((1,), (1,)), ((), ())), preferred_element_type=jnp.float32
    )


def unit_factor(wide, axis):
    return lax.rsqrt(jnp.mean(wide * wide, axis=axis, keepdims=True) + epsilon)


def call(kernel, name, out_shape, scalars, arrays, scratch=(), flops=0, exps=0, moved=0, far=()):
    specs = [pl.BlockSpec(memory_space=pltpu.SMEM)] * len(scalars)
    specs += [pl.BlockSpec(memory_space=pltpu.HBM)] * len(far)
    specs += [pl.BlockSpec(memory_space=pltpu.VMEM)] * len(arrays)
    return pl.pallas_call(
        kernel,
        out_shape=tuple(jax.ShapeDtypeStruct(s, t) for s, t in out_shape),
        in_specs=specs,
        out_specs=tuple(pl.BlockSpec(memory_space=pltpu.VMEM) for _ in out_shape),
        scratch_shapes=list(scratch),
        compiler_params=pltpu.CompilerParams(vmem_limit_bytes=62 * 1024 * 1024),
        cost_estimate=pl.CostEstimate(flops=flops, bytes_accessed=moved, transcendentals=exps),
        name=name,
    )(*scalars, *far, *arrays)


def normalize_kernel(x_ref, gain_ref, out_ref):
    wide = x_ref[...].astype(jnp.float32)
    out_ref[...] = (wide * unit_factor(wide, -1) * gain_ref[...]).astype(jnp.bfloat16)


def normalize_half(features, gain, half):
    width = features.shape[1]
    return pl.pallas_call(
        normalize_kernel,
        grid=(1,),
        in_specs=[
            pl.BlockSpec((BLOCK, width), lambda i: (half, 0)),
            pl.BlockSpec((1, width), lambda i: (0, 0)),
        ],
        out_specs=pl.BlockSpec((BLOCK, width), lambda i: (0, 0)),
        out_shape=jax.ShapeDtypeStruct((BLOCK, width), jnp.bfloat16),
        cost_estimate=pl.CostEstimate(flops=0, bytes_accessed=1 << 19, transcendentals=0),
        name="normalize",
    )(features, gain)


def d_out_kernel(grad_ref, w_ref, out_ref):
    turned = contract_cols(w_ref[...], grad_ref[...]).astype(jnp.bfloat16)
    for h in range(N_SEQ):
        out_ref[h] = turned[h * HEAD_DIM : (h + 1) * HEAD_DIM]


def pick_kernel(place_ref, q_ref, k_ref, v_ref, out_ref):
    odd = lax.rem(place_ref[0], 2) == 1

    def halves(ref):
        wide = ref[...].astype(jnp.float32)
        swapped = jnp.concatenate([wide[:, HEAD_DIM:], wide[:, :HEAD_DIM]], axis=1)
        return jnp.where(odd, swapped, wide), jnp.where(odd, wide, swapped)

    left = lax.broadcasted_iota(jnp.int32, q_ref.shape, 1) < HEAD_DIM
    query, _ = halves(q_ref)
    _, keyrow = halves(k_ref)
    val, _ = halves(v_ref)
    out_ref[:, : 2 * HEAD_DIM] = jnp.where(left, query, keyrow).astype(jnp.bfloat16)
    out_ref[:, 2 * HEAD_DIM :] = jnp.where(left, val, 0.0).astype(jnp.bfloat16)


def pick_head(place, w_qkv):
    width, columns = w_qkv.shape
    step = columns // 3 // (2 * HEAD_DIM)

    def block(t):
        return pl.BlockSpec((width, 2 * HEAD_DIM), lambda i, place: (0, t * step + place[0] // 2))

    return pl.pallas_call(
        pick_kernel,
        grid_spec=pltpu.PrefetchScalarGridSpec(
            num_scalar_prefetch=1,
            grid=(1,),
            in_specs=[block(0), block(1), block(2)],
            out_specs=pl.BlockSpec((width, 4 * HEAD_DIM), lambda i, place: (0, 0)),
        ),
        out_shape=jax.ShapeDtypeStruct((width, 4 * HEAD_DIM), jnp.bfloat16),
        cost_estimate=pl.CostEstimate(flops=0, bytes_accessed=4 << 20, transcendentals=0),
        name="pick_head",
    )(place, w_qkv, w_qkv, w_qkv)


def message_kernel(*refs):
    place_ref, ids_ref, counts_ref = refs[:3]
    blocks = refs[3:9]
    w_ref, tiles_ref, grad_ref = refs[9:12]
    act_ref, to_low_ref, mid_ref, to_high_ref, msg, landed = refs[12:]
    z = place_ref[0]
    for t in range(3):
        both = jnp.concatenate([blocks[2 * t][...], blocks[2 * t + 1][...]], axis=0)
        rows = matmul(both, w_ref[...]).astype(jnp.bfloat16)
        msg[2 * t] = rows[:BLOCK]
        msg[2 * t + 1] = rows[BLOCK:]
    landed[...] = jnp.zeros_like(landed)
    for b in range(2):
        spots = []
        live = []
        for s in range(SLOTS):
            spots.append(jnp.clip(ids_ref[b, s] - 2 * (z - 1), 0, 5))
            mask = jnp.where(s < counts_ref[b], 1.0, 0.0)
            live.append(tiles_ref[b, s].astype(jnp.float32) * mask)
        source = jnp.concatenate([msg[spot] for spot in spots], axis=0)
        agg = matmul(jnp.concatenate(live, axis=1).astype(jnp.bfloat16), source)
        sigma = 1.0 / (1.0 + jnp.exp(-agg))
        rows = slice(b * BLOCK, (b + 1) * BLOCK)
        act_ref[rows] = agg * sigma
        d_agg = grad_ref[rows].astype(jnp.float32) * sigma * (1.0 + agg * (1.0 - sigma))
        d_agg = d_agg.astype(jnp.bfloat16)
        for s in range(SLOTS):
            landed[spots[s]] += matmul(live[s].T.astype(jnp.bfloat16), d_agg)
    for b in range(2):
        rows = slice(b * BLOCK, (b + 1) * BLOCK)
        to_low_ref[rows] = landed[b].astype(jnp.bfloat16)
        mid_ref[rows] = landed[2 + b]
        to_high_ref[rows] = landed[4 + b].astype(jnp.bfloat16)


def split_rows(core, source, keep_ref, give_ref, offset=0):
    rows = source.shape[0] // (2 * N_XY)
    for i in range(N_XY):
        for t in range(source.shape[1] // BLOCK):
            spot = slice(offset + t * rows, offset + (t + 1) * rows)
            columns = slice(t * BLOCK, (t + 1) * BLOCK)
            keep_ref[i, spot] = source[pl.ds((2 * i + core) * rows, rows), columns].astype(jnp.bfloat16)
            give_ref[i, spot] = source[pl.ds((2 * i + 1 - core) * rows, rows), columns].astype(
                jnp.bfloat16
            )


def merge_kernel(heads_ref, mid_ref, above_ref, below_ref, send_ref, d_msg_ref):
    total = mid_ref[...] + above_ref[...].astype(jnp.float32) + below_ref[...].astype(jnp.float32)
    d_msg = total.astype(jnp.bfloat16)
    d_msg_ref[...] = d_msg
    for t in range(N_SEQ):
        columns = d_msg[:, t * BLOCK : (t + 1) * BLOCK]
        send_ref[t, :HEAD_DIM] = heads_ref[t]
        send_ref[t, HEAD_DIM:] = jnp.concatenate([columns[:BLOCK], columns[BLOCK:]], axis=1)


def place_of(z, j):
    return lax.rem(z - j + N_SEQ, N_SEQ)


def fetch_chunks(refs, held, sems):
    copies = [
        pltpu.make_async_copy(ref, held.at[i // 2, pl.ds(i % 2 * BLOCK, BLOCK)], sems.at[i])
        for i, ref in enumerate(refs)
    ]
    for copy in copies:
        copy.start()

    def wait(j):
        copies[2 * j].wait()
        copies[2 * j + 1].wait()

    return wait


def forward_kernel(*refs):
    z = refs[0][0]
    w_ref = refs[17]
    out_ref, kv_ref, hq_ref, ku_ref, raw_ref, stats_ref = refs[18:24]
    v_ext, held, sems = refs[24:]
    wait = fetch_chunks(refs[1:17], held, sems)
    for j in range(N_SEQ):
        wait(j)
        proj = matmul(held[j], w_ref[...]).T.astype(jnp.bfloat16)
        raw_ref[j] = proj[: 2 * HEAD_DIM]
        query = proj[:HEAD_DIM].astype(jnp.float32)
        keyrow = proj[HEAD_DIM : 2 * HEAD_DIM].astype(jnp.float32)
        val = proj[2 * HEAD_DIM : 3 * HEAD_DIM]
        q_unit = (query * unit_factor(query, 0)).astype(jnp.bfloat16).astype(jnp.float32) * SCALE
        k_unit = keyrow * unit_factor(keyrow, 0)
        hq_ref[j] = q_unit.astype(jnp.bfloat16)
        ku_ref[j] = k_unit.astype(jnp.bfloat16)
        v_ext[j, :HEAD_DIM] = val
        v_ext[j, HEAD_DIM:] = jnp.ones((ONES, CHUNK), jnp.bfloat16)
        kv_ref[j] = jnp.concatenate([k_unit, val.astype(jnp.float32)], axis=0).T.astype(jnp.bfloat16)

    def step(i, carry):
        query = jnp.concatenate([hq_ref[i], jnp.zeros_like(hq_ref[i])], axis=0)
        keys = kv_ref[...].reshape(N_SEQ * CHUNK, 2 * HEAD_DIM)
        exps = jnp.exp(matmul(keys, query)).astype(jnp.bfloat16)
        out = matmul(jnp.concatenate([v_ext[j] for j in range(N_SEQ)], axis=1), exps)
        inverse = 1.0 / out[HEAD_DIM : HEAD_DIM + 1]
        stats_ref[i, 0:1] = inverse
        head_out = (out[:HEAD_DIM] * inverse).astype(jnp.bfloat16)
        out_ref[place_of(z, i)] = head_out
        return carry

    lax.fori_loop(0, N_SEQ, step, 0)


def backward_kernel(*refs):
    z = refs[0][0]
    head_ref, kv_ref, hq_ref, ku_ref, raw_ref, stats_ref, d_ref = refs[1:8]
    stack_ref, sums, dqt = refs[8:]
    sums[...] = jnp.zeros_like(sums)

    def step(i, carry):
        zero = jnp.zeros_like(hq_ref[i])
        query = jnp.concatenate([hq_ref[i], zero], axis=0)
        d_out = d_ref[place_of(z, i)]
        d_wide = d_out.astype(jnp.float32)
        d_head = jnp.concatenate([zero, d_out], axis=0)
        rows = jnp.concatenate([hq_ref[i].astype(jnp.float32), d_wide], axis=0).T
        left = lax.broadcasted_iota(jnp.int32, rows.shape, 1) < HEAD_DIM
        rhs = jnp.concatenate([jnp.where(left, 0.0, rows), jnp.where(left, rows, 0.0)], axis=0)
        rhs = rhs.astype(jnp.bfloat16)
        inverse = stats_ref[i, 0:1]
        row_dot = jnp.sum(head_ref[place_of(z, i)].astype(jnp.float32) * d_wide, axis=0, keepdims=True)
        keys = kv_ref[...].reshape(N_SEQ * CHUNK, 2 * HEAD_DIM)
        prob = jnp.exp(matmul(keys, query)) * inverse
        d_scores = (prob * (matmul(keys, d_head) - row_dot)).astype(jnp.bfloat16)
        d_qunit = matmul(jnp.concatenate([ku_ref[j] for j in range(N_SEQ)], axis=1), d_scores)
        both = jnp.concatenate([prob.astype(jnp.bfloat16), d_scores], axis=1)
        sums[...] += matmul(both, rhs).reshape(N_SEQ, CHUNK, 2 * HEAD_DIM)
        dqt[i] = d_qunit * SCALE
        return carry

    lax.fori_loop(0, N_SEQ, step, 0)
    for j in range(N_SEQ):
        turned = sums[j].T
        pieces = []
        for t, d_unit in enumerate((dqt[j], turned[:HEAD_DIM])):
            wide = raw_ref[j, t * HEAD_DIM : (t + 1) * HEAD_DIM].astype(jnp.float32)
            factor = unit_factor(wide, 0)
            mean = jnp.mean(d_unit * wide, axis=0, keepdims=True)
            pieces.append(factor * d_unit - factor * factor * factor * wide * mean)
        stacked = jnp.concatenate(pieces + [turned[HEAD_DIM:]], axis=0).astype(jnp.bfloat16)
        stack_ref[place_of(z, j)] = stacked


def result_kernel(*refs):
    place_ref = refs[0]
    home_ref, stack_ref, w_ref, grad_ref, x_ref, act_ref = refs[17:23]
    out_ref, keep_ref, give_ref, grad_t, grad_node, grad_out, held, sems = refs[23:]
    wait = fetch_chunks(refs[1:17], held, sems)
    z = place_ref[0]
    every = jnp.concatenate([home_ref[h, :HEAD_DIM] for h in range(N_SEQ)], axis=0)
    grad_out[...] = matmul(every, grad_ref[...])
    for j in range(N_SEQ):
        folded = home_ref[place_of(z, j), HEAD_DIM:].astype(jnp.float32)
        columns = jnp.concatenate([folded[:, :BLOCK].T, folded[:, BLOCK:].T], axis=1)
        d_head = stack_ref[place_of(z, j)]
        pad = jnp.zeros((HEAD_DIM, CHUNK), jnp.bfloat16)
        both = jnp.concatenate([d_head, pad, columns.astype(jnp.bfloat16)], axis=0)
        wait(j)
        term = matmul(both, held[j])
        if j == 0:
            grad_t[...] = term
        else:
            grad_t[...] += term
    grad_node[...] = grad_t[...].T
    split_rows(place_ref[1], grad_node, keep_ref, give_ref)
    split_rows(place_ref[1], grad_out, keep_ref, give_ref, 3 * (grad_node.shape[0] // (2 * N_XY)))
    attn = contract_rows(every, w_ref[...])
    out_ref[...] = (x_ref[...].astype(jnp.float32) + attn + act_ref[...]).astype(jnp.bfloat16)


def share_kernel(shares_ref, out_ref):
    total = jnp.zeros(shares_ref.shape[1:], jnp.float32)
    for i in range(N_XY):
        total += shares_ref[i].astype(jnp.float32)
    for h in range(N_SEQ):
        out_ref[h] = total.astype(jnp.bfloat16)


def finish_kernel(every_ref, w_ref, m_ref, gain_ref, qkv_ref, out_ref, msg_ref, gain_out_ref):
    rows = msg_ref.shape[0]
    hd = N_SEQ * HEAD_DIM
    nodes = N_SEQ * CHUNK
    gain_sum = jnp.zeros((rows, BLOCK), jnp.float32)
    low = slice(0, HEAD_DIM)
    high = slice(HEAD_DIM, 2 * HEAD_DIM)
    for t, (band, half) in enumerate(((0, low), (0, high), (1, low))):
        for p in range(N_SEQ // 2):
            pieces = [every_ref[h, band * rows : (band + 1) * rows, half] for h in (2 * p, 2 * p + 1)]
            block = jnp.concatenate(pieces, axis=1).astype(jnp.float32) * (1.0 / nodes)
            columns = slice(t * hd + p * BLOCK, t * hd + (p + 1) * BLOCK)
            qkv_ref[:, columns] = block
            gain_sum += block * w_ref[:, columns].astype(jnp.float32)
    total = jnp.zeros((every_ref.shape[1] - 3 * rows, BLOCK), jnp.float32)
    for h in range(N_SEQ):
        columns = slice(h * BLOCK, (h + 1) * BLOCK)
        block = every_ref[h, 2 * rows : 3 * rows].astype(jnp.float32) * (1.0 / nodes)
        msg_ref[:, columns] = block
        gain_sum += block * m_ref[:, columns].astype(jnp.float32)
        total += every_ref[h, 3 * rows :].astype(jnp.float32)
    half_rows = out_ref.shape[0]
    for t in range(N_SEQ):
        out_ref[:, t * BLOCK : (t + 1) * BLOCK] = total[t * half_rows : (t + 1) * half_rows] * (1.0 / nodes)
    gain_out_ref[...] = jnp.sum(gain_sum.T, axis=0, keepdims=True) / gain_ref[...]


def input_grad_kernel(*refs):
    stack_ref, w_ref, d_msg_ref, w_msg_ref, x_ref, grad_ref, gain_ref, out_ref = refs
    parts = [
        stack_ref[h, t * HEAD_DIM : (t + 1) * HEAD_DIM] for t in range(3) for h in range(N_SEQ)
    ]
    d_norm = matmul(w_ref[...], jnp.concatenate(parts, axis=0)).T
    d_norm += contract_cols(d_msg_ref[...], w_msg_ref[...])
    wide = x_ref[...].astype(jnp.float32)
    inv_rms = unit_factor(wide, -1)
    x_hat = wide * inv_rms
    scaled = d_norm * gain_ref[...]
    d_feat = inv_rms * (scaled - x_hat * jnp.mean(scaled * x_hat, axis=-1, keepdims=True))
    out_ref[...] = (grad_ref[...].astype(jnp.float32) + d_feat).astype(jnp.bfloat16)


def after(value, *others):
    return lax.optimization_barrier((value,) + others)[0]


def exchange(array, axis):
    return lax.all_to_all(array, axis, split_axis=0, concat_axis=0, tiled=True)


def shift(array, distance):
    return lax.ppermute(array, "z", [(i, (i + distance) % N_SEQ) for i in range(N_SEQ)])


def up(array):
    return shift(array, 1)


def down(array):
    return shift(array, -1)


def sum_over_cores(keep, give):
    got = lax.ppermute(give, "c", [(0, 1), (1, 0)])
    return (keep.astype(jnp.float32) + got.astype(jnp.float32)).astype(jnp.bfloat16)


def sum_over_chips(pair):
    return jnp.sum(exchange(pair, ("x", "y")).astype(jnp.float32), axis=0)


def on_device(
    features, out_grad, norm_gain, w_qkv, w_out, w_msg, block_ids, block_counts, edge_tiles
):
    node_rows, width = features.shape
    hd = w_out.shape[0]
    nodes = N_SEQ * node_rows
    bf16, f32 = jnp.bfloat16, jnp.float32
    z = lax.axis_index("z")
    core = lax.axis_index("c")
    place = jnp.stack([z, core]).astype(jnp.int32)
    gain = norm_gain.reshape(1, width)
    wide_shape = ((node_rows, width), f32)
    low_shape = ((node_rows, width), bf16)

    n_a = normalize_half(features, gain, 0)
    a_up, a_down = [n_a, up(n_a)], [n_a, down(n_a)]
    n_b = normalize_half(features, gain, 1)
    b_up, b_down = [n_b, up(n_b)], [n_b, down(n_b)]
    w_head = pick_head(place, w_qkv)
    (d_out,) = call(
        d_out_kernel, "d_out", (((N_SEQ, HEAD_DIM, node_rows), bf16),), (), (out_grad, w_out),
        flops=2 * node_rows * width * hd, moved=2 << 20,
    )
    a_up[1], a_down[1], d_out, w_head = lax.optimization_barrier((a_up[1], a_down[1], d_out, w_head))
    a_up.append(up(a_up[1]))
    a_down.append(down(a_down[1]))
    b_up.append(up(b_up[1]))
    b_down.append(down(b_down[1]))
    a_up.append(up(a_up[2]))
    a_down.append(down(a_down[2]))
    act, to_low, mid, to_high = call(
        message_kernel, "messages", (wide_shape, low_shape, wide_shape, low_shape),
        (place, block_ids, block_counts),
        (after(a_up[1], a_up[2], a_down[2]), b_up[1], n_a, n_b, a_down[1], b_down[1], w_msg, edge_tiles, out_grad),
        [pltpu.VMEM((6, BLOCK, width), bf16), pltpu.VMEM((6, BLOCK, width), f32)],
        flops=8 * node_rows * width * width, exps=node_rows * width, moved=8 << 20,
    )
    d_heads = exchange(after(d_out, a_up[3], a_down[3]), "z")
    b_up.append(up(b_up[2]))
    b_down.append(down(b_down[2]))
    c4 = [up(a_up[3]), down(b_down[3])]
    *c4, to_low, to_high = lax.optimization_barrier((*c4, to_low, to_high))
    above, below = down(to_low), up(to_high)
    pairs = list(zip(a_up, b_up)) + [c4] + list(zip(a_down, b_down))[:0:-1]
    chunks = tuple(half for pair in pairs for half in pair)

    held = pltpu.VMEM((N_SEQ, CHUNK, width), bf16)
    lanes_in = ((N_SEQ, CHUNK, 2 * HEAD_DIM), bf16)
    turned = ((N_SEQ, HEAD_DIM, CHUNK), bf16)
    heads, *saved = call(
        forward_kernel, "attend_forward",
        (turned, lanes_in, turned, turned, ((N_SEQ, 2 * HEAD_DIM, CHUNK), bf16), ((N_SEQ, 8, CHUNK), f32)),
        (place,), (w_head,),
        [pltpu.VMEM((N_SEQ, HEAD_DIM + ONES, CHUNK), bf16), held, pltpu.SemaphoreType.DMA((16,))],
        flops=12 * nodes * nodes * HEAD_DIM, exps=nodes * nodes, moved=8 << 20, far=chunks,
    )
    send, d_msg = call(
        merge_kernel, "merge", (((N_SEQ, HEAD_DIM + BLOCK, CHUNK), bf16), low_shape), (),
        (heads, mid, above, below), moved=4 << 20,
    )
    send, d_heads = lax.optimization_barrier((send, d_heads))
    home = exchange(send, "z")

    rows_here = width // (2 * N_XY)
    rows_out = hd // (2 * N_XY)
    (stack,) = call(
        backward_kernel, "attend_backward", (((N_SEQ, 3 * HEAD_DIM, CHUNK), bf16),),
        (place,), (heads, *saved, d_heads),
        [pltpu.VMEM((N_SEQ, CHUNK, 2 * HEAD_DIM), f32), pltpu.VMEM((N_SEQ, HEAD_DIM, CHUNK), f32)],
        flops=24 * nodes * nodes * HEAD_DIM, exps=nodes * nodes, moved=4 << 20,
    )
    stack, home = lax.optimization_barrier((stack, home))
    stack_home = exchange(stack, "z")

    all_rows = 3 * rows_here + rows_out * width // BLOCK
    part = ((N_XY, all_rows, BLOCK), bf16)
    block_result_array, keep, give = call(
        result_kernel, "result", (low_shape, part, part), (place,),
        (home, stack, w_out, out_grad, features, act),
        [
            pltpu.VMEM((3 * BLOCK, width), f32), pltpu.VMEM((width, 3 * BLOCK), f32),
            pltpu.VMEM((hd, width), f32), held, pltpu.SemaphoreType.DMA((16,)),
        ],
        flops=8 * node_rows * width * width, moved=10 << 20, far=chunks,
    )
    got = lax.ppermute(give, "c", [(0, 1), (1, 0)])
    pair = (keep.astype(f32) + got.astype(f32)).astype(bf16)
    pair, stack_home = lax.optimization_barrier((pair, stack_home))
    shares = exchange(pair, ("x", "y"))
    (mine,) = call(
        share_kernel, "share_sum", (((N_SEQ, all_rows, BLOCK), bf16),), (), (shares,), moved=2 << 20,
    )
    every = exchange(mine, "z")

    (grad_input,) = call(
        input_grad_kernel, "input_grad", (low_shape,), (),
        (after(stack_home, mine), w_qkv, d_msg, w_msg, features, out_grad, gain),
        flops=6 * node_rows * width * hd, moved=8 << 20,
    )

    every, grad_input = lax.optimization_barrier((every, grad_input))
    first = ((lax.axis_index("x") * 4 + lax.axis_index("y")) * 2 + core) * rows_here
    w_rows = lax.dynamic_slice_in_dim(w_qkv, first, rows_here, 0)
    m_rows = lax.dynamic_slice_in_dim(w_msg, first, rows_here, 0)
    gain_rows = lax.dynamic_slice_in_dim(norm_gain, first, rows_here, 0).reshape(1, rows_here)
    grad_qkv, grad_out, grad_msg, grad_gain = call(
        finish_kernel, "finish",
        (((rows_here, 3 * hd), f32), ((rows_out, width), f32), ((rows_here, width), f32), ((1, rows_here), f32)),
        (), (every, w_rows, m_rows, gain_rows), moved=2 << 20,
    )
    return block_result_array, grad_input, grad_gain.reshape(rows_here), grad_qkv, grad_out, grad_msg


def solution(mesh):
    fine = Mesh(mesh.devices.reshape(4, 4, 2, N_SEQ), ("x", "y", "c", "z"))
    dp = ("x", "y", "c")
    rows = ("x", "y", "c", "z")
    return jax.shard_map(
        on_device,
        mesh=fine,
        in_specs=(
            P(rows, None),
            P(rows, None),
            P(),
            P(),
            P(),
            P(),
            P(rows, None),
            P(rows),
            P(rows, None, None, None),
        ),
        out_specs=(
            P(rows, None),
            P(rows, None),
            P(dp),
            P(dp, None),
            P(dp, None),
            P(dp, None),
        ),
        check_vma=False,
    )
```

```python
import jax
import jax.numpy as jnp
from jax import lax
from jax.experimental import pallas as pl
from jax.experimental.pallas import tpu as pltpu
from jax.sharding import Mesh
from jax.sharding import PartitionSpec as P

HEAD_DIM = 64
BLOCK = 128
SLOTS = 4
N_SEQ = 8
N_XY = 16
CHUNK = 256
ONES = 16

exponent_divisor = 32.0
epsilon = 1e-06
SCALE = exponent_divisor / HEAD_DIM


def matmul(left, right):
    return jnp.dot(left, right, preferred_element_type=jnp.float32)


def contract_rows(left, right):
    return lax.dot_general(
        left, right, (((0,), (0,)), ((), ())), preferred_element_type=jnp.float32
    )


def contract_cols(left, right):
    return lax.dot_general(
        left, right, (((1,), (1,)), ((), ())), preferred_element_type=jnp.float32
    )


def unit_factor(wide, axis):
    return lax.rsqrt(jnp.mean(wide * wide, axis=axis, keepdims=True) + epsilon)


def call(kernel, name, out_shape, scalars, arrays, scratch=(), flops=0, exps=0, moved=0, far=()):
    specs = [pl.BlockSpec(memory_space=pltpu.SMEM)] * len(scalars)
    specs += [pl.BlockSpec(memory_space=pltpu.HBM)] * len(far)
    specs += [pl.BlockSpec(memory_space=pltpu.VMEM)] * len(arrays)
    return pl.pallas_call(
        kernel,
        out_shape=tuple(jax.ShapeDtypeStruct(s, t) for s, t in out_shape),
        in_specs=specs,
        out_specs=tuple(pl.BlockSpec(memory_space=pltpu.VMEM) for _ in out_shape),
        scratch_shapes=list(scratch),
        compiler_params=pltpu.CompilerParams(vmem_limit_bytes=63 * 1024 * 1024),
        cost_estimate=pl.CostEstimate(flops=flops, bytes_accessed=moved, transcendentals=exps),
        name=name,
    )(*scalars, *far, *arrays)


def normalize_kernel(x_ref, gain_ref, out_ref):
    wide = x_ref[...].astype(jnp.float32)
    out_ref[...] = (wide * unit_factor(wide, -1) * gain_ref[...]).astype(jnp.bfloat16)


def normalize_half(features, gain, half):
    width = features.shape[1]
    return pl.pallas_call(
        normalize_kernel,
        grid=(1,),
        in_specs=[
            pl.BlockSpec((BLOCK, width), lambda i: (half, 0)),
            pl.BlockSpec((1, width), lambda i: (0, 0)),
        ],
        out_specs=pl.BlockSpec((BLOCK, width), lambda i: (0, 0)),
        out_shape=jax.ShapeDtypeStruct((BLOCK, width), jnp.bfloat16),
        cost_estimate=pl.CostEstimate(flops=0, bytes_accessed=1 << 19, transcendentals=0),
        name="normalize",
    )(features, gain)


def d_out_kernel(grad_ref, w_ref, out_ref):
    turned = contract_cols(w_ref[...], grad_ref[...]).astype(jnp.bfloat16)
    for h in range(N_SEQ):
        out_ref[h] = turned[h * HEAD_DIM : (h + 1) * HEAD_DIM]


def pick_kernel(place_ref, q_ref, k_ref, v_ref, out_ref):
    odd = lax.rem(place_ref[0], 2) == 1

    def halves(ref):
        wide = ref[...].astype(jnp.float32)
        swapped = jnp.concatenate([wide[:, HEAD_DIM:], wide[:, :HEAD_DIM]], axis=1)
        return jnp.where(odd, swapped, wide), jnp.where(odd, wide, swapped)

    left = lax.broadcasted_iota(jnp.int32, q_ref.shape, 1) < HEAD_DIM
    query, _ = halves(q_ref)
    _, keyrow = halves(k_ref)
    val, _ = halves(v_ref)
    out_ref[:, : 2 * HEAD_DIM] = jnp.where(left, query, keyrow).astype(jnp.bfloat16)
    out_ref[:, 2 * HEAD_DIM :] = jnp.where(left, val, 0.0).astype(jnp.bfloat16)


def pick_head(place, w_qkv):
    width, columns = w_qkv.shape
    step = columns // 3 // (2 * HEAD_DIM)

    def block(t):
        return pl.BlockSpec((width, 2 * HEAD_DIM), lambda i, place: (0, t * step + place[0] // 2))

    return pl.pallas_call(
        pick_kernel,
        grid_spec=pltpu.PrefetchScalarGridSpec(
            num_scalar_prefetch=1,
            grid=(1,),
            in_specs=[block(0), block(1), block(2)],
            out_specs=pl.BlockSpec((width, 4 * HEAD_DIM), lambda i, place: (0, 0)),
        ),
        out_shape=jax.ShapeDtypeStruct((width, 4 * HEAD_DIM), jnp.bfloat16),
        cost_estimate=pl.CostEstimate(flops=0, bytes_accessed=4 << 20, transcendentals=0),
        name="pick_head",
    )(place, w_qkv, w_qkv, w_qkv)


def message_kernel(*refs):
    place_ref, ids_ref, counts_ref = refs[:3]
    blocks = refs[3:9]
    w_ref, tiles_ref, grad_ref = refs[9:12]
    act_ref, to_low_ref, mid_ref, to_high_ref, msg, landed = refs[12:]
    z = place_ref[0]
    for t in range(3):
        both = jnp.concatenate([blocks[2 * t][...], blocks[2 * t + 1][...]], axis=0)
        rows = matmul(both, w_ref[...]).astype(jnp.bfloat16)
        msg[2 * t] = rows[:BLOCK]
        msg[2 * t + 1] = rows[BLOCK:]
    landed[...] = jnp.zeros_like(landed)
    for b in range(2):
        spots = []
        live = []
        for s in range(SLOTS):
            spots.append(jnp.clip(ids_ref[b, s] - 2 * (z - 1), 0, 5))
            mask = jnp.where(s < counts_ref[b], 1.0, 0.0)
            live.append(tiles_ref[b, s].astype(jnp.float32) * mask)
        source = jnp.concatenate([msg[spot] for spot in spots], axis=0)
        agg = matmul(jnp.concatenate(live, axis=1).astype(jnp.bfloat16), source)
        sigma = 1.0 / (1.0 + jnp.exp(-agg))
        rows = slice(b * BLOCK, (b + 1) * BLOCK)
        act_ref[rows] = agg * sigma
        d_agg = grad_ref[rows].astype(jnp.float32) * sigma * (1.0 + agg * (1.0 - sigma))
        d_agg = d_agg.astype(jnp.bfloat16)
        for s in range(SLOTS):
            landed[spots[s]] += matmul(live[s].T.astype(jnp.bfloat16), d_agg)
    for b in range(2):
        rows = slice(b * BLOCK, (b + 1) * BLOCK)
        to_low_ref[rows] = landed[b].astype(jnp.bfloat16)
        mid_ref[rows] = landed[2 + b]
        to_high_ref[rows] = landed[4 + b].astype(jnp.bfloat16)


def split_rows(core, source, keep_ref, give_ref, offset=0):
    rows = source.shape[0] // (2 * N_XY)
    for i in range(N_XY):
        for t in range(source.shape[1] // BLOCK):
            spot = slice(offset + t * rows, offset + (t + 1) * rows)
            columns = slice(t * BLOCK, (t + 1) * BLOCK)
            keep_ref[i, spot] = source[pl.ds((2 * i + core) * rows, rows), columns].astype(jnp.bfloat16)
            give_ref[i, spot] = source[pl.ds((2 * i + 1 - core) * rows, rows), columns].astype(
                jnp.bfloat16
            )


def merge_kernel(heads_ref, mid_ref, above_ref, below_ref, send_ref, d_msg_ref):
    total = mid_ref[...] + above_ref[...].astype(jnp.float32) + below_ref[...].astype(jnp.float32)
    d_msg = total.astype(jnp.bfloat16)
    d_msg_ref[...] = d_msg
    for t in range(N_SEQ):
        columns = d_msg[:, t * BLOCK : (t + 1) * BLOCK]
        send_ref[t, :HEAD_DIM] = heads_ref[t]
        send_ref[t, HEAD_DIM:] = jnp.concatenate([columns[:BLOCK], columns[BLOCK:]], axis=1)


def place_of(z, j):
    return lax.rem(z - j + N_SEQ, N_SEQ)


def fetch_chunks(refs, held, sems):
    copies = [
        pltpu.make_async_copy(ref, held.at[i // 2, pl.ds(i % 2 * BLOCK, BLOCK)], sems.at[i])
        for i, ref in enumerate(refs)
    ]
    for copy in copies:
        copy.start()

    def wait(j):
        copies[2 * j].wait()
        copies[2 * j + 1].wait()

    return wait


def forward_kernel(*refs):
    z = refs[0][0]
    w_ref = refs[17]
    out_ref, kv_ref, hq_ref, ku_ref, raw_ref, stats_ref = refs[18:24]
    v_ext, held, sems = refs[24:]
    wait = fetch_chunks(refs[1:17], held, sems)
    for j in range(N_SEQ):
        wait(j)
        proj = matmul(held[j], w_ref[...]).T.astype(jnp.bfloat16)
        raw_ref[j] = proj[: 2 * HEAD_DIM]
        query = proj[:HEAD_DIM].astype(jnp.float32)
        keyrow = proj[HEAD_DIM : 2 * HEAD_DIM].astype(jnp.float32)
        val = proj[2 * HEAD_DIM : 3 * HEAD_DIM]
        q_unit = (query * unit_factor(query, 0)).astype(jnp.bfloat16).astype(jnp.float32) * SCALE
        k_unit = keyrow * unit_factor(keyrow, 0)
        hq_ref[j] = q_unit.astype(jnp.bfloat16)
        ku_ref[j] = k_unit.astype(jnp.bfloat16)
        v_ext[j, :HEAD_DIM] = val
        v_ext[j, HEAD_DIM:] = jnp.ones((ONES, CHUNK), jnp.bfloat16)
        kv_ref[j] = jnp.concatenate([k_unit, val.astype(jnp.float32)], axis=0).T.astype(jnp.bfloat16)

    def step(i, carry):
        query = jnp.concatenate([hq_ref[i], jnp.zeros_like(hq_ref[i])], axis=0)
        keys = kv_ref[...].reshape(N_SEQ * CHUNK, 2 * HEAD_DIM)
        exps = jnp.exp(matmul(keys, query)).astype(jnp.bfloat16)
        out = matmul(jnp.concatenate([v_ext[j] for j in range(N_SEQ)], axis=1), exps)
        inverse = 1.0 / out[HEAD_DIM : HEAD_DIM + 1]
        stats_ref[i, 0:1] = inverse
        head_out = (out[:HEAD_DIM] * inverse).astype(jnp.bfloat16)
        out_ref[place_of(z, i)] = head_out
        return carry

    lax.fori_loop(0, N_SEQ, step, 0)


def backward_kernel(*refs):
    z = refs[0][0]
    head_ref, kv_ref, hq_ref, ku_ref, raw_ref, stats_ref, d_ref = refs[1:8]
    stack_ref, sums, dqt = refs[8:]
    sums[...] = jnp.zeros_like(sums)

    def step(i, carry):
        zero = jnp.zeros_like(hq_ref[i])
        query = jnp.concatenate([hq_ref[i], zero], axis=0)
        d_out = d_ref[place_of(z, i)]
        d_wide = d_out.astype(jnp.float32)
        d_head = jnp.concatenate([zero, d_out], axis=0)
        rows = jnp.concatenate([hq_ref[i].astype(jnp.float32), d_wide], axis=0).T
        left = lax.broadcasted_iota(jnp.int32, rows.shape, 1) < HEAD_DIM
        rhs = jnp.concatenate([jnp.where(left, 0.0, rows), jnp.where(left, rows, 0.0)], axis=0)
        rhs = rhs.astype(jnp.bfloat16)
        inverse = stats_ref[i, 0:1]
        row_dot = jnp.sum(head_ref[place_of(z, i)].astype(jnp.float32) * d_wide, axis=0, keepdims=True)
        keys = kv_ref[...].reshape(N_SEQ * CHUNK, 2 * HEAD_DIM)
        prob = jnp.exp(matmul(keys, query)) * inverse
        d_scores = (prob * (matmul(keys, d_head) - row_dot)).astype(jnp.bfloat16)
        d_qunit = matmul(jnp.concatenate([ku_ref[j] for j in range(N_SEQ)], axis=1), d_scores)
        both = jnp.concatenate([prob.astype(jnp.bfloat16), d_scores], axis=1)
        sums[...] += matmul(both, rhs).reshape(N_SEQ, CHUNK, 2 * HEAD_DIM)
        dqt[i] = d_qunit * SCALE
        return carry

    lax.fori_loop(0, N_SEQ, step, 0)
    for j in range(N_SEQ):
        turned = sums[j].T
        pieces = []
        for t, d_unit in enumerate((dqt[j], turned[:HEAD_DIM])):
            wide = raw_ref[j, t * HEAD_DIM : (t + 1) * HEAD_DIM].astype(jnp.float32)
            factor = unit_factor(wide, 0)
            mean = jnp.mean(d_unit * wide, axis=0, keepdims=True)
            pieces.append(factor * d_unit - factor * factor * factor * wide * mean)
        stacked = jnp.concatenate(pieces + [turned[HEAD_DIM:]], axis=0).astype(jnp.bfloat16)
        stack_ref[place_of(z, j)] = stacked


def result_kernel(*refs):
    place_ref = refs[0]
    home_ref, stack_ref, w_ref, grad_ref, x_ref, act_ref = refs[17:23]
    out_ref, keep_ref, give_ref, grad_t, grad_node, grad_out, held, sems = refs[23:]
    wait = fetch_chunks(refs[1:17], held, sems)
    z = place_ref[0]
    every = jnp.concatenate([home_ref[h, :HEAD_DIM] for h in range(N_SEQ)], axis=0)
    grad_out[...] = matmul(every, grad_ref[...])
    for j in range(N_SEQ):
        folded = home_ref[place_of(z, j), HEAD_DIM:].astype(jnp.float32)
        columns = jnp.concatenate([folded[:, :BLOCK].T, folded[:, BLOCK:].T], axis=1)
        d_head = stack_ref[place_of(z, j)]
        pad = jnp.zeros((HEAD_DIM, CHUNK), jnp.bfloat16)
        both = jnp.concatenate([d_head, pad, columns.astype(jnp.bfloat16)], axis=0)
        wait(j)
        term = matmul(both, held[j])
        if j == 0:
            grad_t[...] = term
        else:
            grad_t[...] += term
    grad_node[...] = grad_t[...].T
    split_rows(place_ref[1], grad_node, keep_ref, give_ref)
    split_rows(place_ref[1], grad_out, keep_ref, give_ref, 3 * (grad_node.shape[0] // (2 * N_XY)))
    attn = contract_rows(every, w_ref[...])
    out_ref[...] = (x_ref[...].astype(jnp.float32) + attn + act_ref[...]).astype(jnp.bfloat16)


def share_kernel(shares_ref, out_ref):
    total = jnp.zeros(shares_ref.shape[1:], jnp.float32)
    for i in range(N_XY):
        total += shares_ref[i].astype(jnp.float32)
    for h in range(N_SEQ):
        out_ref[h] = total.astype(jnp.bfloat16)


def finish_kernel(every_ref, w_ref, m_ref, gain_ref, qkv_ref, out_ref, msg_ref, gain_out_ref):
    rows = msg_ref.shape[0]
    hd = N_SEQ * HEAD_DIM
    nodes = N_SEQ * CHUNK
    gain_sum = jnp.zeros((rows, BLOCK), jnp.float32)
    low = slice(0, HEAD_DIM)
    high = slice(HEAD_DIM, 2 * HEAD_DIM)
    for t, (band, half) in enumerate(((0, low), (0, high), (1, low))):
        for p in range(N_SEQ // 2):
            pieces = [every_ref[h, band * rows : (band + 1) * rows, half] for h in (2 * p, 2 * p + 1)]
            block = jnp.concatenate(pieces, axis=1).astype(jnp.float32) * (1.0 / nodes)
            columns = slice(t * hd + p * BLOCK, t * hd + (p + 1) * BLOCK)
            qkv_ref[:, columns] = block
            gain_sum += block * w_ref[:, columns].astype(jnp.float32)
    total = jnp.zeros((every_ref.shape[1] - 3 * rows, BLOCK), jnp.float32)
    for h in range(N_SEQ):
        columns = slice(h * BLOCK, (h + 1) * BLOCK)
        block = every_ref[h, 2 * rows : 3 * rows].astype(jnp.float32) * (1.0 / nodes)
        msg_ref[:, columns] = block
        gain_sum += block * m_ref[:, columns].astype(jnp.float32)
        total += every_ref[h, 3 * rows :].astype(jnp.float32)
    half_rows = out_ref.shape[0]
    for t in range(N_SEQ):
        out_ref[:, t * BLOCK : (t + 1) * BLOCK] = total[t * half_rows : (t + 1) * half_rows] * (1.0 / nodes)
    gain_out_ref[...] = jnp.sum(gain_sum.T, axis=0, keepdims=True) / gain_ref[...]


def input_grad_kernel(*refs):
    stack_ref, w_ref, d_msg_ref, w_msg_ref, x_ref, grad_ref, gain_ref, out_ref = refs
    parts = [
        stack_ref[h, t * HEAD_DIM : (t + 1) * HEAD_DIM] for t in range(3) for h in range(N_SEQ)
    ]
    d_norm = matmul(w_ref[...], jnp.concatenate(parts, axis=0)).T
    d_norm += contract_cols(d_msg_ref[...], w_msg_ref[...])
    wide = x_ref[...].astype(jnp.float32)
    inv_rms = unit_factor(wide, -1)
    x_hat = wide * inv_rms
    scaled = d_norm * gain_ref[...]
    d_feat = inv_rms * (scaled - x_hat * jnp.mean(scaled * x_hat, axis=-1, keepdims=True))
    out_ref[...] = (grad_ref[...].astype(jnp.float32) + d_feat).astype(jnp.bfloat16)


def after(value, *others):
    return lax.optimization_barrier((value,) + others)[0]


def exchange(array, axis):
    return lax.all_to_all(array, axis, split_axis=0, concat_axis=0, tiled=True)


def shift(array, distance):
    return lax.ppermute(array, "z", [(i, (i + distance) % N_SEQ) for i in range(N_SEQ)])


def up(array):
    return shift(array, 1)


def down(array):
    return shift(array, -1)


def sum_over_cores(keep, give):
    got = lax.ppermute(give, "c", [(0, 1), (1, 0)])
    return (keep.astype(jnp.float32) + got.astype(jnp.float32)).astype(jnp.bfloat16)


def sum_over_chips(pair):
    return jnp.sum(exchange(pair, ("x", "y")).astype(jnp.float32), axis=0)


def on_device(
    features, out_grad, norm_gain, w_qkv, w_out, w_msg, block_ids, block_counts, edge_tiles
):
    node_rows, width = features.shape
    hd = w_out.shape[0]
    nodes = N_SEQ * node_rows
    bf16, f32 = jnp.bfloat16, jnp.float32
    z = lax.axis_index("z")
    core = lax.axis_index("c")
    place = jnp.stack([z, core]).astype(jnp.int32)
    gain = norm_gain.reshape(1, width)
    wide_shape = ((node_rows, width), f32)
    low_shape = ((node_rows, width), bf16)

    n_a = normalize_half(features, gain, 0)
    a_up, a_down = [n_a, up(n_a)], [n_a, down(n_a)]
    n_b = normalize_half(features, gain, 1)
    b_up, b_down = [n_b, up(n_b)], [n_b, down(n_b)]
    w_head = pick_head(place, w_qkv)
    (d_out,) = call(
        d_out_kernel, "d_out", (((N_SEQ, HEAD_DIM, node_rows), bf16),), (), (out_grad, w_out),
        flops=2 * node_rows * width * hd, moved=2 << 20,
    )
    a_up[1], a_down[1], d_out, w_head = lax.optimization_barrier((a_up[1], a_down[1], d_out, w_head))
    a_up.append(up(a_up[1]))
    a_down.append(down(a_down[1]))
    b_up.append(up(b_up[1]))
    b_down.append(down(b_down[1]))
    a_up.append(up(a_up[2]))
    a_down.append(down(a_down[2]))
    act, to_low, mid, to_high = call(
        message_kernel, "messages", (wide_shape, low_shape, wide_shape, low_shape),
        (place, block_ids, block_counts),
        (after(a_up[1], a_up[2], a_down[2]), b_up[1], n_a, n_b, a_down[1], b_down[1], w_msg, edge_tiles, out_grad),
        [pltpu.VMEM((6, BLOCK, width), bf16), pltpu.VMEM((6, BLOCK, width), f32)],
        flops=8 * node_rows * width * width, exps=node_rows * width, moved=8 << 20,
    )
    d_heads = exchange(after(d_out, a_up[3], a_down[3]), "z")
    b_up.append(up(b_up[2]))
    b_down.append(down(b_down[2]))
    a_up[3], b_down[3], to_low, to_high = lax.optimization_barrier((a_up[3], b_down[3], to_low, to_high))
    c4 = [up(a_up[3]), down(b_down[3])]
    above, below = down(to_low), up(to_high)
    pairs = list(zip(a_up, b_up)) + [c4] + list(zip(a_down, b_down))[:0:-1]
    chunks = tuple(half for pair in pairs for half in pair)

    held = pltpu.VMEM((N_SEQ, CHUNK, width), bf16)
    lanes_in = ((N_SEQ, CHUNK, 2 * HEAD_DIM), bf16)
    turned = ((N_SEQ, HEAD_DIM, CHUNK), bf16)
    heads, *saved = call(
        forward_kernel, "attend_forward",
        (turned, lanes_in, turned, turned, ((N_SEQ, 2 * HEAD_DIM, CHUNK), bf16), ((N_SEQ, 8, CHUNK), f32)),
        (place,), (w_head,),
        [pltpu.VMEM((N_SEQ, HEAD_DIM + ONES, CHUNK), bf16), held, pltpu.SemaphoreType.DMA((16,))],
        flops=12 * nodes * nodes * HEAD_DIM, exps=nodes * nodes, moved=8 << 20, far=chunks,
    )
    send, d_msg = call(
        merge_kernel, "merge", (((N_SEQ, HEAD_DIM + BLOCK, CHUNK), bf16), low_shape), (),
        (heads, mid, above, below), moved=4 << 20,
    )
    send, d_heads = lax.optimization_barrier((send, d_heads))
    home = exchange(send, "z")

    rows_here = width // (2 * N_XY)
    rows_out = hd // (2 * N_XY)
    (stack,) = call(
        backward_kernel, "attend_backward", (((N_SEQ, 3 * HEAD_DIM, CHUNK), bf16),),
        (place,), (heads, *saved, d_heads),
        [pltpu.VMEM((N_SEQ, CHUNK, 2 * HEAD_DIM), f32), pltpu.VMEM((N_SEQ, HEAD_DIM, CHUNK), f32)],
        flops=24 * nodes * nodes * HEAD_DIM, exps=nodes * nodes, moved=4 << 20,
    )
    stack, home = lax.optimization_barrier((stack, home))
    stack_home = exchange(stack, "z")

    all_rows = 3 * rows_here + rows_out * width // BLOCK
    part = ((N_XY, all_rows, BLOCK), bf16)
    block_result_array, keep, give = call(
        result_kernel, "result", (low_shape, part, part), (place,),
        (home, stack, w_out, out_grad, features, act),
        [
            pltpu.VMEM((3 * BLOCK, width), f32), pltpu.VMEM((width, 3 * BLOCK), f32),
            pltpu.VMEM((hd, width), f32), held, pltpu.SemaphoreType.DMA((16,)),
        ],
        flops=8 * node_rows * width * width, moved=10 << 20, far=chunks,
    )
    got = lax.ppermute(give, "c", [(0, 1), (1, 0)])
    pair = (keep.astype(f32) + got.astype(f32)).astype(bf16)
    pair, stack_home = lax.optimization_barrier((pair, stack_home))
    shares = exchange(pair, ("x", "y"))
    (mine,) = call(
        share_kernel, "share_sum", (((N_SEQ, all_rows, BLOCK), bf16),), (), (shares,), moved=2 << 20,
    )
    every = exchange(mine, "z")

    (grad_input,) = call(
        input_grad_kernel, "input_grad", (low_shape,), (),
        (after(stack_home, mine), w_qkv, d_msg, w_msg, features, out_grad, gain),
        flops=6 * node_rows * width * hd, moved=8 << 20,
    )

    every, grad_input = lax.optimization_barrier((every, grad_input))
    first = ((lax.axis_index("x") * 4 + lax.axis_index("y")) * 2 + core) * rows_here
    w_rows = lax.dynamic_slice_in_dim(w_qkv, first, rows_here, 0)
    m_rows = lax.dynamic_slice_in_dim(w_msg, first, rows_here, 0)
    gain_rows = lax.dynamic_slice_in_dim(norm_gain, first, rows_here, 0).reshape(1, rows_here)
    grad_qkv, grad_out, grad_msg, grad_gain = call(
        finish_kernel, "finish",
        (((rows_here, 3 * hd), f32), ((rows_out, width), f32), ((rows_here, width), f32), ((1, rows_here), f32)),
        (), (every, w_rows, m_rows, gain_rows), moved=2 << 20,
    )
    return block_result_array, grad_input, grad_gain.reshape(rows_here), grad_qkv, grad_out, grad_msg


def solution(mesh):
    fine = Mesh(mesh.devices.reshape(4, 4, 2, N_SEQ), ("x", "y", "c", "z"))
    dp = ("x", "y", "c")
    rows = ("x", "y", "c", "z")
    return jax.shard_map(
        on_device,
        mesh=fine,
        in_specs=(
            P(rows, None),
            P(rows, None),
            P(),
            P(),
            P(),
            P(),
            P(rows, None),
            P(rows),
            P(rows, None, None, None),
        ),
        out_specs=(
            P(rows, None),
            P(rows, None),
            P(dp),
            P(dp, None),
            P(dp, None),
            P(dp, None),
        ),
        check_vma=False,
    )
```

```python
import jax
import jax.numpy as jnp
from jax import lax
from jax.experimental import pallas as pl
from jax.experimental.pallas import tpu as pltpu
from jax.sharding import Mesh
from jax.sharding import PartitionSpec as P

HEAD_DIM = 64
BLOCK = 128
SLOTS = 4
N_SEQ = 8
N_XY = 16
CHUNK = 256
ONES = 16

exponent_divisor = 32.0
epsilon = 1e-06
SCALE = exponent_divisor / HEAD_DIM


def matmul(left, right):
    return jnp.dot(left, right, preferred_element_type=jnp.float32)


def contract_rows(left, right):
    return lax.dot_general(
        left, right, (((0,), (0,)), ((), ())), preferred_element_type=jnp.float32
    )


def contract_cols(left, right):
    return lax.dot_general(
        left, right, (((1,), (1,)), ((), ())), preferred_element_type=jnp.float32
    )


def unit_factor(wide, axis):
    return lax.rsqrt(jnp.mean(wide * wide, axis=axis, keepdims=True) + epsilon)


def call(kernel, name, out_shape, scalars, arrays, scratch=(), flops=0, exps=0, moved=0, far=()):
    specs = [pl.BlockSpec(memory_space=pltpu.SMEM)] * len(scalars)
    specs += [pl.BlockSpec(memory_space=pltpu.HBM)] * len(far)
    specs += [pl.BlockSpec(memory_space=pltpu.VMEM)] * len(arrays)
    return pl.pallas_call(
        kernel,
        out_shape=tuple(jax.ShapeDtypeStruct(s, t) for s, t in out_shape),
        in_specs=specs,
        out_specs=tuple(pl.BlockSpec(memory_space=pltpu.VMEM) for _ in out_shape),
        scratch_shapes=list(scratch),
        compiler_params=pltpu.CompilerParams(vmem_limit_bytes=63 * 1024 * 1024 + 512 * 1024),
        cost_estimate=pl.CostEstimate(flops=flops, bytes_accessed=moved, transcendentals=exps),
        name=name,
    )(*scalars, *far, *arrays)


def normalize_kernel(x_ref, gain_ref, *out_refs):
    for half, out_ref in enumerate(out_refs):
        wide = x_ref[half * BLOCK : (half + 1) * BLOCK].astype(jnp.float32)
        out_ref[...] = (wide * unit_factor(wide, -1) * gain_ref[...]).astype(jnp.bfloat16)


def d_out_kernel(grad_ref, w_ref, out_ref):
    turned = contract_cols(w_ref[...], grad_ref[...]).astype(jnp.bfloat16)
    for h in range(N_SEQ):
        out_ref[h] = turned[h * HEAD_DIM : (h + 1) * HEAD_DIM]


def pick_kernel(place_ref, q_ref, k_ref, v_ref, out_ref):
    odd = lax.rem(place_ref[0], 2) == 1

    def halves(ref):
        wide = ref[...].astype(jnp.float32)
        swapped = jnp.concatenate([wide[:, HEAD_DIM:], wide[:, :HEAD_DIM]], axis=1)
        return jnp.where(odd, swapped, wide), jnp.where(odd, wide, swapped)

    left = lax.broadcasted_iota(jnp.int32, q_ref.shape, 1) < HEAD_DIM
    query, _ = halves(q_ref)
    _, keyrow = halves(k_ref)
    val, _ = halves(v_ref)
    out_ref[:, : 2 * HEAD_DIM] = jnp.where(left, query, keyrow).astype(jnp.bfloat16)
    out_ref[:, 2 * HEAD_DIM :] = jnp.where(left, val, 0.0).astype(jnp.bfloat16)


def pick_head(place, w_qkv):
    width, columns = w_qkv.shape
    step = columns // 3 // (2 * HEAD_DIM)

    def block(t):
        return pl.BlockSpec((width, 2 * HEAD_DIM), lambda i, place: (0, t * step + place[0] // 2))

    return pl.pallas_call(
        pick_kernel,
        grid_spec=pltpu.PrefetchScalarGridSpec(
            num_scalar_prefetch=1,
            grid=(1,),
            in_specs=[block(0), block(1), block(2)],
            out_specs=pl.BlockSpec((width, 4 * HEAD_DIM), lambda i, place: (0, 0)),
        ),
        out_shape=jax.ShapeDtypeStruct((width, 4 * HEAD_DIM), jnp.bfloat16),
        cost_estimate=pl.CostEstimate(flops=0, bytes_accessed=4 << 20, transcendentals=0),
        name="pick_head",
    )(place, w_qkv, w_qkv, w_qkv)


def message_kernel(*refs):
    place_ref, ids_ref, counts_ref = refs[:3]
    blocks = refs[3:9]
    w_ref, tiles_ref, grad_ref = refs[9:12]
    act_ref, to_low_ref, mid_ref, to_high_ref, msg, landed = refs[12:]
    z = place_ref[0]
    for t in range(3):
        both = jnp.concatenate([blocks[2 * t][...], blocks[2 * t + 1][...]], axis=0)
        rows = matmul(both, w_ref[...]).astype(jnp.bfloat16)
        msg[2 * t] = rows[:BLOCK]
        msg[2 * t + 1] = rows[BLOCK:]
    landed[...] = jnp.zeros_like(landed)
    for b in range(2):
        spots = []
        live = []
        for s in range(SLOTS):
            spots.append(jnp.clip(ids_ref[b, s] - 2 * (z - 1), 0, 5))
            mask = jnp.where(s < counts_ref[b], 1.0, 0.0)
            live.append(tiles_ref[b, s].astype(jnp.float32) * mask)
        source = jnp.concatenate([msg[spot] for spot in spots], axis=0)
        agg = matmul(jnp.concatenate(live, axis=1).astype(jnp.bfloat16), source)
        sigma = 1.0 / (1.0 + jnp.exp(-agg))
        rows = slice(b * BLOCK, (b + 1) * BLOCK)
        act_ref[rows] = agg * sigma
        d_agg = grad_ref[rows].astype(jnp.float32) * sigma * (1.0 + agg * (1.0 - sigma))
        d_agg = d_agg.astype(jnp.bfloat16)
        for s in range(SLOTS):
            landed[spots[s]] += matmul(live[s].T.astype(jnp.bfloat16), d_agg)
    for b in range(2):
        rows = slice(b * BLOCK, (b + 1) * BLOCK)
        to_low_ref[rows] = landed[b].astype(jnp.bfloat16)
        mid_ref[rows] = landed[2 + b]
        to_high_ref[rows] = landed[4 + b].astype(jnp.bfloat16)


def split_rows(core, source, keep_ref, give_ref, offset=0):
    rows = source.shape[0] // (2 * N_XY)
    for i in range(N_XY):
        for t in range(source.shape[1] // BLOCK):
            spot = slice(offset + t * rows, offset + (t + 1) * rows)
            columns = slice(t * BLOCK, (t + 1) * BLOCK)
            keep_ref[i, spot] = source[pl.ds((2 * i + core) * rows, rows), columns].astype(jnp.bfloat16)
            give_ref[i, spot] = source[pl.ds((2 * i + 1 - core) * rows, rows), columns].astype(
                jnp.bfloat16
            )


def merge_kernel(heads_ref, mid_ref, above_ref, below_ref, send_ref, d_msg_ref):
    total = mid_ref[...] + above_ref[...].astype(jnp.float32) + below_ref[...].astype(jnp.float32)
    d_msg = total.astype(jnp.bfloat16)
    d_msg_ref[...] = d_msg
    for t in range(N_SEQ):
        columns = d_msg[:, t * BLOCK : (t + 1) * BLOCK]
        send_ref[t, :HEAD_DIM] = heads_ref[t]
        send_ref[t, HEAD_DIM:] = jnp.concatenate([columns[:BLOCK], columns[BLOCK:]], axis=1)


def place_of(z, j):
    return lax.rem(z - j + N_SEQ, N_SEQ)


def fetch_chunks(refs, held, sems):
    copies = [
        pltpu.make_async_copy(ref, held.at[i // 2, pl.ds(i % 2 * BLOCK, BLOCK)], sems.at[i])
        for i, ref in enumerate(refs)
    ]
    for copy in copies:
        copy.start()

    def wait(j):
        copies[2 * j].wait()
        copies[2 * j + 1].wait()

    return wait


def forward_kernel(*refs):
    z = refs[0][0]
    w_ref = refs[17]
    out_ref, kv_ref, hq_ref, ku_ref, raw_ref, stats_ref = refs[18:24]
    v_ext, held, sems = refs[24:]
    wait = fetch_chunks(refs[1:17], held, sems)
    for j in range(N_SEQ):
        if j % 4 == 0:
            for i in range(j, j + 4):
                wait(i)
            rows = held[j : j + 4].reshape(4 * CHUNK, held.shape[2])
            group = matmul(rows, w_ref[...]).T.astype(jnp.bfloat16)
        proj = group[:, j % 4 * CHUNK : (j % 4 + 1) * CHUNK]
        raw_ref[j] = proj[: 2 * HEAD_DIM]
        query = proj[:HEAD_DIM].astype(jnp.float32)
        keyrow = proj[HEAD_DIM : 2 * HEAD_DIM].astype(jnp.float32)
        val = proj[2 * HEAD_DIM : 3 * HEAD_DIM]
        q_unit = (query * unit_factor(query, 0)).astype(jnp.bfloat16).astype(jnp.float32) * SCALE
        k_unit = keyrow * unit_factor(keyrow, 0)
        hq_ref[j] = q_unit.astype(jnp.bfloat16)
        ku_ref[j] = k_unit.astype(jnp.bfloat16)
        v_ext[j, :HEAD_DIM] = val
        v_ext[j, HEAD_DIM:] = jnp.ones((ONES, CHUNK), jnp.bfloat16)
        kv_ref[j] = jnp.concatenate([k_unit, val.astype(jnp.float32)], axis=0).T.astype(jnp.bfloat16)

    def step(i, carry):
        query = jnp.concatenate([hq_ref[i], jnp.zeros_like(hq_ref[i])], axis=0)
        keys = kv_ref[...].reshape(N_SEQ * CHUNK, 2 * HEAD_DIM)
        exps = jnp.exp(matmul(keys, query)).astype(jnp.bfloat16)
        out = matmul(jnp.concatenate([v_ext[j] for j in range(N_SEQ)], axis=1), exps)
        inverse = 1.0 / out[HEAD_DIM : HEAD_DIM + 1]
        stats_ref[i, 0:1] = inverse
        head_out = (out[:HEAD_DIM] * inverse).astype(jnp.bfloat16)
        out_ref[place_of(z, i)] = head_out
        return carry

    lax.fori_loop(0, N_SEQ, step, 0)


def backward_kernel(*refs):
    z = refs[0][0]
    head_ref, kv_ref, hq_ref, ku_ref, raw_ref, stats_ref, d_ref = refs[1:8]
    stack_ref, sums, dqt = refs[8:]
    sums[...] = jnp.zeros_like(sums)

    def step(i, carry):
        zero = jnp.zeros_like(hq_ref[i])
        query = jnp.concatenate([hq_ref[i], zero], axis=0)
        d_out = d_ref[place_of(z, i)]
        d_wide = d_out.astype(jnp.float32)
        d_head = jnp.concatenate([zero, d_out], axis=0)
        rows = jnp.concatenate([hq_ref[i].astype(jnp.float32), d_wide], axis=0).T
        left = lax.broadcasted_iota(jnp.int32, rows.shape, 1) < HEAD_DIM
        rhs = jnp.concatenate([jnp.where(left, 0.0, rows), jnp.where(left, rows, 0.0)], axis=0)
        rhs = rhs.astype(jnp.bfloat16)
        inverse = stats_ref[i, 0:1]
        row_dot = jnp.sum(head_ref[place_of(z, i)].astype(jnp.float32) * d_wide, axis=0, keepdims=True)
        keys = kv_ref[...].reshape(N_SEQ * CHUNK, 2 * HEAD_DIM)
        prob = jnp.exp(matmul(keys, query)) * inverse
        d_scores = (prob * (matmul(keys, d_head) - row_dot)).astype(jnp.bfloat16)
        d_qunit = matmul(jnp.concatenate([ku_ref[j] for j in range(N_SEQ)], axis=1), d_scores)
        both = jnp.concatenate([prob.astype(jnp.bfloat16), d_scores], axis=1)
        sums[...] += matmul(both, rhs).reshape(N_SEQ, CHUNK, 2 * HEAD_DIM)
        dqt[i] = d_qunit * SCALE
        return carry

    lax.fori_loop(0, N_SEQ, step, 0)
    for j in range(N_SEQ):
        turned = sums[j].T
        pieces = []
        for t, d_unit in enumerate((dqt[j], turned[:HEAD_DIM])):
            wide = raw_ref[j, t * HEAD_DIM : (t + 1) * HEAD_DIM].astype(jnp.float32)
            factor = unit_factor(wide, 0)
            mean = jnp.mean(d_unit * wide, axis=0, keepdims=True)
            pieces.append(factor * d_unit - factor * factor * factor * wide * mean)
        stacked = jnp.concatenate(pieces + [turned[HEAD_DIM:]], axis=0).astype(jnp.bfloat16)
        stack_ref[place_of(z, j)] = stacked


def result_kernel(*refs):
    place_ref = refs[0]
    home_ref, stack_ref, w_ref, grad_ref, x_ref, act_ref = refs[17:23]
    out_ref, keep_ref, give_ref, grad_t, grad_node, grad_out, held, sems = refs[23:]
    wait = fetch_chunks(refs[1:17], held, sems)
    z = place_ref[0]
    every = jnp.concatenate([home_ref[h, :HEAD_DIM] for h in range(N_SEQ)], axis=0)
    grad_out[...] = matmul(every, grad_ref[...])
    for j in range(N_SEQ):
        folded = home_ref[place_of(z, j), HEAD_DIM:].astype(jnp.float32)
        columns = jnp.concatenate([folded[:, :BLOCK].T, folded[:, BLOCK:].T], axis=1)
        d_head = stack_ref[place_of(z, j)]
        pad = jnp.zeros((HEAD_DIM, CHUNK), jnp.bfloat16)
        both = jnp.concatenate([d_head, pad, columns.astype(jnp.bfloat16)], axis=0)
        wait(j)
        term = matmul(both, held[j])
        if j == 0:
            grad_t[...] = term
        else:
            grad_t[...] += term
    grad_node[...] = grad_t[...].T
    split_rows(place_ref[1], grad_node, keep_ref, give_ref)
    split_rows(place_ref[1], grad_out, keep_ref, give_ref, 3 * (grad_node.shape[0] // (2 * N_XY)))
    attn = contract_rows(every, w_ref[...])
    out_ref[...] = (x_ref[...].astype(jnp.float32) + attn + act_ref[...]).astype(jnp.bfloat16)


def share_kernel(shares_ref, out_ref):
    total = jnp.zeros(shares_ref.shape[1:], jnp.float32)
    for i in range(N_XY):
        total += shares_ref[i].astype(jnp.float32)
    for h in range(N_SEQ):
        out_ref[h] = total.astype(jnp.bfloat16)


def finish_kernel(every_ref, w_ref, m_ref, gain_ref, qkv_ref, out_ref, msg_ref, gain_out_ref):
    rows = msg_ref.shape[0]
    hd = N_SEQ * HEAD_DIM
    nodes = N_SEQ * CHUNK
    gain_sum = jnp.zeros((rows, BLOCK), jnp.float32)
    low = slice(0, HEAD_DIM)
    high = slice(HEAD_DIM, 2 * HEAD_DIM)
    for t, (band, half) in enumerate(((0, low), (0, high), (1, low))):
        for p in range(N_SEQ // 2):
            pieces = [every_ref[h, band * rows : (band + 1) * rows, half] for h in (2 * p, 2 * p + 1)]
            block = jnp.concatenate(pieces, axis=1).astype(jnp.float32) * (1.0 / nodes)
            columns = slice(t * hd + p * BLOCK, t * hd + (p + 1) * BLOCK)
            qkv_ref[:, columns] = block
            gain_sum += block * w_ref[:, columns].astype(jnp.float32)
    total = jnp.zeros((every_ref.shape[1] - 3 * rows, BLOCK), jnp.float32)
    for h in range(N_SEQ):
        columns = slice(h * BLOCK, (h + 1) * BLOCK)
        block = every_ref[h, 2 * rows : 3 * rows].astype(jnp.float32) * (1.0 / nodes)
        msg_ref[:, columns] = block
        gain_sum += block * m_ref[:, columns].astype(jnp.float32)
        total += every_ref[h, 3 * rows :].astype(jnp.float32)
    half_rows = out_ref.shape[0]
    for t in range(N_SEQ):
        out_ref[:, t * BLOCK : (t + 1) * BLOCK] = total[t * half_rows : (t + 1) * half_rows] * (1.0 / nodes)
    gain_out_ref[...] = jnp.sum(gain_sum.T, axis=0, keepdims=True) / gain_ref[...]


def input_grad_kernel(*refs):
    stack_ref, w_ref, d_msg_ref, w_msg_ref, x_ref, grad_ref, gain_ref, out_ref = refs
    parts = [
        stack_ref[h, t * HEAD_DIM : (t + 1) * HEAD_DIM] for t in range(3) for h in range(N_SEQ)
    ]
    d_norm = matmul(w_ref[...], jnp.concatenate(parts, axis=0)).T
    d_norm += contract_cols(d_msg_ref[...], w_msg_ref[...])
    wide = x_ref[...].astype(jnp.float32)
    inv_rms = unit_factor(wide, -1)
    x_hat = wide * inv_rms
    scaled = d_norm * gain_ref[...]
    d_feat = inv_rms * (scaled - x_hat * jnp.mean(scaled * x_hat, axis=-1, keepdims=True))
    out_ref[...] = (grad_ref[...].astype(jnp.float32) + d_feat).astype(jnp.bfloat16)


def after(value, *others):
    return lax.optimization_barrier((value,) + others)[0]


def exchange(array, axis):
    return lax.all_to_all(array, axis, split_axis=0, concat_axis=0, tiled=True)


def shift(array, distance):
    return lax.ppermute(array, "z", [(i, (i + distance) % N_SEQ) for i in range(N_SEQ)])


def up(array):
    return shift(array, 1)


def down(array):
    return shift(array, -1)


def sum_over_cores(keep, give):
    got = lax.ppermute(give, "c", [(0, 1), (1, 0)])
    return (keep.astype(jnp.float32) + got.astype(jnp.float32)).astype(jnp.bfloat16)


def sum_over_chips(pair):
    return jnp.sum(exchange(pair, ("x", "y")).astype(jnp.float32), axis=0)


def on_device(
    features, out_grad, norm_gain, w_qkv, w_out, w_msg, block_ids, block_counts, edge_tiles
):
    node_rows, width = features.shape
    hd = w_out.shape[0]
    nodes = N_SEQ * node_rows
    bf16, f32 = jnp.bfloat16, jnp.float32
    z = lax.axis_index("z")
    core = lax.axis_index("c")
    place = jnp.stack([z, core]).astype(jnp.int32)
    gain = norm_gain.reshape(1, width)
    wide_shape = ((node_rows, width), f32)
    low_shape = ((node_rows, width), bf16)

    n_a, n_b = call(
        normalize_kernel, "normalize", (((BLOCK, width), bf16),) * 2, (), (features, gain), moved=1 << 20
    )
    a_up, a_down = [n_a, up(n_a)], [n_a, down(n_a)]
    b_up, b_down = [n_b, up(n_b)], [n_b, down(n_b)]
    w_head = pick_head(place, w_qkv)
    (d_out,) = call(
        d_out_kernel, "d_out", (((N_SEQ, HEAD_DIM, node_rows), bf16),), (), (out_grad, w_out),
        flops=2 * node_rows * width * hd, moved=2 << 20,
    )
    a_up[1], a_down[1], d_out, w_head = lax.optimization_barrier((a_up[1], a_down[1], d_out, w_head))
    a_up.append(up(a_up[1]))
    a_down.append(down(a_down[1]))
    b_up.append(up(b_up[1]))
    b_down.append(down(b_down[1]))
    a_up.append(up(a_up[2]))
    a_down.append(down(a_down[2]))
    act, to_low, mid, to_high = call(
        message_kernel, "messages", (wide_shape, low_shape, wide_shape, low_shape),
        (place, block_ids, block_counts),
        (after(a_up[1], a_up[2], a_down[2]), b_up[1], n_a, n_b, a_down[1], b_down[1], w_msg, edge_tiles, out_grad),
        [pltpu.VMEM((6, BLOCK, width), bf16), pltpu.VMEM((6, BLOCK, width), f32)],
        flops=8 * node_rows * width * width, exps=node_rows * width, moved=8 << 20,
    )
    d_heads = exchange(after(d_out, a_up[3], a_down[3]), "z")
    b_up.append(up(b_up[2]))
    b_down.append(down(b_down[2]))
    a_up[3], b_down[3], to_low, to_high = lax.optimization_barrier((a_up[3], b_down[3], to_low, to_high))
    c4 = [up(a_up[3]), down(b_down[3])]
    above, below = down(to_low), up(to_high)
    pairs = list(zip(a_up, b_up)) + [c4] + list(zip(a_down, b_down))[:0:-1]
    chunks = tuple(half for pair in pairs for half in pair)

    held = pltpu.VMEM((N_SEQ, CHUNK, width), bf16)
    lanes_in = ((N_SEQ, CHUNK, 2 * HEAD_DIM), bf16)
    turned = ((N_SEQ, HEAD_DIM, CHUNK), bf16)
    heads, *saved = call(
        forward_kernel, "attend_forward",
        (turned, lanes_in, turned, turned, ((N_SEQ, 2 * HEAD_DIM, CHUNK), bf16), ((N_SEQ, 8, CHUNK), f32)),
        (place,), (w_head,),
        [pltpu.VMEM((N_SEQ, HEAD_DIM + ONES, CHUNK), bf16), held, pltpu.SemaphoreType.DMA((16,))],
        flops=12 * nodes * nodes * HEAD_DIM, exps=nodes * nodes, moved=8 << 20, far=chunks,
    )
    send, d_msg = call(
        merge_kernel, "merge", (((N_SEQ, HEAD_DIM + BLOCK, CHUNK), bf16), low_shape), (),
        (heads, mid, above, below), moved=4 << 20,
    )
    send, d_heads = lax.optimization_barrier((send, d_heads))
    home = exchange(send, "z")

    rows_here = width // (2 * N_XY)
    rows_out = hd // (2 * N_XY)
    (stack,) = call(
        backward_kernel, "attend_backward", (((N_SEQ, 3 * HEAD_DIM, CHUNK), bf16),),
        (place,), (heads, *saved, d_heads),
        [pltpu.VMEM((N_SEQ, CHUNK, 2 * HEAD_DIM), f32), pltpu.VMEM((N_SEQ, HEAD_DIM, CHUNK), f32)],
        flops=24 * nodes * nodes * HEAD_DIM, exps=nodes * nodes, moved=4 << 20,
    )
    stack, home = lax.optimization_barrier((stack, home))
    stack_home = exchange(stack, "z")

    all_rows = 3 * rows_here + rows_out * width // BLOCK
    part = ((N_XY, all_rows, BLOCK), bf16)
    block_result_array, keep, give = call(
        result_kernel, "result", (low_shape, part, part), (place,),
        (home, stack, w_out, out_grad, features, act),
        [
            pltpu.VMEM((3 * BLOCK, width), f32), pltpu.VMEM((width, 3 * BLOCK), f32),
            pltpu.VMEM((hd, width), f32), held, pltpu.SemaphoreType.DMA((16,)),
        ],
        flops=8 * node_rows * width * width, moved=10 << 20, far=chunks,
    )
    got = lax.ppermute(give, "c", [(0, 1), (1, 0)])
    pair = (keep.astype(f32) + got.astype(f32)).astype(bf16)
    pair, stack_home = lax.optimization_barrier((pair, stack_home))
    shares = exchange(pair, ("x", "y"))
    (mine,) = call(
        share_kernel, "share_sum", (((N_SEQ, all_rows, BLOCK), bf16),), (), (shares,), moved=2 << 20,
    )
    every = exchange(mine, "z")

    (grad_input,) = call(
        input_grad_kernel, "input_grad", (low_shape,), (),
        (after(stack_home, mine), w_qkv, d_msg, w_msg, features, out_grad, gain),
        flops=6 * node_rows * width * hd, moved=8 << 20,
    )

    every, grad_input = lax.optimization_barrier((every, grad_input))
    first = ((lax.axis_index("x") * 4 + lax.axis_index("y")) * 2 + core) * rows_here
    w_rows = lax.dynamic_slice_in_dim(w_qkv, first, rows_here, 0)
    m_rows = lax.dynamic_slice_in_dim(w_msg, first, rows_here, 0)
    gain_rows = lax.dynamic_slice_in_dim(norm_gain, first, rows_here, 0).reshape(1, rows_here)
    grad_qkv, grad_out, grad_msg, grad_gain = call(
        finish_kernel, "finish",
        (((rows_here, 3 * hd), f32), ((rows_out, width), f32), ((rows_here, width), f32), ((1, rows_here), f32)),
        (), (every, w_rows, m_rows, gain_rows), moved=2 << 20,
    )
    return block_result_array, grad_input, grad_gain.reshape(rows_here), grad_qkv, grad_out, grad_msg


def solution(mesh):
    fine = Mesh(mesh.devices.reshape(4, 4, 2, N_SEQ), ("x", "y", "c", "z"))
    dp = ("x", "y", "c")
    rows = ("x", "y", "c", "z")
    return jax.shard_map(
        on_device,
        mesh=fine,
        in_specs=(
            P(rows, None),
            P(rows, None),
            P(),
            P(),
            P(),
            P(),
            P(rows, None),
            P(rows),
            P(rows, None, None, None),
        ),
        out_specs=(
            P(rows, None),
            P(rows, None),
            P(dp),
            P(dp, None),
            P(dp, None),
            P(dp, None),
        ),
        check_vma=False,
    )
```

```python
import jax
import jax.numpy as jnp
from jax import lax
from jax.experimental import pallas as pl
from jax.experimental.pallas import tpu as pltpu
from jax.sharding import Mesh
from jax.sharding import PartitionSpec as P

HEAD_DIM = 64
BLOCK = 128
SLOTS = 4
N_SEQ = 8
N_XY = 16
CHUNK = 256
ONES = 16

exponent_divisor = 32.0
epsilon = 1e-06
SCALE = exponent_divisor / HEAD_DIM


def matmul(left, right):
    return jnp.dot(left, right, preferred_element_type=jnp.float32)


def contract_rows(left, right):
    return lax.dot_general(
        left, right, (((0,), (0,)), ((), ())), preferred_element_type=jnp.float32
    )


def contract_cols(left, right):
    return lax.dot_general(
        left, right, (((1,), (1,)), ((), ())), preferred_element_type=jnp.float32
    )


def unit_factor(wide, axis):
    return lax.rsqrt(jnp.mean(wide * wide, axis=axis, keepdims=True) + epsilon)


def call(kernel, name, out_shape, scalars, arrays, scratch=(), flops=0, exps=0, moved=0, far=()):
    specs = [pl.BlockSpec(memory_space=pltpu.SMEM)] * len(scalars)
    specs += [pl.BlockSpec(memory_space=pltpu.HBM)] * len(far)
    specs += [pl.BlockSpec(memory_space=pltpu.VMEM)] * len(arrays)
    return pl.pallas_call(
        kernel,
        out_shape=tuple(jax.ShapeDtypeStruct(s, t) for s, t in out_shape),
        in_specs=specs,
        out_specs=tuple(pl.BlockSpec(memory_space=pltpu.VMEM) for _ in out_shape),
        scratch_shapes=list(scratch),
        compiler_params=pltpu.CompilerParams(vmem_limit_bytes=63 * 1024 * 1024 + 512 * 1024),
        cost_estimate=pl.CostEstimate(flops=flops, bytes_accessed=moved, transcendentals=exps),
        name=name,
    )(*scalars, *far, *arrays)


def normalize_kernel(x_ref, gain_ref, *out_refs):
    for half, out_ref in enumerate(out_refs):
        wide = x_ref[half * BLOCK : (half + 1) * BLOCK].astype(jnp.float32)
        out_ref[...] = (wide * unit_factor(wide, -1) * gain_ref[...]).astype(jnp.bfloat16)


def d_out_kernel(grad_ref, w_ref, out_ref):
    turned = contract_cols(w_ref[...], grad_ref[...]).astype(jnp.bfloat16)
    for h in range(N_SEQ):
        out_ref[h] = turned[h * HEAD_DIM : (h + 1) * HEAD_DIM]


def pick_kernel(place_ref, q_ref, k_ref, v_ref, out_ref):
    odd = lax.rem(place_ref[0], 2) == 1

    def halves(ref):
        wide = ref[...].astype(jnp.float32)
        swapped = jnp.concatenate([wide[:, HEAD_DIM:], wide[:, :HEAD_DIM]], axis=1)
        return jnp.where(odd, swapped, wide), jnp.where(odd, wide, swapped)

    left = lax.broadcasted_iota(jnp.int32, q_ref.shape, 1) < HEAD_DIM
    query, _ = halves(q_ref)
    _, keyrow = halves(k_ref)
    val, _ = halves(v_ref)
    out_ref[:, : 2 * HEAD_DIM] = jnp.where(left, query, keyrow).astype(jnp.bfloat16)
    out_ref[:, 2 * HEAD_DIM :] = jnp.where(left, val, 0.0).astype(jnp.bfloat16)


def pick_head(place, w_qkv):
    width, columns = w_qkv.shape
    step = columns // 3 // (2 * HEAD_DIM)

    def block(t):
        return pl.BlockSpec((width, 2 * HEAD_DIM), lambda i, place: (0, t * step + place[0] // 2))

    return pl.pallas_call(
        pick_kernel,
        grid_spec=pltpu.PrefetchScalarGridSpec(
            num_scalar_prefetch=1,
            grid=(1,),
            in_specs=[block(0), block(1), block(2)],
            out_specs=pl.BlockSpec((width, 4 * HEAD_DIM), lambda i, place: (0, 0)),
        ),
        out_shape=jax.ShapeDtypeStruct((width, 4 * HEAD_DIM), jnp.bfloat16),
        cost_estimate=pl.CostEstimate(flops=0, bytes_accessed=4 << 20, transcendentals=0),
        name="pick_head",
    )(place, w_qkv, w_qkv, w_qkv)


def message_kernel(*refs):
    place_ref, ids_ref, counts_ref = refs[:3]
    blocks = refs[3:9]
    w_ref, tiles_ref, grad_ref = refs[9:12]
    act_ref, to_low_ref, mid_ref, to_high_ref, msg, landed = refs[12:]
    z = place_ref[0]
    for t in range(3):
        both = jnp.concatenate([blocks[2 * t][...], blocks[2 * t + 1][...]], axis=0)
        rows = matmul(both, w_ref[...]).astype(jnp.bfloat16)
        msg[2 * t] = rows[:BLOCK]
        msg[2 * t + 1] = rows[BLOCK:]
    landed[...] = jnp.zeros_like(landed)
    for b in range(2):
        spots = []
        live = []
        for s in range(SLOTS):
            spots.append(jnp.clip(ids_ref[b, s] - 2 * (z - 1), 0, 5))
            mask = jnp.where(s < counts_ref[b], 1.0, 0.0)
            live.append(tiles_ref[b, s].astype(jnp.float32) * mask)
        source = jnp.concatenate([msg[spot] for spot in spots], axis=0)
        agg = matmul(jnp.concatenate(live, axis=1).astype(jnp.bfloat16), source)
        sigma = 1.0 / (1.0 + jnp.exp(-agg))
        rows = slice(b * BLOCK, (b + 1) * BLOCK)
        act_ref[rows] = agg * sigma
        d_agg = grad_ref[rows].astype(jnp.float32) * sigma * (1.0 + agg * (1.0 - sigma))
        d_agg = d_agg.astype(jnp.bfloat16)
        for s in range(SLOTS):
            landed[spots[s]] += matmul(live[s].T.astype(jnp.bfloat16), d_agg)
    for b in range(2):
        rows = slice(b * BLOCK, (b + 1) * BLOCK)
        to_low_ref[rows] = landed[b].astype(jnp.bfloat16)
        mid_ref[rows] = landed[2 + b]
        to_high_ref[rows] = landed[4 + b].astype(jnp.bfloat16)


def split_rows(core, source, keep_ref, give_ref, offset=0):
    rows = source.shape[0] // (2 * N_XY)
    for i in range(N_XY):
        for t in range(source.shape[1] // BLOCK):
            spot = slice(offset + t * rows, offset + (t + 1) * rows)
            columns = slice(t * BLOCK, (t + 1) * BLOCK)
            keep_ref[i, spot] = source[pl.ds((2 * i + core) * rows, rows), columns].astype(jnp.bfloat16)
            give_ref[i, spot] = source[pl.ds((2 * i + 1 - core) * rows, rows), columns].astype(
                jnp.bfloat16
            )


def merge_kernel(heads_ref, mid_ref, above_ref, below_ref, send_ref, d_msg_ref):
    total = mid_ref[...] + above_ref[...].astype(jnp.float32) + below_ref[...].astype(jnp.float32)
    d_msg = total.astype(jnp.bfloat16)
    d_msg_ref[...] = d_msg
    for t in range(N_SEQ):
        columns = d_msg[:, t * BLOCK : (t + 1) * BLOCK]
        send_ref[t, :HEAD_DIM] = heads_ref[t]
        send_ref[t, HEAD_DIM:] = jnp.concatenate([columns[:BLOCK], columns[BLOCK:]], axis=1)


def place_of(z, j):
    return lax.rem(z - j + N_SEQ, N_SEQ)


def fetch_chunks(refs, held, sems):
    copies = [
        pltpu.make_async_copy(ref, held.at[i // 2, pl.ds(i % 2 * BLOCK, BLOCK)], sems.at[i])
        for i, ref in enumerate(refs)
    ]
    for copy in copies:
        copy.start()

    def wait(j):
        copies[2 * j].wait()
        copies[2 * j + 1].wait()

    return wait


def forward_kernel(*refs):
    z = refs[0][0]
    w_ref = refs[17]
    out_ref, kv_ref, hq_ref, ku_ref, raw_ref, stats_ref = refs[18:24]
    v_ext, held, sems = refs[24:]
    wait = fetch_chunks(refs[1:17], held, sems)
    for j in range(N_SEQ):
        if j % 4 == 0:
            for i in range(j, j + 4):
                wait(i)
            rows = held[j : j + 4].reshape(4 * CHUNK, held.shape[2])
            group = matmul(rows, w_ref[...]).T.astype(jnp.bfloat16)
        proj = group[:, j % 4 * CHUNK : (j % 4 + 1) * CHUNK]
        raw_ref[j] = proj[: 2 * HEAD_DIM]
        query = proj[:HEAD_DIM].astype(jnp.float32)
        keyrow = proj[HEAD_DIM : 2 * HEAD_DIM].astype(jnp.float32)
        val = proj[2 * HEAD_DIM : 3 * HEAD_DIM]
        q_unit = (query * unit_factor(query, 0)).astype(jnp.bfloat16).astype(jnp.float32) * SCALE
        k_unit = keyrow * unit_factor(keyrow, 0)
        hq_ref[j] = q_unit.astype(jnp.bfloat16)
        ku_ref[j] = k_unit.astype(jnp.bfloat16)
        v_ext[j, :HEAD_DIM] = val
        v_ext[j, HEAD_DIM:] = jnp.ones((ONES, CHUNK), jnp.bfloat16)
        kv_ref[j] = jnp.concatenate([k_unit, val.astype(jnp.float32)], axis=0).T.astype(jnp.bfloat16)

    def step(i, carry):
        query = jnp.concatenate([hq_ref[i], jnp.zeros_like(hq_ref[i])], axis=0)
        keys = kv_ref[...].reshape(N_SEQ * CHUNK, 2 * HEAD_DIM)
        exps = jnp.exp(matmul(keys, query)).astype(jnp.bfloat16)
        out = matmul(jnp.concatenate([v_ext[j] for j in range(N_SEQ)], axis=1), exps)
        inverse = 1.0 / out[HEAD_DIM : HEAD_DIM + 1]
        stats_ref[i, 0:1] = inverse
        head_out = (out[:HEAD_DIM] * inverse).astype(jnp.bfloat16)
        out_ref[place_of(z, i)] = head_out
        return carry

    lax.fori_loop(0, N_SEQ, step, 0)


def backward_kernel(*refs):
    z = refs[0][0]
    head_ref, kv_ref, hq_ref, ku_ref, raw_ref, stats_ref, d_ref = refs[1:8]
    stack_ref, sums, dqt = refs[8:]
    sums[...] = jnp.zeros_like(sums)

    def step(i, carry):
        zero = jnp.zeros_like(hq_ref[i])
        query = jnp.concatenate([hq_ref[i], zero], axis=0)
        d_out = d_ref[place_of(z, i)]
        d_wide = d_out.astype(jnp.float32)
        d_head = jnp.concatenate([zero, d_out], axis=0)
        rows = jnp.concatenate([hq_ref[i].astype(jnp.float32), d_wide], axis=0).T
        left = lax.broadcasted_iota(jnp.int32, rows.shape, 1) < HEAD_DIM
        rhs = jnp.concatenate([jnp.where(left, 0.0, rows), jnp.where(left, rows, 0.0)], axis=0)
        rhs = rhs.astype(jnp.bfloat16)
        inverse = stats_ref[i, 0:1]
        row_dot = jnp.sum(head_ref[place_of(z, i)].astype(jnp.float32) * d_wide, axis=0, keepdims=True)
        keys = kv_ref[...].reshape(N_SEQ * CHUNK, 2 * HEAD_DIM)
        prob = jnp.exp(matmul(keys, query)) * inverse
        d_scores = (prob * (matmul(keys, d_head) - row_dot)).astype(jnp.bfloat16)
        d_qunit = matmul(jnp.concatenate([ku_ref[j] for j in range(N_SEQ)], axis=1), d_scores)
        both = jnp.concatenate([prob.astype(jnp.bfloat16), d_scores], axis=1)
        sums[...] += matmul(both, rhs).reshape(N_SEQ, CHUNK, 2 * HEAD_DIM)
        dqt[i] = d_qunit * SCALE
        return carry

    lax.fori_loop(0, N_SEQ, step, 0)
    for j in range(N_SEQ):
        turned = sums[j].T
        pieces = []
        for t, d_unit in enumerate((dqt[j], turned[:HEAD_DIM])):
            wide = raw_ref[j, t * HEAD_DIM : (t + 1) * HEAD_DIM].astype(jnp.float32)
            factor = unit_factor(wide, 0)
            mean = jnp.mean(d_unit * wide, axis=0, keepdims=True)
            pieces.append(factor * d_unit - factor * factor * factor * wide * mean)
        stacked = jnp.concatenate(pieces + [turned[HEAD_DIM:]], axis=0).astype(jnp.bfloat16)
        stack_ref[place_of(z, j)] = stacked


def result_kernel(*refs):
    place_ref = refs[0]
    home_ref, stack_ref, w_ref, grad_ref, x_ref, act_ref = refs[17:23]
    out_ref, keep_ref, give_ref, grad_t, grad_node, grad_out, held, sems = refs[23:]
    wait = fetch_chunks(refs[1:17], held, sems)
    z = place_ref[0]
    every = jnp.concatenate([home_ref[h, :HEAD_DIM] for h in range(N_SEQ)], axis=0)
    grad_out[...] = matmul(every, grad_ref[...])
    for j in range(N_SEQ):
        folded = home_ref[place_of(z, j), HEAD_DIM:].astype(jnp.float32)
        columns = jnp.concatenate([folded[:, :BLOCK].T, folded[:, BLOCK:].T], axis=1)
        d_head = stack_ref[place_of(z, j)]
        pad = jnp.zeros((HEAD_DIM, CHUNK), jnp.bfloat16)
        both = jnp.concatenate([d_head, pad, columns.astype(jnp.bfloat16)], axis=0)
        wait(j)
        term = matmul(both, held[j])
        if j == 0:
            grad_t[...] = term
        else:
            grad_t[...] += term
    grad_node[...] = grad_t[...].T
    split_rows(place_ref[1], grad_node, keep_ref, give_ref)
    split_rows(place_ref[1], grad_out, keep_ref, give_ref, 3 * (grad_node.shape[0] // (2 * N_XY)))
    attn = contract_rows(every, w_ref[...])
    out_ref[...] = (x_ref[...].astype(jnp.float32) + attn + act_ref[...]).astype(jnp.bfloat16)


def share_kernel(shares_ref, out_ref):
    total = jnp.zeros(shares_ref.shape[1:], jnp.float32)
    for i in range(N_XY):
        total += shares_ref[i].astype(jnp.float32)
    for h in range(N_SEQ):
        out_ref[h] = total.astype(jnp.bfloat16)


def finish_kernel(every_ref, w_ref, m_ref, gain_ref, qkv_ref, out_ref, msg_ref, gain_out_ref):
    rows = msg_ref.shape[0]
    hd = N_SEQ * HEAD_DIM
    nodes = N_SEQ * CHUNK
    gain_sum = jnp.zeros((rows, BLOCK), jnp.float32)
    low = slice(0, HEAD_DIM)
    high = slice(HEAD_DIM, 2 * HEAD_DIM)
    for t, (band, half) in enumerate(((0, low), (0, high), (1, low))):
        for p in range(N_SEQ // 2):
            pieces = [every_ref[h, band * rows : (band + 1) * rows, half] for h in (2 * p, 2 * p + 1)]
            block = jnp.concatenate(pieces, axis=1).astype(jnp.float32) * (1.0 / nodes)
            columns = slice(t * hd + p * BLOCK, t * hd + (p + 1) * BLOCK)
            qkv_ref[:, columns] = block
            gain_sum += block * w_ref[:, columns].astype(jnp.float32)
    total = jnp.zeros((every_ref.shape[1] - 3 * rows, BLOCK), jnp.float32)
    for h in range(N_SEQ):
        columns = slice(h * BLOCK, (h + 1) * BLOCK)
        block = every_ref[h, 2 * rows : 3 * rows].astype(jnp.float32) * (1.0 / nodes)
        msg_ref[:, columns] = block
        gain_sum += block * m_ref[:, columns].astype(jnp.float32)
        total += every_ref[h, 3 * rows :].astype(jnp.float32)
    half_rows = out_ref.shape[0]
    for t in range(N_SEQ):
        out_ref[:, t * BLOCK : (t + 1) * BLOCK] = total[t * half_rows : (t + 1) * half_rows] * (1.0 / nodes)
    gain_out_ref[...] = jnp.sum(gain_sum.T, axis=0, keepdims=True) / gain_ref[...]


def input_grad_kernel(*refs):
    stack_ref, w_ref, d_msg_ref, w_msg_ref, x_ref, grad_ref, gain_ref, out_ref = refs
    parts = [
        stack_ref[h, t * HEAD_DIM : (t + 1) * HEAD_DIM] for t in range(3) for h in range(N_SEQ)
    ]
    d_norm = matmul(w_ref[...], jnp.concatenate(parts, axis=0)).T
    d_norm += contract_cols(d_msg_ref[...], w_msg_ref[...])
    wide = x_ref[...].astype(jnp.float32)
    inv_rms = unit_factor(wide, -1)
    x_hat = wide * inv_rms
    scaled = d_norm * gain_ref[...]
    d_feat = inv_rms * (scaled - x_hat * jnp.mean(scaled * x_hat, axis=-1, keepdims=True))
    out_ref[...] = (grad_ref[...].astype(jnp.float32) + d_feat).astype(jnp.bfloat16)


def after(value, *others):
    return lax.optimization_barrier((value,) + others)[0]


def exchange(array, axis):
    return lax.all_to_all(array, axis, split_axis=0, concat_axis=0, tiled=True)


def shift(array, distance):
    return lax.ppermute(array, "z", [(i, (i + distance) % N_SEQ) for i in range(N_SEQ)])


def up(array):
    return shift(array, 1)


def down(array):
    return shift(array, -1)


def sum_over_cores(keep, give):
    got = lax.ppermute(give, "c", [(0, 1), (1, 0)])
    return (keep.astype(jnp.float32) + got.astype(jnp.float32)).astype(jnp.bfloat16)


def sum_over_chips(pair):
    return jnp.sum(exchange(pair, ("x", "y")).astype(jnp.float32), axis=0)


def on_device(
    features, out_grad, norm_gain, w_qkv, w_out, w_msg, block_ids, block_counts, edge_tiles
):
    node_rows, width = features.shape
    hd = w_out.shape[0]
    nodes = N_SEQ * node_rows
    bf16, f32 = jnp.bfloat16, jnp.float32
    z = lax.axis_index("z")
    core = lax.axis_index("c")
    place = jnp.stack([z, core]).astype(jnp.int32)
    gain = norm_gain.reshape(1, width)
    wide_shape = ((node_rows, width), f32)
    low_shape = ((node_rows, width), bf16)

    n_a, n_b = call(
        normalize_kernel, "normalize", (((BLOCK, width), bf16),) * 2, (), (features, gain), moved=1 << 20
    )
    a_up, a_down = [n_a, up(n_a)], [n_a, down(n_a)]
    b_up, b_down = [n_b, up(n_b)], [n_b, down(n_b)]
    w_head = pick_head(place, w_qkv)
    (d_out,) = call(
        d_out_kernel, "d_out", (((N_SEQ, HEAD_DIM, node_rows), bf16),), (), (out_grad, w_out),
        flops=2 * node_rows * width * hd, moved=2 << 20,
    )
    a_up[1], a_down[1], d_out, w_head = lax.optimization_barrier((a_up[1], a_down[1], d_out, w_head))
    a_up.append(up(a_up[1]))
    a_down.append(down(a_down[1]))
    b_up.append(up(b_up[1]))
    b_down.append(down(b_down[1]))
    d_heads = exchange(after(d_out, a_up[2]), "z")
    a_up.append(up(a_up[2]))
    a_down.append(down(a_down[2]))
    act, to_low, mid, to_high = call(
        message_kernel, "messages", (wide_shape, low_shape, wide_shape, low_shape),
        (place, block_ids, block_counts),
        (after(a_up[1], a_up[2], a_down[2]), b_up[1], n_a, n_b, a_down[1], b_down[1], w_msg, edge_tiles, out_grad),
        [pltpu.VMEM((6, BLOCK, width), bf16), pltpu.VMEM((6, BLOCK, width), f32)],
        flops=8 * node_rows * width * width, exps=node_rows * width, moved=8 << 20,
    )
    b_up.append(up(b_up[2]))
    b_down.append(down(b_down[2]))
    a_up[3], b_down[3], to_low, to_high, d_heads = lax.optimization_barrier(
        (a_up[3], b_down[3], to_low, to_high, d_heads)
    )
    c4 = [up(a_up[3]), down(b_down[3])]
    above, below = down(to_low), up(to_high)
    pairs = list(zip(a_up, b_up)) + [c4] + list(zip(a_down, b_down))[:0:-1]
    chunks = tuple(half for pair in pairs for half in pair)

    held = pltpu.VMEM((N_SEQ, CHUNK, width), bf16)
    lanes_in = ((N_SEQ, CHUNK, 2 * HEAD_DIM), bf16)
    turned = ((N_SEQ, HEAD_DIM, CHUNK), bf16)
    heads, *saved = call(
        forward_kernel, "attend_forward",
        (turned, lanes_in, turned, turned, ((N_SEQ, 2 * HEAD_DIM, CHUNK), bf16), ((N_SEQ, 8, CHUNK), f32)),
        (place,), (w_head,),
        [pltpu.VMEM((N_SEQ, HEAD_DIM + ONES, CHUNK), bf16), held, pltpu.SemaphoreType.DMA((16,))],
        flops=12 * nodes * nodes * HEAD_DIM, exps=nodes * nodes, moved=8 << 20, far=chunks,
    )
    send, d_msg = call(
        merge_kernel, "merge", (((N_SEQ, HEAD_DIM + BLOCK, CHUNK), bf16), low_shape), (),
        (heads, mid, above, below), moved=4 << 20,
    )
    send, d_heads = lax.optimization_barrier((send, d_heads))
    home = exchange(send, "z")

    rows_here = width // (2 * N_XY)
    rows_out = hd // (2 * N_XY)
    (stack,) = call(
        backward_kernel, "attend_backward", (((N_SEQ, 3 * HEAD_DIM, CHUNK), bf16),),
        (place,), (heads, *saved, d_heads),
        [pltpu.VMEM((N_SEQ, CHUNK, 2 * HEAD_DIM), f32), pltpu.VMEM((N_SEQ, HEAD_DIM, CHUNK), f32)],
        flops=24 * nodes * nodes * HEAD_DIM, exps=nodes * nodes, moved=4 << 20,
    )
    stack, home = lax.optimization_barrier((stack, home))
    stack_home = exchange(stack, "z")

    all_rows = 3 * rows_here + rows_out * width // BLOCK
    part = ((N_XY, all_rows, BLOCK), bf16)
    block_result_array, keep, give = call(
        result_kernel, "result", (low_shape, part, part), (place,),
        (home, stack, w_out, out_grad, features, act),
        [
            pltpu.VMEM((3 * BLOCK, width), f32), pltpu.VMEM((width, 3 * BLOCK), f32),
            pltpu.VMEM((hd, width), f32), held, pltpu.SemaphoreType.DMA((16,)),
        ],
        flops=8 * node_rows * width * width, moved=10 << 20, far=chunks,
    )
    got = lax.ppermute(give, "c", [(0, 1), (1, 0)])
    pair = (keep.astype(f32) + got.astype(f32)).astype(bf16)
    pair, stack_home = lax.optimization_barrier((pair, stack_home))
    shares = exchange(pair, ("x", "y"))
    (mine,) = call(
        share_kernel, "share_sum", (((N_SEQ, all_rows, BLOCK), bf16),), (), (shares,), moved=2 << 20,
    )
    every = exchange(mine, "z")

    (grad_input,) = call(
        input_grad_kernel, "input_grad", (low_shape,), (),
        (after(stack_home, mine), w_qkv, d_msg, w_msg, features, out_grad, gain),
        flops=6 * node_rows * width * hd, moved=8 << 20,
    )

    every, grad_input = lax.optimization_barrier((every, grad_input))
    first = ((lax.axis_index("x") * 4 + lax.axis_index("y")) * 2 + core) * rows_here
    w_rows = lax.dynamic_slice_in_dim(w_qkv, first, rows_here, 0)
    m_rows = lax.dynamic_slice_in_dim(w_msg, first, rows_here, 0)
    gain_rows = lax.dynamic_slice_in_dim(norm_gain, first, rows_here, 0).reshape(1, rows_here)
    grad_qkv, grad_out, grad_msg, grad_gain = call(
        finish_kernel, "finish",
        (((rows_here, 3 * hd), f32), ((rows_out, width), f32), ((rows_here, width), f32), ((1, rows_here), f32)),
        (), (every, w_rows, m_rows, gain_rows), moved=2 << 20,
    )
    return block_result_array, grad_input, grad_gain.reshape(rows_here), grad_qkv, grad_out, grad_msg


def solution(mesh):
    fine = Mesh(mesh.devices.reshape(4, 4, 2, N_SEQ), ("x", "y", "c", "z"))
    dp = ("x", "y", "c")
    rows = ("x", "y", "c", "z")
    return jax.shard_map(
        on_device,
        mesh=fine,
        in_specs=(
            P(rows, None),
            P(rows, None),
            P(),
            P(),
            P(),
            P(),
            P(rows, None),
            P(rows),
            P(rows, None, None, None),
        ),
        out_specs=(
            P(rows, None),
            P(rows, None),
            P(dp),
            P(dp, None),
            P(dp, None),
            P(dp, None),
        ),
        check_vma=False,
    )
```
